32 devices in a mesh: row: 4 (over y, x), col: 4 (over z), depth: 2 (over core).
Axes of the slice: x: 2, y: 2, z: 4, core: 2. Of those that a mesh axis runs over, the one named last changes fastest.
Arguments:
- tokens: bfloat16 [512, 8192], P(('col', 'depth'), 'row'), may hold values from -6 to 6
- gate_weight: bfloat16 [8192, 14336], P('row', 'col'), may hold values from -0.0625 to 0.0625
- up_weight: bfloat16 [8192, 14336], P('row', 'col'), may hold values from -0.0625 to 0.0625
- down_weight: bfloat16 [14336, 8192], P('col', 'row'), may hold values from -0.046875 to 0.046875
- cotangent: bfloat16 [512, 8192], P(('col', 'depth'), 'row'), may hold values from -6 to 6
Outputs:
- output: bfloat16 [512, 8192], P(('col', 'depth'), 'row')
- tokens_grad: bfloat16 [512, 8192], P(('col', 'depth'), 'row')
- gate_grad: bfloat16 [8192, 14336], P('row', ('col', 'depth'))
- up_grad: bfloat16 [8192, 14336], P('row', ('col', 'depth'))
- down_grad: bfloat16 [14336, 8192], P(('col', 'depth'), 'row')
The draws below stay inside these ranges and needn't reach their ends.
All inputs are finite; a program needn't handle non-finite values.
Results may differ from the reference program's by a relative error of at most 0.012.
Values may be sent and summed in bfloat16 or wider, within the bound.
A program may use at most 128 MiB of HBM per device.

```python
import jax
import jax.numpy as jnp
from jax import lax

D = 8192
FF = 14336
TOKENS = 512


def levels(own_key, extent, split, smallest, high):
    loudness, own = 1.0, jax.random.fold_in(own_key, 6)
    for dim, parts in split:
        draws = jnp.exp(jax.random.uniform(jax.random.fold_in(own, dim), (parts,), jnp.float32, smallest / len(split), high / len(split)))
        loudness = loudness * jnp.repeat(draws, extent[dim] // parts).reshape([-1 if axis == dim else 1 for axis in range(len(extent))])
    return loudness


def bell_draw(rng, shape, scale, bound, pieces=(), dtype=jnp.bfloat16):
    drawn = jax.random.normal(rng, shape, jnp.float32) * scale
    if len(pieces) > 0:
        drawn = levels(rng, shape, pieces, -0.22, 0.18) * drawn
    return jnp.clip(drawn, min=-bound, max=bound).astype(dtype)


def setup_inputs(seed: int = 0) -> dict:
    key_list = jax.random.split(jax.random.key(seed), 6)
    return {
        "tokens": bell_draw(key_list[0], (TOKENS, D), 1.0, 6.0, ((0, 8), (1, 4))),
        "gate_weight": bell_draw(key_list[1], (D, FF), D ** -0.5, 0.0625, ((0, 4), (1, 4))),
        "up_weight": bell_draw(key_list[2], (D, FF), D ** -0.5, 0.0625, ((0, 4), (1, 4))),
        "down_weight": bell_draw(key_list[3], (FF, D), FF ** -0.5, 0.046875, ((0, 4), (1, 4))),
        "cotangent": bell_draw(key_list[4], (TOKENS, D), 1.0, 6.0, ((0, 8), (1, 4))),
    }


def dot_nt(left, right):
    return lax.dot_general(left, right, (((1,), (1,)), ((), ())), preferred_element_type=jnp.float32)


def dot_tn(left, right):
    return lax.dot_general(left, right, (((0,), (0,)), ((), ())), preferred_element_type=jnp.float32)


def reference(tokens, gate_weight, up_weight, down_weight, cotangent):
    gate = jnp.dot(tokens, gate_weight, preferred_element_type=jnp.float32)
    up = jnp.dot(tokens, up_weight, preferred_element_type=jnp.float32)
    sig = jax.nn.sigmoid(gate)
    act = (gate * sig * up).astype(jnp.bfloat16)
    output = jnp.dot(act, down_weight, preferred_element_type=jnp.float32).astype(jnp.bfloat16)
    dact = dot_nt(cotangent, down_weight)
    dgate = (dact * up * sig * (1.0 + gate * (1.0 - sig))).astype(jnp.bfloat16)
    dup = (dact * gate * sig).astype(jnp.bfloat16)
    tokens_grad = (dot_nt(dgate, gate_weight) + dot_nt(dup, up_weight)).astype(jnp.bfloat16)
    gate_grad = dot_tn(tokens, dgate).astype(jnp.bfloat16)
    up_grad = dot_tn(tokens, dup).astype(jnp.bfloat16)
    down_grad = dot_tn(act, cotangent).astype(jnp.bfloat16)
    return (output, tokens_grad, gate_grad, up_grad, down_grad)
```

```python
import functools

import jax
import jax.numpy as jnp
from jax import lax
from jax.experimental import pallas as pl
from jax.experimental.pallas import tpu as pltpu
from jax.sharding import PartitionSpec as P

MESH = pl.DeviceIdType.MESH
BF16 = jnp.bfloat16
F32 = jnp.float32


def dot_nn(left, right):
    return jnp.dot(left, right, preferred_element_type=F32)


def dot_nt(left, right):
    return lax.dot_general(
        left, right, (((1,), (1,)), ((), ())), preferred_element_type=F32
    )


def dot_tn(left, right):
    return lax.dot_general(
        left, right, (((0,), (0,)), ((), ())), preferred_element_type=F32
    )


def block(index, size):
    return pl.ds(pl.multiple_of(index * size, size), size)


def kernel(
    dims,
    x_ref, cot_ref, wg_hbm, wu_hbm, wd_hbm,
    out_ref, tg_ref, x_out, cot_out, act_out, dg_out, du_out,
    wg, wu, wd, x_full, cot_full,
    gu_part, gu_recv, d_part, d_recv, gu_own, act, dg, du,
    o_part, o_sib, o_sum, o_recv, t_part, t_sib, t_sum, t_recv,
    w_sem, copy_sem, x_ssem, x_rsem, c_ssem, c_rsem,
    gu_ssem, gu_rsem, d_ssem, d_rsem, act_ssem, act_rsem, h_ssem, h_rsem,
    osib_ssem, osib_rsem, oz_ssem, oz_rsem,
    tsib_ssem, tsib_rsem, tz_ssem, tz_rsem,
):
    n, nz, tl, tr, chunks, ch, parts, pw, sliced = dims
    r = lax.axis_index("row")
    z = lax.axis_index("col")
    d = lax.axis_index("depth")
    half = chunks * ch

    def peer(k):
        return {"row": lax.rem(r + k, n)}

    def zpeer(k):
        return {"col": lax.rem(z + k, nz)}

    sibling = {"depth": 1 - d}

    barrier = pltpu.get_barrier_semaphore()
    for k in range(1, n):
        pl.semaphore_signal(barrier, inc=1, device_id=peer(k), device_id_type=MESH)
    for k in range(1, nz):
        pl.semaphore_signal(barrier, inc=1, device_id=zpeer(k), device_id_type=MESH)
    pl.semaphore_signal(barrier, inc=1, device_id=sibling, device_id_type=MESH)

    if sliced:
        sources = (wg_hbm, wu_hbm, wd_hbm)
    else:
        mine = block(d, half)
        sources = (wg_hbm.at[:, mine], wu_hbm.at[:, mine], wd_hbm.at[mine, :])
    loads = [
        pltpu.make_async_copy(src, dst, w_sem.at[i])
        for i, (src, dst) in enumerate(zip(sources, (wg, wu, wd)))
    ]
    for load in loads:
        load.start()

    def remote(src, dst, ssem, rsem, where):
        return pltpu.make_async_remote_copy(
            src_ref=src, dst_ref=dst, send_sem=ssem, recv_sem=rsem,
            device_id=where, device_id_type=MESH,
        )

    def gather(full, ssem, rsem):
        def hop(zz, way):
            slot = zz * 2 + d
            ref = full.at[block(slot, tl)]
            where = ({"col": z + 1}, {"col": z - 1}, sibling)[way]
            return remote(ref, ref, ssem.at[zz, way], rsem.at[slot], where)

        def arrived(slot):
            ref = full.at[block(slot, tl)]
            remote(ref, ref, ssem.at[0, 0], rsem.at[slot], sibling).wait_recv()

        def first(shard):
            full[block(z * 2 + d, tl), :] = shard[...]

            @pl.when(z + 1 < nz)
            def _():
                hop(z, 0).start()

            @pl.when(z > 0)
            def _():
                hop(z, 1).start()

            hop(z, 2).start()

        def stage(s):
            low, high = z - s, z + s

            @pl.when(low >= 0)
            def _():
                arrived(low * 2 + d)

                @pl.when(z + 1 < nz)
                def _():
                    hop(low, 0).start()

                hop(low, 2).start()

            @pl.when(high < nz)
            def _():
                arrived(high * 2 + d)

                @pl.when(z > 0)
                def _():
                    hop(high, 1).start()

                hop(high, 2).start()

        def last():
            for zz in range(nz):
                arrived(zz * 2 + 1 - d)

        def drain():
            for zz in range(nz):
                @pl.when((zz <= z) & (z + 1 < nz))
                def _():
                    hop(zz, 0).wait_send()

                @pl.when((zz >= z) & (z > 0))
                def _():
                    hop(zz, 1).wait_send()

                hop(zz, 2).wait_send()

        return first, stage, last, drain

    x_first, x_stage, x_last, x_drain = gather(x_full, x_ssem, x_rsem)
    c_first, c_stage, c_last, c_drain = gather(cot_full, c_ssem, c_rsem)

    def gu_copy(c, k):
        rows = block(lax.rem(r + k, n), tr)
        return remote(gu_part.at[c, :, rows, :], gu_recv.at[c, k - 1],
                      gu_ssem.at[c, k - 1], gu_rsem.at[c, k - 1], peer(k))

    def d_copy(c, k):
        rows = block(lax.rem(r + k, n), tr)
        return remote(d_part.at[c, rows, :], d_recv.at[c, k - 1],
                      d_ssem.at[c, k - 1], d_rsem.at[c, k - 1], peer(k))

    mine_rows = block(r, tr)

    def act_copy(c, k, owner=None):
        rows = mine_rows if owner is None else block(owner, tr)
        ref = act.at[rows, block(c, ch)]
        return remote(ref, ref, act_ssem.at[c, k - 1], act_rsem.at[c, k - 1], peer(k))

    def h_copy(which, c, k, owner=None):
        rows = mine_rows if owner is None else block(owner, tr)
        ref = (dg, du)[which].at[rows, block(c, ch)]
        return remote(ref, ref, h_ssem.at[which, c, k - 1], h_rsem.at[which, c, k - 1], peer(k))

    def sender(k):
        return lax.rem(r - k + n, n)

    pl.semaphore_wait(barrier, n - 1 + nz - 1 + 1)

    x_first(x_ref)
    for s in range(1, nz):
        if s == nz - 1:
            c_first(cot_ref)
        x_stage(s)
    x_last()
    if nz == 1:
        c_first(cot_ref)
    x_save = pltpu.make_async_copy(x_full, x_out, copy_sem.at[0])
    x_save.start()

    loads[0].wait()
    loads[1].wait()

    @pl.loop(0, chunks)
    def _(c):
        gu_part[c, 0, :, :] = dot_nn(x_full[...], wg[:, block(c, ch)]).astype(BF16)
        gu_part[c, 1, :, :] = dot_nn(x_full[...], wu[:, block(c, ch)]).astype(BF16)
        for k in range(1, n):
            gu_copy(c, k).start()
        for s in range(1, nz):
            @pl.when(c == min(2 * s - 1, chunks - 1))
            def _():
                c_stage(s)

    c_last()
    cot_save = pltpu.make_async_copy(cot_full, cot_out, copy_sem.at[1])
    cot_save.start()
    loads[2].wait()

    @pl.loop(0, chunks)
    def _(c):
        d_part[c, :, :] = dot_nt(cot_full[...], wd[block(c, ch), :]).astype(BF16)
        for k in range(1, n):
            d_copy(c, k).start()

    @pl.loop(0, chunks)
    def _(c):
        gate = gu_part[c, 0, mine_rows, :].astype(F32)
        up = gu_part[c, 1, mine_rows, :].astype(F32)
        for k in range(1, n):
            gu_copy(c, k).wait_recv()
            gate += gu_recv[c, k - 1, 0].astype(F32)
            up += gu_recv[c, k - 1, 1].astype(F32)
        gu_own[c, 0] = gate
        gu_own[c, 1] = up
        act[mine_rows, block(c, ch)] = (gate * jax.nn.sigmoid(gate) * up).astype(BF16)
        for k in range(1, n):
            act_copy(c, k).start()

    @pl.loop(0, chunks)
    def _(c):
        dact = d_part[c, mine_rows, :].astype(F32)
        for k in range(1, n):
            d_copy(c, k).wait_recv()
            dact += d_recv[c, k - 1].astype(F32)
        gate, up = gu_own[c, 0], gu_own[c, 1]
        sig = jax.nn.sigmoid(gate)
        dg[mine_rows, block(c, ch)] = (
            dact * up * sig * (1.0 + gate * (1.0 - sig))
        ).astype(BF16)
        du[mine_rows, block(c, ch)] = (dact * gate * sig).astype(BF16)
        for k in range(1, n):
            h_copy(0, c, k).start()
            h_copy(1, c, k).start()

    def summing(part, sib, total, recv, sib_ssem, sib_rsem, z_ssem, z_rsem):
        def to_sibling(p):
            cols = block(p, pw)
            return remote(part.at[1 - d, :, :, cols], sib.at[:, :, cols],
                          sib_ssem.at[p], sib_rsem.at[p], sibling)

        def to_col(p, k):
            cols = block(p, pw)
            return remote(total.at[lax.rem(z + k, nz), :, cols], recv.at[k - 1, :, cols],
                          z_ssem.at[p, k - 1], z_rsem.at[p, k - 1], zpeer(k))

        def put(p, value):
            cols = block(p, pw)
            for zz in range(nz):
                for dd in range(2):
                    slot = zz * 2 + dd
                    part[dd, zz, :, cols] = value[slot * tl:(slot + 1) * tl].astype(BF16)
            to_sibling(p).start()

        def spread():
            @pl.loop(0, parts)
            def _(p):
                cols = block(p, pw)
                to_sibling(p).wait_recv()
                total[:, :, cols] = (
                    part[d, :, :, cols].astype(F32) + sib[:, :, cols].astype(F32)
                ).astype(BF16)
                for k in range(1, nz):
                    to_col(p, k).start()

        def finish(result):
            @pl.loop(0, parts)
            def _(p):
                cols = block(p, pw)
                value = total[z, :, cols].astype(F32)
                for k in range(1, nz):
                    to_col(p, k).wait_recv()
                    value += recv[k - 1, :, cols].astype(F32)
                result[:, cols] = value.astype(BF16)

        def drain():
            @pl.loop(0, parts)
            def _(p):
                to_sibling(p).wait_send()
                for k in range(1, nz):
                    to_col(p, k).wait_send()

        return put, spread, finish, drain

    o_put, o_spread, o_finish, o_drain = summing(
        o_part, o_sib, o_sum, o_recv, osib_ssem, osib_rsem, oz_ssem, oz_rsem)
    t_put, t_spread, t_finish, t_drain = summing(
        t_part, t_sib, t_sum, t_recv, tsib_ssem, tsib_rsem, tz_ssem, tz_rsem)

    @pl.loop(0, chunks)
    def _(c):
        for k in range(1, n):
            act_copy(c, k, sender(k)).wait_recv()

    act_save = pltpu.make_async_copy(act, act_out, copy_sem.at[2])
    act_save.start()

    @pl.loop(0, parts)
    def _(p):
        o_put(p, dot_nn(act[...], wd[:, block(p, pw)]))

    o_spread()

    @pl.loop(0, chunks)
    def _(c):
        for k in range(1, n):
            h_copy(0, c, k, sender(k)).wait_recv()
            h_copy(1, c, k, sender(k)).wait_recv()

    dg_save = pltpu.make_async_copy(dg, dg_out, copy_sem.at[3])
    du_save = pltpu.make_async_copy(du, du_out, copy_sem.at[4])
    dg_save.start()
    du_save.start()

    @pl.loop(0, parts)
    def _(p):
        t_put(p, dot_nt(dg[...], wg[block(p, pw), :]) + dot_nt(du[...], wu[block(p, pw), :]))

    t_spread()
    o_finish(out_ref)
    t_finish(tg_ref)

    x_drain()
    c_drain()

    @pl.loop(0, chunks)
    def _(c):
        for k in range(1, n):
            gu_copy(c, k).wait_send()
            d_copy(c, k).wait_send()
            act_copy(c, k).wait_send()
            h_copy(0, c, k).wait_send()
            h_copy(1, c, k).wait_send()

    o_drain()
    t_drain()
    for save in (x_save, cot_save, act_save, dg_save, du_save):
        save.wait()


def group_kernel(
    dims,
    x_ref, cot_ref, wg_hbm, wu_hbm, wd_hbm,
    out_ref, tg_ref, x_out, cot_out, act_out, dg_out, du_out,
    wg, wu, wd, x_full, cot_full, part, recv, h, acc, s_part, s_sib, s_sum, s_recv,
    w_sem, copy_sem, save_sem, x_ssem, x_rsem, c_ssem, c_rsem,
    rs_ssem, rs_rsem, ag_ssem, ag_rsem, sib_ssem, sib_rsem, z_ssem, z_rsem,
):
    nz, tl, half, pw = dims
    feats = x_full.shape[1]
    tg, tr, hw = 2 * tl, tl // 2, half // 2
    units = 2 * nz
    wide = (hw // 2 + 127) // 128 * 128
    widths = (wide, hw - wide)
    starts = (0, wide)
    r = lax.axis_index("row")
    z = lax.axis_index("col")
    d = lax.axis_index("depth")
    rx = r + 1 - 2 * (r % 2)
    ry = r + 2 - 4 * (r // 2)
    rd = 3 - r
    sibling = {"depth": 1 - d}
    way = 1 - 2 * (z // max(nz // 2, 1))

    barrier = pltpu.get_barrier_semaphore()
    for where in (rx, ry):
        pl.semaphore_signal(barrier, inc=1, device_id={"row": where}, device_id_type=MESH)
    for k in range(1, nz):
        pl.semaphore_signal(barrier, inc=1, device_id={"col": lax.rem(z + k, nz)}, device_id_type=MESH)
    pl.semaphore_signal(barrier, inc=1, device_id=sibling, device_id_type=MESH)

    def load(i, s):
        here = pl.ds(s * hw, hw)
        there = block(2 * d + s, hw)
        src, dst = (
            (wg_hbm.at[:, there], wg.at[:, here]),
            (wu_hbm.at[:, there], wu.at[:, here]),
            (wd_hbm.at[there, :], wd.at[here, :]),
        )[i]
        return pltpu.make_async_copy(src, dst, w_sem.at[i, s])

    for i in range(3):
        load(i, 0).start()

    def remote(src, dst, ssem, rsem, where):
        return pltpu.make_async_remote_copy(
            src_ref=src, dst_ref=dst, send_sem=ssem, recv_sem=rsem,
            device_id=where, device_id_type=MESH,
        )

    def index(u):
        return lax.rem((u + 1) // 2, nz)

    def side(u):
        return lax.rem(u + 1 + (index(u) == 0).astype(jnp.int32), 2)

    def group(i):
        return lax.rem(z + i * way + nz, nz)

    def ends(u):
        flip = lax.rem(u, 2)
        return rx + flip * (ry - rx), ry + flip * (rx - ry)

    def span_of(u, b):
        return pl.ds(pl.multiple_of(side(u) * hw + starts[b], 128), widths[b])

    def gather(full, ssem, rsem):
        def hop(zz, to):
            slot = zz * 2 + d
            ref = full.at[block(slot, tl)]
            where = ({"col": z + 1}, {"col": z - 1}, sibling)[to]
            return remote(ref, ref, ssem.at[zz, to], rsem.at[slot], where)

        def arrived(slot):
            ref = full.at[block(slot, tl)]
            remote(ref, ref, ssem.at[0, 0], rsem.at[slot], sibling).wait_recv()

        def first(shard):
            full[block(z * 2 + d, tl), :] = shard[...]
            hop(z, 2).start()

            @pl.when(z + 1 < nz)
            def _():
                hop(z, 0).start()

            @pl.when(z > 0)
            def _():
                hop(z, 1).start()

        def stage(s):
            low, high = z - s, z + s

            @pl.when(low >= 0)
            def _():
                arrived(low * 2 + d)

                @pl.when(z + 1 < nz)
                def _():
                    hop(low, 0).start()

                hop(low, 2).start()

            @pl.when(high < nz)
            def _():
                arrived(high * 2 + d)

                @pl.when(z > 0)
                def _():
                    hop(high, 1).start()

                hop(high, 2).start()

        def other(g):
            arrived(g * 2 + 1 - d)

        def drain():
            for zz in range(nz):
                @pl.when((zz <= z) & (z + 1 < nz))
                def _():
                    hop(zz, 0).wait_send()

                @pl.when((zz >= z) & (z > 0))
                def _():
                    hop(zz, 1).wait_send()

                hop(zz, 2).wait_send()

        return first, stage, other, drain

    x_first, x_stage, x_other, x_drain = gather(x_full, x_ssem, x_rsem)
    c_first, c_stage, c_other, c_drain = gather(cot_full, c_ssem, c_rsem)

    def rs(u, b, m):
        i = index(u)
        near, far = ends(u) if b == 0 else ends(u)[::-1]
        owner = (rd, near, far)[m]
        to = far if m == 2 else near
        cols = span_of(u, b)
        return remote(part.at[i, :, block(owner, tr), cols],
                      recv.at[i, m, :, :, cols],
                      rs_ssem.at[u, b, m], rs_rsem.at[u, b, m], {"row": to})

    def rows(g, owner):
        return pl.ds(pl.multiple_of(g * tg + owner * tr, tr), tr)

    def ag(u, m, incoming=False):
        g = group(index(u))
        p, q = ends(u)
        owner = (p, q, rd, rd)[m] if incoming else (r, r, p, q)[m]
        cols = block(side(u), hw) if m < 2 else span_of(u, m - 2)
        ref = h.at[:, rows(g, owner), cols]
        to = (p, q, q, p)[m]
        return remote(ref, ref, ag_ssem.at[u, m], ag_rsem.at[u, m], {"row": to})

    def to_sibling(i):
        g = group(i)
        return remote(s_part.at[g, :, 1 - d], s_sib.at[g], sib_ssem.at[i], sib_rsem.at[i], sibling)

    def to_col(i):
        g = group(i)
        k = lax.rem(z - g + nz, nz) - 1
        return remote(s_sum.at[g], s_recv.at[k], z_ssem.at[i], z_rsem.at[k], {"col": g})

    def saves(u):
        span, cols = block(group(index(u)), tg), block(side(u), hw)
        return [
            pltpu.make_async_copy(h.at[j, span, cols], out.at[span, cols], save_sem.at[u, j])
            for j, out in enumerate((act_out, dg_out, du_out))
        ]

    x_save = pltpu.make_async_copy(x_full, x_out, copy_sem.at[0])
    cot_save = pltpu.make_async_copy(cot_full, cot_out, copy_sem.at[1])

    def compute(u):
        i = index(u)
        g = group(i)
        span = block(g, tg)
        cols = block(side(u), hw)
        opens = (u == 0) | ((i > 0) & (lax.rem(u, 2) == 1))

        @pl.when((u > 0) & (u < nz))
        def _():
            x_stage(u)
            c_stage(u)

        @pl.when(opens)
        def _():
            x_other(g)

        @pl.when(u == 0)
        def _():
            load(0, 0).wait()
            load(1, 0).wait()

        @pl.when(u == 1)
        def _():
            for k in range(3):
                load(k, 1).wait()

        part[i, 0, :, cols] = dot_nn(x_full[span, :], wg[:, cols]).astype(BF16)
        part[i, 1, :, cols] = dot_nn(x_full[span, :], wu[:, cols]).astype(BF16)

        @pl.when(opens)
        def _():
            c_other(g)

        @pl.when(u == 0)
        def _():
            load(2, 0).wait()
            for k in range(3):
                load(k, 1).start()

        part[i, 2, :, cols] = dot_nt(cot_full[span, :], wd[cols, :]).astype(BF16)

        for m in range(2):
            for b in range(2):
                rs(u, b, m).start()

    def relay(u):
        i = index(u)
        for b in range(2):
            rs(u, b, 0).wait_recv()
            spot, cols = block(ends(u)[1 - b], tr), span_of(u, b)
            part[i, :, spot, cols] = (
                part[i, :, spot, cols].astype(F32) + recv[i, 0, :, :, cols].astype(F32)
            ).astype(BF16)
            rs(u, b, 2).start()

    def hidden(u):
        i = index(u)
        own = rows(group(i), r)
        for b in range(2):
            rs(u, b, 1).wait_recv()
            rs(u, b, 2).wait_recv()
            cols = span_of(u, b)
            gate, up, dact = (
                part[i, j, block(r, tr), cols].astype(F32)
                + recv[i, 1, j, :, cols].astype(F32)
                + recv[i, 2, j, :, cols].astype(F32)
                for j in range(3)
            )
            sig = jax.nn.sigmoid(gate)
            h[0, own, cols] = (gate * sig * up).astype(BF16)
            h[1, own, cols] = (dact * up * sig * (1.0 + gate * (1.0 - sig))).astype(BF16)
            h[2, own, cols] = (dact * gate * sig).astype(BF16)
        ag(u, 0).start()
        ag(u, 1).start()

    def forward(u):
        for m in range(2):
            ag(u, m, True).wait_recv()
            ag(u, m + 2).start()

    def project(u):
        i = index(u)
        g = group(i)
        span, hid = block(g, tg), block(side(u), hw)
        slot = jnp.minimum(i, 1)
        opens = (u == 0) | ((i > 0) & (lax.rem(u, 2) == 1))
        ag(u, 2, True).wait_recv()
        ag(u, 3, True).wait_recv()
        for save in saves(u):
            save.start()

        def products(cols):
            out = dot_nn(h[0, span, hid], wd[hid, cols])
            grad = dot_nt(h[1, span, hid], wg[cols, hid]) + dot_nt(h[2, span, hid], wu[cols, hid])
            return out, grad

        @pl.when(opens)
        def _():
            @pl.loop(0, feats // pw)
            def _(p):
                cols = block(p, pw)
                out, grad = products(cols)
                acc[slot, 0, :, cols] = out
                acc[slot, 1, :, cols] = grad

        @pl.when(jnp.logical_not(opens))
        def _():
            @pl.loop(0, feats // pw)
            def _(p):
                cols = block(p, pw)
                for j, value in enumerate(products(cols)):
                    value = (value + acc[slot, j, :, cols]).astype(BF16)
                    for dd in range(2):
                        s_part[g, j, dd, :, cols] = value[dd * tl:(dd + 1) * tl]

            to_sibling(i).start()

    def spread(i):
        g = group(i)
        to_sibling(i).wait_recv()
        for j in range(2):
            s_sum[g, j] = (s_part[g, j, d].astype(F32) + s_sib[g, j].astype(F32)).astype(BF16)
        to_col(i).start()

    pl.semaphore_wait(barrier, 2 + nz - 1 + 1)
    x_first(x_ref)
    c_first(cot_ref)

    @pl.loop(0, units + 3)
    def _(t):
        @pl.when(t < units)
        def _():
            compute(t)

        @pl.when(t == units - 2)
        def _():
            x_save.start()
            cot_save.start()

        @pl.when((t >= 2) & (t < units + 2))
        def _():
            forward(t - 2)

        @pl.when((t >= 1) & (t < units + 1))
        def _():
            hidden(t - 1)

        @pl.when(t >= 3)
        def _():
            project(t - 3)

        @pl.when(t < units)
        def _():
            relay(t)

        @pl.when((t >= 5) & (t < units + 2) & (lax.rem(t, 2) == 1))
        def _():
            spread((t - 3) // 2)

    to_sibling(0).wait_recv()

    def landed(k):
        remote(s_sum.at[0], s_recv.at[k], z_ssem.at[0], z_rsem.at[k], sibling).wait_recv()

    for k in range(nz - 1):
        landed(k)
    for j, result in enumerate((out_ref, tg_ref)):
        value = s_part[z, j, d].astype(F32) + s_sib[z, j].astype(F32)
        for k in range(nz - 1):
            value += s_recv[k, j].astype(F32)
        result[...] = value.astype(BF16)

    x_drain()
    c_drain()

    @pl.loop(0, units)
    def _(u):
        for b in range(2):
            for m in range(3):
                rs(u, b, m).wait_send()
        for m in range(4):
            ag(u, m).wait_send()
        for save in saves(u):
            save.wait()

    @pl.loop(0, nz)
    def _(i):
        to_sibling(i).wait_send()

        @pl.when(i > 0)
        def _():
            to_col(i).wait_send()

    x_save.wait()
    cot_save.wait()


def per_device(n, nz, tokens, gate_weight, up_weight, down_weight, cotangent):
    tl, feats = tokens.shape
    half = gate_weight.shape[1] // 2
    total = tl * nz * 2
    tr = total // n
    ch = 256 if half % 256 == 0 else half
    chunks = half // ch
    pw = 512 if feats % 512 == 0 else feats
    parts = feats // pw
    sliced = half % 128 != 0
    if sliced:
        start = lax.axis_index("depth") * half
        weights = (
            lax.dynamic_slice_in_dim(gate_weight, start, half, 1),
            lax.dynamic_slice_in_dim(up_weight, start, half, 1),
            lax.dynamic_slice_in_dim(down_weight, start, half, 0),
        )
    else:
        weights = (gate_weight, up_weight, down_weight)

    def sds(*shape):
        return jax.ShapeDtypeStruct(shape, BF16)

    def buf(*shape):
        return pltpu.VMEM(shape, BF16)

    def sem(*shape):
        return pltpu.SemaphoreType.DMA(shape)

    vmem = pl.BlockSpec(memory_space=pltpu.VMEM)
    hbm = pl.BlockSpec(memory_space=pl.ANY)
    if n == 4 and nz % 2 == 0 and tl % 32 == 0 and half % 256 == 0 and half >= 512:
        output, tokens_grad, x_both, cot_both, act, dgate, dup = pl.pallas_call(
            functools.partial(group_kernel, (nz, tl, half, 2 * pw if parts % 2 == 0 else pw)),
            out_shape=(
                sds(tl, feats), sds(tl, feats), sds(total, feats), sds(total, feats),
                sds(total, half), sds(total, half), sds(total, half),
            ),
            in_specs=[vmem, vmem, hbm, hbm, hbm],
            out_specs=(vmem, vmem, hbm, hbm, hbm, hbm, hbm),
            scratch_shapes=[
                buf(feats, half), buf(feats, half), buf(half, feats),
                buf(total, feats), buf(total, feats),
                buf(nz, 3, 2 * tl, half), buf(nz, 3, 3, tl // 2, half),
                buf(3, total, half), pltpu.VMEM((2, 2, 2 * tl, feats), F32),
                buf(nz, 2, 2, tl, feats), buf(nz, 2, tl, feats), buf(nz, 2, tl, feats),
                buf(max(nz - 1, 1), 2, tl, feats),
                sem(3, 2), sem(2), sem(2 * nz, 3),
                sem(nz, 3), sem(nz * 2), sem(nz, 3), sem(nz * 2),
                sem(2 * nz, 2, 3), sem(2 * nz, 2, 3), sem(2 * nz, 4), sem(2 * nz, 4),
                sem(nz), sem(nz), sem(nz), sem(nz),
            ],
            compiler_params=pltpu.CompilerParams(
                collective_id=1, has_side_effects=True, vmem_limit_bytes=60 * 2**20
            ),
            cost_estimate=pl.CostEstimate(
                flops=12 * total * feats * half, bytes_accessed=8 * feats * half,
                transcendentals=0,
            ),
        )(tokens, cotangent, *weights)
    else:
        sums = [
            buf(2, nz, tl, feats), buf(nz, tl, feats), buf(nz, tl, feats),
            buf(max(nz - 1, 1), tl, feats),
        ]
        sum_sems = [sem(parts), sem(parts), sem(parts, nz), sem(parts, nz)]
        output, tokens_grad, x_both, cot_both, act, dgate, dup = pl.pallas_call(
            functools.partial(kernel, (n, nz, tl, tr, chunks, ch, parts, pw, sliced)),
            out_shape=(
                sds(tl, feats), sds(tl, feats), sds(total, feats), sds(total, feats),
                sds(total, half), sds(total, half), sds(total, half),
            ),
            in_specs=[vmem, vmem, hbm, hbm, hbm],
            out_specs=(vmem, vmem, hbm, hbm, hbm, hbm, hbm),
            scratch_shapes=[
                buf(feats, half), buf(feats, half), buf(half, feats),
                buf(total, feats), buf(total, feats),
                buf(chunks, 2, total, ch), buf(chunks, n - 1, 2, tr, ch),
                buf(chunks, total, ch), buf(chunks, n - 1, tr, ch),
                pltpu.VMEM((chunks, 2, tr, ch), F32),
                buf(total, half), buf(total, half), buf(total, half),
                *sums, *sums,
                sem(3), sem(5),
                sem(nz, 3), sem(nz * 2), sem(nz, 3), sem(nz * 2),
                sem(chunks, n - 1), sem(chunks, n - 1),
                sem(chunks, n - 1), sem(chunks, n - 1),
                sem(chunks, n - 1), sem(chunks, n - 1),
                sem(2, chunks, n - 1), sem(2, chunks, n - 1),
                *sum_sems, *sum_sems,
            ],
            compiler_params=pltpu.CompilerParams(
                collective_id=0, has_side_effects=True, vmem_limit_bytes=60 * 2**20
            ),
            cost_estimate=pl.CostEstimate(
                flops=12 * total * feats * half, bytes_accessed=8 * feats * half,
                transcendentals=0,
            ),
        )(tokens, cotangent, *weights)
    gate_grad = dot_tn(x_both, dgate)
    up_grad = dot_tn(x_both, dup)
    down_grad = dot_tn(act, cot_both)
    return (
        output,
        tokens_grad,
        gate_grad.astype(BF16),
        up_grad.astype(BF16),
        down_grad.astype(BF16),
    )


def solution(mesh):
    return jax.shard_map(
        functools.partial(per_device, mesh.shape["row"], mesh.shape["col"]),
        mesh=mesh,
        in_specs=(
            P(("col", "depth"), "row"),
            P("row", "col"),
            P("row", "col"),
            P("col", "row"),
            P(("col", "depth"), "row"),
        ),
        out_specs=(
            P(("col", "depth"), "row"),
            P(("col", "depth"), "row"),
            P("row", ("col", "depth")),
            P("row", ("col", "depth")),
            P(("col", "depth"), "row"),
        ),
        check_vma=False,
    )
```

```python
import functools

import jax
import jax.numpy as jnp
from jax import lax
from jax.experimental import pallas as pl
from jax.experimental.pallas import tpu as pltpu
from jax.sharding import PartitionSpec as P

MESH = pl.DeviceIdType.MESH
BF16 = jnp.bfloat16
F32 = jnp.float32


def dot_nn(left, right):
    return jnp.dot(left, right, preferred_element_type=F32)


def dot_nt(left, right):
    return lax.dot_general(
        left, right, (((1,), (1,)), ((), ())), preferred_element_type=F32
    )


def dot_tn(left, right):
    return lax.dot_general(
        left, right, (((0,), (0,)), ((), ())), preferred_element_type=F32
    )


def block(index, size):
    return pl.ds(pl.multiple_of(index * size, size), size)


def kernel(
    dims,
    x_ref, cot_ref, wg_hbm, wu_hbm, wd_hbm,
    out_ref, tg_ref, x_out, cot_out, act_out, dg_out, du_out,
    wg, wu, wd, x_full, cot_full,
    gu_part, gu_recv, d_part, d_recv, gu_own, act, dg, du,
    o_part, o_sib, o_sum, o_recv, t_part, t_sib, t_sum, t_recv,
    w_sem, copy_sem, x_ssem, x_rsem, c_ssem, c_rsem,
    gu_ssem, gu_rsem, d_ssem, d_rsem, act_ssem, act_rsem, h_ssem, h_rsem,
    osib_ssem, osib_rsem, oz_ssem, oz_rsem,
    tsib_ssem, tsib_rsem, tz_ssem, tz_rsem,
):
    n, nz, tl, tr, chunks, ch, parts, pw, sliced = dims
    r = lax.axis_index("row")
    z = lax.axis_index("col")
    d = lax.axis_index("depth")
    half = chunks * ch

    def peer(k):
        return {"row": lax.rem(r + k, n)}

    def zpeer(k):
        return {"col": lax.rem(z + k, nz)}

    sibling = {"depth": 1 - d}

    barrier = pltpu.get_barrier_semaphore()
    for k in range(1, n):
        pl.semaphore_signal(barrier, inc=1, device_id=peer(k), device_id_type=MESH)
    for k in range(1, nz):
        pl.semaphore_signal(barrier, inc=1, device_id=zpeer(k), device_id_type=MESH)
    pl.semaphore_signal(barrier, inc=1, device_id=sibling, device_id_type=MESH)

    if sliced:
        sources = (wg_hbm, wu_hbm, wd_hbm)
    else:
        mine = block(d, half)
        sources = (wg_hbm.at[:, mine], wu_hbm.at[:, mine], wd_hbm.at[mine, :])
    loads = [
        pltpu.make_async_copy(src, dst, w_sem.at[i])
        for i, (src, dst) in enumerate(zip(sources, (wg, wu, wd)))
    ]
    for load in loads:
        load.start()

    def remote(src, dst, ssem, rsem, where):
        return pltpu.make_async_remote_copy(
            src_ref=src, dst_ref=dst, send_sem=ssem, recv_sem=rsem,
            device_id=where, device_id_type=MESH,
        )

    def gather(full, ssem, rsem):
        def hop(zz, way):
            slot = zz * 2 + d
            ref = full.at[block(slot, tl)]
            where = ({"col": z + 1}, {"col": z - 1}, sibling)[way]
            return remote(ref, ref, ssem.at[zz, way], rsem.at[slot], where)

        def arrived(slot):
            ref = full.at[block(slot, tl)]
            remote(ref, ref, ssem.at[0, 0], rsem.at[slot], sibling).wait_recv()

        def first(shard):
            full[block(z * 2 + d, tl), :] = shard[...]

            @pl.when(z + 1 < nz)
            def _():
                hop(z, 0).start()

            @pl.when(z > 0)
            def _():
                hop(z, 1).start()

            hop(z, 2).start()

        def stage(s):
            low, high = z - s, z + s

            @pl.when(low >= 0)
            def _():
                arrived(low * 2 + d)

                @pl.when(z + 1 < nz)
                def _():
                    hop(low, 0).start()

                hop(low, 2).start()

            @pl.when(high < nz)
            def _():
                arrived(high * 2 + d)

                @pl.when(z > 0)
                def _():
                    hop(high, 1).start()

                hop(high, 2).start()

        def last():
            for zz in range(nz):
                arrived(zz * 2 + 1 - d)

        def drain():
            for zz in range(nz):
                @pl.when((zz <= z) & (z + 1 < nz))
                def _():
                    hop(zz, 0).wait_send()

                @pl.when((zz >= z) & (z > 0))
                def _():
                    hop(zz, 1).wait_send()

                hop(zz, 2).wait_send()

        return first, stage, last, drain

    x_first, x_stage, x_last, x_drain = gather(x_full, x_ssem, x_rsem)
    c_first, c_stage, c_last, c_drain = gather(cot_full, c_ssem, c_rsem)

    def gu_copy(c, k):
        rows = block(lax.rem(r + k, n), tr)
        return remote(gu_part.at[c, :, rows, :], gu_recv.at[c, k - 1],
                      gu_ssem.at[c, k - 1], gu_rsem.at[c, k - 1], peer(k))

    def d_copy(c, k):
        rows = block(lax.rem(r + k, n), tr)
        return remote(d_part.at[c, rows, :], d_recv.at[c, k - 1],
                      d_ssem.at[c, k - 1], d_rsem.at[c, k - 1], peer(k))

    mine_rows = block(r, tr)

    def act_copy(c, k, owner=None):
        rows = mine_rows if owner is None else block(owner, tr)
        ref = act.at[rows, block(c, ch)]
        return remote(ref, ref, act_ssem.at[c, k - 1], act_rsem.at[c, k - 1], peer(k))

    def h_copy(which, c, k, owner=None):
        rows = mine_rows if owner is None else block(owner, tr)
        ref = (dg, du)[which].at[rows, block(c, ch)]
        return remote(ref, ref, h_ssem.at[which, c, k - 1], h_rsem.at[which, c, k - 1], peer(k))

    def sender(k):
        return lax.rem(r - k + n, n)

    pl.semaphore_wait(barrier, n - 1 + nz - 1 + 1)

    x_first(x_ref)
    for s in range(1, nz):
        if s == nz - 1:
            c_first(cot_ref)
        x_stage(s)
    x_last()
    if nz == 1:
        c_first(cot_ref)
    x_save = pltpu.make_async_copy(x_full, x_out, copy_sem.at[0])
    x_save.start()

    loads[0].wait()
    loads[1].wait()

    @pl.loop(0, chunks)
    def _(c):
        gu_part[c, 0, :, :] = dot_nn(x_full[...], wg[:, block(c, ch)]).astype(BF16)
        gu_part[c, 1, :, :] = dot_nn(x_full[...], wu[:, block(c, ch)]).astype(BF16)
        for k in range(1, n):
            gu_copy(c, k).start()
        for s in range(1, nz):
            @pl.when(c == min(2 * s - 1, chunks - 1))
            def _():
                c_stage(s)

    c_last()
    cot_save = pltpu.make_async_copy(cot_full, cot_out, copy_sem.at[1])
    cot_save.start()
    loads[2].wait()

    @pl.loop(0, chunks)
    def _(c):
        d_part[c, :, :] = dot_nt(cot_full[...], wd[block(c, ch), :]).astype(BF16)
        for k in range(1, n):
            d_copy(c, k).start()

    @pl.loop(0, chunks)
    def _(c):
        gate = gu_part[c, 0, mine_rows, :].astype(F32)
        up = gu_part[c, 1, mine_rows, :].astype(F32)
        for k in range(1, n):
            gu_copy(c, k).wait_recv()
            gate += gu_recv[c, k - 1, 0].astype(F32)
            up += gu_recv[c, k - 1, 1].astype(F32)
        gu_own[c, 0] = gate
        gu_own[c, 1] = up
        act[mine_rows, block(c, ch)] = (gate * jax.nn.sigmoid(gate) * up).astype(BF16)
        for k in range(1, n):
            act_copy(c, k).start()

    @pl.loop(0, chunks)
    def _(c):
        dact = d_part[c, mine_rows, :].astype(F32)
        for k in range(1, n):
            d_copy(c, k).wait_recv()
            dact += d_recv[c, k - 1].astype(F32)
        gate, up = gu_own[c, 0], gu_own[c, 1]
        sig = jax.nn.sigmoid(gate)
        dg[mine_rows, block(c, ch)] = (
            dact * up * sig * (1.0 + gate * (1.0 - sig))
        ).astype(BF16)
        du[mine_rows, block(c, ch)] = (dact * gate * sig).astype(BF16)
        for k in range(1, n):
            h_copy(0, c, k).start()
            h_copy(1, c, k).start()

    def summing(part, sib, total, recv, sib_ssem, sib_rsem, z_ssem, z_rsem):
        def to_sibling(p):
            cols = block(p, pw)
            return remote(part.at[1 - d, :, :, cols], sib.at[:, :, cols],
                          sib_ssem.at[p], sib_rsem.at[p], sibling)

        def to_col(p, k):
            cols = block(p, pw)
            return remote(total.at[lax.rem(z + k, nz), :, cols], recv.at[k - 1, :, cols],
                          z_ssem.at[p, k - 1], z_rsem.at[p, k - 1], zpeer(k))

        def put(p, value):
            cols = block(p, pw)
            for zz in range(nz):
                for dd in range(2):
                    slot = zz * 2 + dd
                    part[dd, zz, :, cols] = value[slot * tl:(slot + 1) * tl].astype(BF16)
            to_sibling(p).start()

        def spread():
            @pl.loop(0, parts)
            def _(p):
                cols = block(p, pw)
                to_sibling(p).wait_recv()
                total[:, :, cols] = (
                    part[d, :, :, cols].astype(F32) + sib[:, :, cols].astype(F32)
                ).astype(BF16)
                for k in range(1, nz):
                    to_col(p, k).start()

        def finish(result):
            @pl.loop(0, parts)
            def _(p):
                cols = block(p, pw)
                value = total[z, :, cols].astype(F32)
                for k in range(1, nz):
                    to_col(p, k).wait_recv()
                    value += recv[k - 1, :, cols].astype(F32)
                result[:, cols] = value.astype(BF16)

        def drain():
            @pl.loop(0, parts)
            def _(p):
                to_sibling(p).wait_send()
                for k in range(1, nz):
                    to_col(p, k).wait_send()

        return put, spread, finish, drain

    o_put, o_spread, o_finish, o_drain = summing(
        o_part, o_sib, o_sum, o_recv, osib_ssem, osib_rsem, oz_ssem, oz_rsem)
    t_put, t_spread, t_finish, t_drain = summing(
        t_part, t_sib, t_sum, t_recv, tsib_ssem, tsib_rsem, tz_ssem, tz_rsem)

    @pl.loop(0, chunks)
    def _(c):
        for k in range(1, n):
            act_copy(c, k, sender(k)).wait_recv()

    act_save = pltpu.make_async_copy(act, act_out, copy_sem.at[2])
    act_save.start()

    @pl.loop(0, parts)
    def _(p):
        o_put(p, dot_nn(act[...], wd[:, block(p, pw)]))

    o_spread()

    @pl.loop(0, chunks)
    def _(c):
        for k in range(1, n):
            h_copy(0, c, k, sender(k)).wait_recv()
            h_copy(1, c, k, sender(k)).wait_recv()

    dg_save = pltpu.make_async_copy(dg, dg_out, copy_sem.at[3])
    du_save = pltpu.make_async_copy(du, du_out, copy_sem.at[4])
    dg_save.start()
    du_save.start()

    @pl.loop(0, parts)
    def _(p):
        t_put(p, dot_nt(dg[...], wg[block(p, pw), :]) + dot_nt(du[...], wu[block(p, pw), :]))

    t_spread()
    o_finish(out_ref)
    t_finish(tg_ref)

    x_drain()
    c_drain()

    @pl.loop(0, chunks)
    def _(c):
        for k in range(1, n):
            gu_copy(c, k).wait_send()
            d_copy(c, k).wait_send()
            act_copy(c, k).wait_send()
            h_copy(0, c, k).wait_send()
            h_copy(1, c, k).wait_send()

    o_drain()
    t_drain()
    for save in (x_save, cot_save, act_save, dg_save, du_save):
        save.wait()


def step_of(z, i):
    outer = (z == 0) | (z == 3)
    swap = jnp.where(outer & (i == 2), 1, 0) - jnp.where(outer & (i == 3), 1, 0)
    return i + swap


LAST = ((0, 2), (1, 0), (2, 3), (3, 1))


def last_source(z):
    return jnp.where(z == 0, 1, jnp.where(z == 1, 3, jnp.where(z == 2, 0, 2)))


def group_kernel(
    dims,
    x_ref, cot_ref, wg_hbm, wu_hbm, wd_hbm,
    base_ref, last_ref, x_out, cot_out, act_out, dg_out, du_out,
    wg, wu, wd, x_full, cot_full, part, recv, h, acc, s_part, s_sib, s_sum, s_recv,
    w_sem, copy_sem, save_sem, x_ssem, x_rsem, c_ssem, c_rsem,
    rs_ssem, rs_rsem, ag_ssem, ag_rsem, sib_ssem, sib_rsem, z_ssem, z_rsem, last_sem,
):
    nz, tl, half, pw = dims
    feats = x_full.shape[1]
    tg, tr, hw = 2 * tl, tl // 2, half // 2
    units = 2 * nz
    wide = (hw // 2 + 127) // 128 * 128
    widths = (wide, hw - wide)
    starts = (0, wide)
    r = lax.axis_index("row")
    z = lax.axis_index("col")
    d = lax.axis_index("depth")
    rx = r + 1 - 2 * (r % 2)
    ry = r + 2 - 4 * (r // 2)
    rd = 3 - r
    sibling = {"depth": 1 - d}
    way = 1 - 2 * (z // max(nz // 2, 1))

    barrier = pltpu.get_barrier_semaphore()
    for where in (rx, ry):
        pl.semaphore_signal(barrier, inc=1, device_id={"row": where}, device_id_type=MESH)
    for k in range(1, nz):
        pl.semaphore_signal(barrier, inc=1, device_id={"col": lax.rem(z + k, nz)}, device_id_type=MESH)
    pl.semaphore_signal(barrier, inc=1, device_id=sibling, device_id_type=MESH)

    def load(i, s):
        here = pl.ds(s * hw, hw)
        there = block(2 * d + s, hw)
        src, dst = (
            (wg_hbm.at[:, there], wg.at[:, here]),
            (wu_hbm.at[:, there], wu.at[:, here]),
            (wd_hbm.at[there, :], wd.at[here, :]),
        )[i]
        return pltpu.make_async_copy(src, dst, w_sem.at[i, s])

    for i in range(3):
        load(i, 0).start()

    def remote(src, dst, ssem, rsem, where):
        return pltpu.make_async_remote_copy(
            src_ref=src, dst_ref=dst, send_sem=ssem, recv_sem=rsem,
            device_id=where, device_id_type=MESH,
        )

    def index(u):
        return u // 2

    def side(u):
        return lax.rem(u, 2)

    def group(i):
        return lax.rem(z + step_of(z, i) * way + nz, nz)

    def ends(u):
        flip = lax.rem(u, 2)
        return rx + flip * (ry - rx), ry + flip * (rx - ry)

    def span_of(u, b):
        return pl.ds(pl.multiple_of(side(u) * hw + starts[b], 128), widths[b])

    def gather(full, ssem, rsem):
        def hop(zz, to):
            slot = zz * 2 + d
            ref = full.at[block(slot, tl)]
            where = ({"col": z + 1}, {"col": z - 1}, sibling)[to]
            return remote(ref, ref, ssem.at[zz, to], rsem.at[slot], where)

        def arrived(slot):
            ref = full.at[block(slot, tl)]
            remote(ref, ref, ssem.at[0, 0], rsem.at[slot], sibling).wait_recv()

        def first(shard):
            full[block(z * 2 + d, tl), :] = shard[...]
            hop(z, 2).start()

            @pl.when(z + 1 < nz)
            def _():
                hop(z, 0).start()

            @pl.when(z > 0)
            def _():
                hop(z, 1).start()

        def stage(s):
            low, high = z - s, z + s

            @pl.when(low >= 0)
            def _():
                arrived(low * 2 + d)

                @pl.when(z + 1 < nz)
                def _():
                    hop(low, 0).start()

                hop(low, 2).start()

            @pl.when(high < nz)
            def _():
                arrived(high * 2 + d)

                @pl.when(z > 0)
                def _():
                    hop(high, 1).start()

                hop(high, 2).start()

        def other(g):
            arrived(g * 2 + 1 - d)

        def drain():
            for zz in range(nz):
                @pl.when((zz <= z) & (z + 1 < nz))
                def _():
                    hop(zz, 0).wait_send()

                @pl.when((zz >= z) & (z > 0))
                def _():
                    hop(zz, 1).wait_send()

                hop(zz, 2).wait_send()

        return first, stage, other, drain

    x_first, x_stage, x_other, x_drain = gather(x_full, x_ssem, x_rsem)
    c_first, c_stage, c_other, c_drain = gather(cot_full, c_ssem, c_rsem)

    def rs(u, b, m):
        i = index(u)
        near, far = ends(u) if b == 0 else ends(u)[::-1]
        owner = (rd, near, far)[m]
        to = far if m == 2 else near
        cols = span_of(u, b)
        return remote(part.at[i, :, block(owner, tr), cols],
                      recv.at[i, m, :, :, cols],
                      rs_ssem.at[u, b, m], rs_rsem.at[u, b, m], {"row": to})

    def rows(g, owner):
        return pl.ds(pl.multiple_of(g * tg + owner * tr, tr), tr)

    def ag(u, m, incoming=False):
        g = group(index(u))
        p, q = ends(u)
        owner = (p, q, rd, rd)[m] if incoming else (r, r, p, q)[m]
        cols = block(side(u), hw) if m < 2 else span_of(u, m - 2)
        ref = h.at[:, rows(g, owner), cols]
        to = (p, q, q, p)[m]
        return remote(ref, ref, ag_ssem.at[u, m], ag_rsem.at[u, m], {"row": to})

    def to_sibling(i):
        g = group(i)
        return remote(s_part.at[g, :, 1 - d], s_sib.at[g], sib_ssem.at[i], sib_rsem.at[i], sibling)

    def to_col(i):
        g = group(i)
        k = lax.rem(z - g + nz, nz) - 1
        return remote(s_sum.at[g], s_recv.at[k], z_ssem.at[i], z_rsem.at[k], {"col": g})

    def saves(u):
        span, cols = block(group(index(u)), tg), block(side(u), hw)
        return [
            pltpu.make_async_copy(h.at[j, span, cols], out.at[span, cols], save_sem.at[u, j])
            for j, out in enumerate((act_out, dg_out, du_out))
        ]

    x_save = pltpu.make_async_copy(x_full, x_out, copy_sem.at[0])
    cot_save = pltpu.make_async_copy(cot_full, cot_out, copy_sem.at[1])

    def compute(u):
        i = index(u)
        g = group(i)
        span = block(g, tg)
        cols = block(side(u), hw)
        opens = side(u) == 0

        @pl.when(opens)
        def _():
            x_other(g)

        @pl.when(u == 0)
        def _():
            load(0, 0).wait()
            load(1, 0).wait()

        @pl.when(u == 1)
        def _():
            for k in range(3):
                load(k, 1).wait()

        part[i, 0, :, cols] = dot_nn(x_full[span, :], wg[:, cols]).astype(BF16)
        part[i, 1, :, cols] = dot_nn(x_full[span, :], wu[:, cols]).astype(BF16)

        @pl.when(opens)
        def _():
            c_other(g)

        @pl.when(u == 0)
        def _():
            load(2, 0).wait()
            for k in range(3):
                load(k, 1).start()

        part[i, 2, :, cols] = dot_nt(cot_full[span, :], wd[cols, :]).astype(BF16)

        for m in range(2):
            for b in range(2):
                rs(u, b, m).start()

    def relay(u):
        i = index(u)
        for b in range(2):
            rs(u, b, 0).wait_recv()
            spot, cols = block(ends(u)[1 - b], tr), span_of(u, b)
            part[i, :, spot, cols] = (
                part[i, :, spot, cols].astype(F32) + recv[i, 0, :, :, cols].astype(F32)
            ).astype(BF16)
            rs(u, b, 2).start()

    def hidden(u):
        i = index(u)
        own = rows(group(i), r)
        for b in range(2):
            rs(u, b, 1).wait_recv()
            rs(u, b, 2).wait_recv()
            cols = span_of(u, b)
            gate, up, dact = (
                part[i, j, block(r, tr), cols].astype(F32)
                + recv[i, 1, j, :, cols].astype(F32)
                + recv[i, 2, j, :, cols].astype(F32)
                for j in range(3)
            )
            sig = jax.nn.sigmoid(gate)
            h[0, own, cols] = (gate * sig * up).astype(BF16)
            h[1, own, cols] = (dact * up * sig * (1.0 + gate * (1.0 - sig))).astype(BF16)
            h[2, own, cols] = (dact * gate * sig).astype(BF16)
        ag(u, 0).start()
        ag(u, 1).start()

    def forward(u):
        for m in range(2):
            ag(u, m, True).wait_recv()
            ag(u, m + 2).start()

    def project(u):
        i = index(u)
        g = group(i)
        span, hid = block(g, tg), block(side(u), hw)
        ag(u, 2, True).wait_recv()
        ag(u, 3, True).wait_recv()
        for save in saves(u):
            save.start()

        def products(cols):
            out = dot_nn(h[0, span, hid], wd[hid, cols])
            grad = dot_nt(h[1, span, hid], wg[cols, hid]) + dot_nt(h[2, span, hid], wu[cols, hid])
            return out, grad

        @pl.when(side(u) == 0)
        def _():
            @pl.loop(0, feats // pw)
            def _(p):
                cols = block(p, pw)
                out, grad = products(cols)
                acc[0, :, cols] = out
                acc[1, :, cols] = grad

        @pl.when(side(u) == 1)
        def _():
            @pl.loop(0, feats // pw)
            def _(p):
                cols = block(p, pw)
                for j, value in enumerate(products(cols)):
                    value = (value + acc[j, :, cols]).astype(BF16)
                    for dd in range(2):
                        s_part[g, j, dd, :, cols] = value[dd * tl:(dd + 1) * tl]

            to_sibling(i).start()

    def spread(i):
        g = group(i)
        to_sibling(i).wait_recv()
        for j in range(2):
            s_sum[g, j] = (s_part[g, j, d].astype(F32) + s_sib[g, j].astype(F32)).astype(BF16)

        @pl.when((i > 0) & (i < nz - 1))
        def _():
            to_col(i).start()

    pl.semaphore_wait(barrier, 2 + nz - 1 + 1)
    x_first(x_ref)
    c_first(cot_ref)

    @pl.loop(0, units + 3)
    def _(t):
        @pl.when(t < units)
        def _():
            compute(t)

        @pl.when(t == units - 2)
        def _():
            x_save.start()
            cot_save.start()

        @pl.when((t >= 2) & (t < units + 2))
        def _():
            forward(t - 2)

        @pl.when((t >= 1) & (t < units + 1))
        def _():
            hidden(t - 1)

        @pl.when(t >= 3)
        def _():
            project(t - 3)

        @pl.when(t < units)
        def _():
            relay(t)

        @pl.when((t > 0) & (t < nz))
        def _():
            x_stage(t)
            c_stage(t)

        @pl.when((t >= 4) & (lax.rem(t, 2) == 0))
        def _():
            spread(t // 2 - 2)

    to_last = pltpu.make_async_copy(s_sum.at[group(nz - 1)], last_ref, last_sem)
    to_last.start()
    late = lax.rem(last_source(z) - z + nz, nz) - 1

    def landed(k):
        remote(s_sum.at[0], s_recv.at[k], z_ssem.at[0], z_rsem.at[k], sibling).wait_recv()

    for k in range(nz - 1):
        @pl.when(k != late)
        def _():
            landed(k)

    value = s_sum[z].astype(F32)
    for k in range(1, nz - 1):
        value += s_recv[lax.rem(late + k, nz - 1)].astype(F32)
    base_ref[...] = value

    x_drain()
    c_drain()

    @pl.loop(0, units)
    def _(u):
        for b in range(2):
            for m in range(3):
                rs(u, b, m).wait_send()
        for m in range(4):
            ag(u, m).wait_send()
        for save in saves(u):
            save.wait()

    @pl.loop(0, nz)
    def _(i):
        to_sibling(i).wait_send()

        @pl.when((i > 0) & (i < nz - 1))
        def _():
            to_col(i).wait_send()

    x_save.wait()
    cot_save.wait()
    to_last.wait()


def per_device(n, nz, tokens, gate_weight, up_weight, down_weight, cotangent):
    tl, feats = tokens.shape
    half = gate_weight.shape[1] // 2
    total = tl * nz * 2
    tr = total // n
    ch = 256 if half % 256 == 0 else half
    chunks = half // ch
    pw = 512 if feats % 512 == 0 else feats
    parts = feats // pw
    sliced = half % 128 != 0
    if sliced:
        start = lax.axis_index("depth") * half
        weights = (
            lax.dynamic_slice_in_dim(gate_weight, start, half, 1),
            lax.dynamic_slice_in_dim(up_weight, start, half, 1),
            lax.dynamic_slice_in_dim(down_weight, start, half, 0),
        )
    else:
        weights = (gate_weight, up_weight, down_weight)

    def sds(*shape):
        return jax.ShapeDtypeStruct(shape, BF16)

    def buf(*shape):
        return pltpu.VMEM(shape, BF16)

    def sem(*shape):
        return pltpu.SemaphoreType.DMA(shape)

    vmem = pl.BlockSpec(memory_space=pltpu.VMEM)
    hbm = pl.BlockSpec(memory_space=pl.ANY)
    if n == 4 and nz == 4 and tl % 32 == 0 and half % 256 == 0 and half >= 512:
        base, last, x_both, cot_both, act, dgate, dup = pl.pallas_call(
            functools.partial(group_kernel, (nz, tl, half, 2 * pw if parts % 2 == 0 else pw)),
            out_shape=(
                jax.ShapeDtypeStruct((2, tl, feats), F32), sds(2, tl, feats),
                sds(total, feats), sds(total, feats),
                sds(total, half), sds(total, half), sds(total, half),
            ),
            in_specs=[vmem, vmem, hbm, hbm, hbm],
            out_specs=(vmem, hbm, hbm, hbm, hbm, hbm, hbm),
            scratch_shapes=[
                buf(feats, half), buf(feats, half), buf(half, feats),
                buf(total, feats), buf(total, feats),
                buf(nz, 3, 2 * tl, half), buf(nz, 3, 3, tl // 2, half),
                buf(3, total, half), pltpu.VMEM((2, 2 * tl, feats), F32),
                buf(nz, 2, 2, tl, feats), buf(nz, 2, tl, feats), buf(nz, 2, tl, feats),
                buf(max(nz - 1, 1), 2, tl, feats),
                sem(3, 2), sem(2), sem(2 * nz, 3),
                sem(nz, 3), sem(nz * 2), sem(nz, 3), sem(nz * 2),
                sem(2 * nz, 2, 3), sem(2 * nz, 2, 3), sem(2 * nz, 4), sem(2 * nz, 4),
                sem(nz), sem(nz), sem(nz), sem(nz), pltpu.SemaphoreType.DMA,
            ],
            compiler_params=pltpu.CompilerParams(
                collective_id=1, has_side_effects=True, vmem_limit_bytes=60 * 2**20
            ),
            cost_estimate=pl.CostEstimate(
                flops=12 * total * feats * half, bytes_accessed=8 * feats * half,
                transcendentals=0,
            ),
        )(tokens, cotangent, *weights)
        sent = lax.ppermute(last, "col", LAST)
        total_sums = (base + sent.astype(F32)).astype(BF16)
        output, tokens_grad = total_sums[0], total_sums[1]
    else:
        sums = [
            buf(2, nz, tl, feats), buf(nz, tl, feats), buf(nz, tl, feats),
            buf(max(nz - 1, 1), tl, feats),
        ]
        sum_sems = [sem(parts), sem(parts), sem(parts, nz), sem(parts, nz)]
        output, tokens_grad, x_both, cot_both, act, dgate, dup = pl.pallas_call(
            functools.partial(kernel, (n, nz, tl, tr, chunks, ch, parts, pw, sliced)),
            out_shape=(
                sds(tl, feats), sds(tl, feats), sds(total, feats), sds(total, feats),
                sds(total, half), sds(total, half), sds(total, half),
            ),
            in_specs=[vmem, vmem, hbm, hbm, hbm],
            out_specs=(vmem, vmem, hbm, hbm, hbm, hbm, hbm),
            scratch_shapes=[
                buf(feats, half), buf(feats, half), buf(half, feats),
                buf(total, feats), buf(total, feats),
                buf(chunks, 2, total, ch), buf(chunks, n - 1, 2, tr, ch),
                buf(chunks, total, ch), buf(chunks, n - 1, tr, ch),
                pltpu.VMEM((chunks, 2, tr, ch), F32),
                buf(total, half), buf(total, half), buf(total, half),
                *sums, *sums,
                sem(3), sem(5),
                sem(nz, 3), sem(nz * 2), sem(nz, 3), sem(nz * 2),
                sem(chunks, n - 1), sem(chunks, n - 1),
                sem(chunks, n - 1), sem(chunks, n - 1),
                sem(chunks, n - 1), sem(chunks, n - 1),
                sem(2, chunks, n - 1), sem(2, chunks, n - 1),
                *sum_sems, *sum_sems,
            ],
            compiler_params=pltpu.CompilerParams(
                collective_id=0, has_side_effects=True, vmem_limit_bytes=60 * 2**20
            ),
            cost_estimate=pl.CostEstimate(
                flops=12 * total * feats * half, bytes_accessed=8 * feats * half,
                transcendentals=0,
            ),
        )(tokens, cotangent, *weights)
    gate_grad = dot_tn(x_both, dgate)
    up_grad = dot_tn(x_both, dup)
    down_grad = dot_tn(act, cot_both)
    return (
        output,
        tokens_grad,
        gate_grad.astype(BF16),
        up_grad.astype(BF16),
        down_grad.astype(BF16),
    )


def solution(mesh):
    return jax.shard_map(
        functools.partial(per_device, mesh.shape["row"], mesh.shape["col"]),
        mesh=mesh,
        in_specs=(
            P(("col", "depth"), "row"),
            P("row", "col"),
            P("row", "col"),
            P("col", "row"),
            P(("col", "depth"), "row"),
        ),
        out_specs=(
            P(("col", "depth"), "row"),
            P(("col", "depth"), "row"),
            P("row", ("col", "depth")),
            P("row", ("col", "depth")),
            P(("col", "depth"), "row"),
        ),
        check_vma=False,
    )
```

```python
import functools

import jax
import jax.numpy as jnp
from jax import lax
from jax.experimental import pallas as pl
from jax.experimental.pallas import tpu as pltpu
from jax.sharding import PartitionSpec as P

MESH = pl.DeviceIdType.MESH
BF16 = jnp.bfloat16
F32 = jnp.float32


def dot_nn(left, right):
    return jnp.dot(left, right, preferred_element_type=F32)


def dot_nt(left, right):
    return lax.dot_general(
        left, right, (((1,), (1,)), ((), ())), preferred_element_type=F32
    )


def dot_tn(left, right):
    return lax.dot_general(
        left, right, (((0,), (0,)), ((), ())), preferred_element_type=F32
    )


def block(index, size):
    return pl.ds(pl.multiple_of(index * size, size), size)


def kernel(
    dims,
    x_ref, cot_ref, wg_hbm, wu_hbm, wd_hbm,
    out_ref, tg_ref, x_out, cot_out, act_out, dg_out, du_out,
    wg, wu, wd, x_full, cot_full,
    gu_part, gu_recv, d_part, d_recv, gu_own, act, dg, du,
    o_part, o_sib, o_sum, o_recv, t_part, t_sib, t_sum, t_recv,
    w_sem, copy_sem, x_ssem, x_rsem, c_ssem, c_rsem,
    gu_ssem, gu_rsem, d_ssem, d_rsem, act_ssem, act_rsem, h_ssem, h_rsem,
    osib_ssem, osib_rsem, oz_ssem, oz_rsem,
    tsib_ssem, tsib_rsem, tz_ssem, tz_rsem,
):
    n, nz, tl, tr, chunks, ch, parts, pw, sliced = dims
    r = lax.axis_index("row")
    z = lax.axis_index("col")
    d = lax.axis_index("depth")
    half = chunks * ch

    def peer(k):
        return {"row": lax.rem(r + k, n)}

    def zpeer(k):
        return {"col": lax.rem(z + k, nz)}

    sibling = {"depth": 1 - d}

    barrier = pltpu.get_barrier_semaphore()
    for k in range(1, n):
        pl.semaphore_signal(barrier, inc=1, device_id=peer(k), device_id_type=MESH)
    for k in range(1, nz):
        pl.semaphore_signal(barrier, inc=1, device_id=zpeer(k), device_id_type=MESH)
    pl.semaphore_signal(barrier, inc=1, device_id=sibling, device_id_type=MESH)

    if sliced:
        sources = (wg_hbm, wu_hbm, wd_hbm)
    else:
        mine = block(d, half)
        sources = (wg_hbm.at[:, mine], wu_hbm.at[:, mine], wd_hbm.at[mine, :])
    loads = [
        pltpu.make_async_copy(src, dst, w_sem.at[i])
        for i, (src, dst) in enumerate(zip(sources, (wg, wu, wd)))
    ]
    for load in loads:
        load.start()

    def remote(src, dst, ssem, rsem, where):
        return pltpu.make_async_remote_copy(
            src_ref=src, dst_ref=dst, send_sem=ssem, recv_sem=rsem,
            device_id=where, device_id_type=MESH,
        )

    def gather(full, ssem, rsem):
        def hop(zz, way):
            slot = zz * 2 + d
            ref = full.at[block(slot, tl)]
            where = ({"col": z + 1}, {"col": z - 1}, sibling)[way]
            return remote(ref, ref, ssem.at[zz, way], rsem.at[slot], where)

        def arrived(slot):
            ref = full.at[block(slot, tl)]
            remote(ref, ref, ssem.at[0, 0], rsem.at[slot], sibling).wait_recv()

        def first(shard):
            full[block(z * 2 + d, tl), :] = shard[...]

            @pl.when(z + 1 < nz)
            def _():
                hop(z, 0).start()

            @pl.when(z > 0)
            def _():
                hop(z, 1).start()

            hop(z, 2).start()

        def stage(s):
            low, high = z - s, z + s

            @pl.when(low >= 0)
            def _():
                arrived(low * 2 + d)

                @pl.when(z + 1 < nz)
                def _():
                    hop(low, 0).start()

                hop(low, 2).start()

            @pl.when(high < nz)
            def _():
                arrived(high * 2 + d)

                @pl.when(z > 0)
                def _():
                    hop(high, 1).start()

                hop(high, 2).start()

        def last():
            for zz in range(nz):
                arrived(zz * 2 + 1 - d)

        def drain():
            for zz in range(nz):
                @pl.when((zz <= z) & (z + 1 < nz))
                def _():
                    hop(zz, 0).wait_send()

                @pl.when((zz >= z) & (z > 0))
                def _():
                    hop(zz, 1).wait_send()

                hop(zz, 2).wait_send()

        return first, stage, last, drain

    x_first, x_stage, x_last, x_drain = gather(x_full, x_ssem, x_rsem)
    c_first, c_stage, c_last, c_drain = gather(cot_full, c_ssem, c_rsem)

    def gu_copy(c, k):
        rows = block(lax.rem(r + k, n), tr)
        return remote(gu_part.at[c, :, rows, :], gu_recv.at[c, k - 1],
                      gu_ssem.at[c, k - 1], gu_rsem.at[c, k - 1], peer(k))

    def d_copy(c, k):
        rows = block(lax.rem(r + k, n), tr)
        return remote(d_part.at[c, rows, :], d_recv.at[c, k - 1],
                      d_ssem.at[c, k - 1], d_rsem.at[c, k - 1], peer(k))

    mine_rows = block(r, tr)

    def act_copy(c, k, owner=None):
        rows = mine_rows if owner is None else block(owner, tr)
        ref = act.at[rows, block(c, ch)]
        return remote(ref, ref, act_ssem.at[c, k - 1], act_rsem.at[c, k - 1], peer(k))

    def h_copy(which, c, k, owner=None):
        rows = mine_rows if owner is None else block(owner, tr)
        ref = (dg, du)[which].at[rows, block(c, ch)]
        return remote(ref, ref, h_ssem.at[which, c, k - 1], h_rsem.at[which, c, k - 1], peer(k))

    def sender(k):
        return lax.rem(r - k + n, n)

    pl.semaphore_wait(barrier, n - 1 + nz - 1 + 1)

    x_first(x_ref)
    for s in range(1, nz):
        if s == nz - 1:
            c_first(cot_ref)
        x_stage(s)
    x_last()
    if nz == 1:
        c_first(cot_ref)
    x_save = pltpu.make_async_copy(x_full, x_out, copy_sem.at[0])
    x_save.start()

    loads[0].wait()
    loads[1].wait()

    @pl.loop(0, chunks)
    def _(c):
        gu_part[c, 0, :, :] = dot_nn(x_full[...], wg[:, block(c, ch)]).astype(BF16)
        gu_part[c, 1, :, :] = dot_nn(x_full[...], wu[:, block(c, ch)]).astype(BF16)
        for k in range(1, n):
            gu_copy(c, k).start()
        for s in range(1, nz):
            @pl.when(c == min(2 * s - 1, chunks - 1))
            def _():
                c_stage(s)

    c_last()
    cot_save = pltpu.make_async_copy(cot_full, cot_out, copy_sem.at[1])
    cot_save.start()
    loads[2].wait()

    @pl.loop(0, chunks)
    def _(c):
        d_part[c, :, :] = dot_nt(cot_full[...], wd[block(c, ch), :]).astype(BF16)
        for k in range(1, n):
            d_copy(c, k).start()

    @pl.loop(0, chunks)
    def _(c):
        gate = gu_part[c, 0, mine_rows, :].astype(F32)
        up = gu_part[c, 1, mine_rows, :].astype(F32)
        for k in range(1, n):
            gu_copy(c, k).wait_recv()
            gate += gu_recv[c, k - 1, 0].astype(F32)
            up += gu_recv[c, k - 1, 1].astype(F32)
        gu_own[c, 0] = gate
        gu_own[c, 1] = up
        act[mine_rows, block(c, ch)] = (gate * jax.nn.sigmoid(gate) * up).astype(BF16)
        for k in range(1, n):
            act_copy(c, k).start()

    @pl.loop(0, chunks)
    def _(c):
        dact = d_part[c, mine_rows, :].astype(F32)
        for k in range(1, n):
            d_copy(c, k).wait_recv()
            dact += d_recv[c, k - 1].astype(F32)
        gate, up = gu_own[c, 0], gu_own[c, 1]
        sig = jax.nn.sigmoid(gate)
        dg[mine_rows, block(c, ch)] = (
            dact * up * sig * (1.0 + gate * (1.0 - sig))
        ).astype(BF16)
        du[mine_rows, block(c, ch)] = (dact * gate * sig).astype(BF16)
        for k in range(1, n):
            h_copy(0, c, k).start()
            h_copy(1, c, k).start()

    def summing(part, sib, total, recv, sib_ssem, sib_rsem, z_ssem, z_rsem):
        def to_sibling(p):
            cols = block(p, pw)
            return remote(part.at[1 - d, :, :, cols], sib.at[:, :, cols],
                          sib_ssem.at[p], sib_rsem.at[p], sibling)

        def to_col(p, k):
            cols = block(p, pw)
            return remote(total.at[lax.rem(z + k, nz), :, cols], recv.at[k - 1, :, cols],
                          z_ssem.at[p, k - 1], z_rsem.at[p, k - 1], zpeer(k))

        def put(p, value):
            cols = block(p, pw)
            for zz in range(nz):
                for dd in range(2):
                    slot = zz * 2 + dd
                    part[dd, zz, :, cols] = value[slot * tl:(slot + 1) * tl].astype(BF16)
            to_sibling(p).start()

        def spread():
            @pl.loop(0, parts)
            def _(p):
                cols = block(p, pw)
                to_sibling(p).wait_recv()
                total[:, :, cols] = (
                    part[d, :, :, cols].astype(F32) + sib[:, :, cols].astype(F32)
                ).astype(BF16)
                for k in range(1, nz):
                    to_col(p, k).start()

        def finish(result):
            @pl.loop(0, parts)
            def _(p):
                cols = block(p, pw)
                value = total[z, :, cols].astype(F32)
                for k in range(1, nz):
                    to_col(p, k).wait_recv()
                    value += recv[k - 1, :, cols].astype(F32)
                result[:, cols] = value.astype(BF16)

        def drain():
            @pl.loop(0, parts)
            def _(p):
                to_sibling(p).wait_send()
                for k in range(1, nz):
                    to_col(p, k).wait_send()

        return put, spread, finish, drain

    o_put, o_spread, o_finish, o_drain = summing(
        o_part, o_sib, o_sum, o_recv, osib_ssem, osib_rsem, oz_ssem, oz_rsem)
    t_put, t_spread, t_finish, t_drain = summing(
        t_part, t_sib, t_sum, t_recv, tsib_ssem, tsib_rsem, tz_ssem, tz_rsem)

    @pl.loop(0, chunks)
    def _(c):
        for k in range(1, n):
            act_copy(c, k, sender(k)).wait_recv()

    act_save = pltpu.make_async_copy(act, act_out, copy_sem.at[2])
    act_save.start()

    @pl.loop(0, parts)
    def _(p):
        o_put(p, dot_nn(act[...], wd[:, block(p, pw)]))

    o_spread()

    @pl.loop(0, chunks)
    def _(c):
        for k in range(1, n):
            h_copy(0, c, k, sender(k)).wait_recv()
            h_copy(1, c, k, sender(k)).wait_recv()

    dg_save = pltpu.make_async_copy(dg, dg_out, copy_sem.at[3])
    du_save = pltpu.make_async_copy(du, du_out, copy_sem.at[4])
    dg_save.start()
    du_save.start()

    @pl.loop(0, parts)
    def _(p):
        t_put(p, dot_nt(dg[...], wg[block(p, pw), :]) + dot_nt(du[...], wu[block(p, pw), :]))

    t_spread()
    o_finish(out_ref)
    t_finish(tg_ref)

    x_drain()
    c_drain()

    @pl.loop(0, chunks)
    def _(c):
        for k in range(1, n):
            gu_copy(c, k).wait_send()
            d_copy(c, k).wait_send()
            act_copy(c, k).wait_send()
            h_copy(0, c, k).wait_send()
            h_copy(1, c, k).wait_send()

    o_drain()
    t_drain()
    for save in (x_save, cot_save, act_save, dg_save, du_save):
        save.wait()


VISITS = (0, 2, 3, 1)
LAST = tuple((z, (z + VISITS[3]) % 4) for z in range(4))


def group_kernel(
    dims,
    x_ref, cot_ref, wg_hbm, wu_hbm, wd_hbm,
    base_ref, last_ref, x_out, cot_out, act_out, dg_out, du_out,
    wg, wu, wd, x_full, cot_full, part, recv, h, acc, s_part, s_sib, s_sum, s_recv,
    w_sem, copy_sem, save_sem, x_ssem, x_rsem, c_ssem, c_rsem,
    rs_ssem, rs_rsem, ag_ssem, ag_rsem, sib_ssem, sib_rsem, z_ssem, z_rsem, last_sem,
):
    nz, tl, half, pw = dims
    feats = x_full.shape[1]
    tg, tr, hw = 2 * tl, tl // 2, half // 2
    units = 2 * nz
    wide = (hw // 2 + 127) // 128 * 128
    widths = (wide, hw - wide)
    starts = (0, wide)
    r = lax.axis_index("row")
    z = lax.axis_index("col")
    d = lax.axis_index("depth")
    rx = r + 1 - 2 * (r % 2)
    ry = r + 2 - 4 * (r // 2)
    rd = 3 - r
    sibling = {"depth": 1 - d}

    barrier = pltpu.get_barrier_semaphore()
    for where in (rx, ry):
        pl.semaphore_signal(barrier, inc=1, device_id={"row": where}, device_id_type=MESH)
    for k in range(1, nz):
        pl.semaphore_signal(barrier, inc=1, device_id={"col": lax.rem(z + k, nz)}, device_id_type=MESH)
    pl.semaphore_signal(barrier, inc=1, device_id=sibling, device_id_type=MESH)

    def load(i, s):
        here = block(s, hw)
        there = block(2 * d + s, hw)
        src, dst = (
            (wg_hbm.at[:, there], wg.at[:, here]),
            (wu_hbm.at[:, there], wu.at[:, here]),
            (wd_hbm.at[there, :], wd.at[here, :]),
        )[i]
        return pltpu.make_async_copy(src, dst, w_sem.at[i, s])

    for i in range(3):
        load(i, 0).start()

    def remote(src, dst, ssem, rsem, where):
        return pltpu.make_async_remote_copy(
            src_ref=src, dst_ref=dst, send_sem=ssem, recv_sem=rsem,
            device_id=where, device_id_type=MESH,
        )

    def index(u):
        return u // 2

    def side(u):
        return lax.rem(u, 2)

    def group(i):
        if isinstance(i, int):
            return lax.rem(z + VISITS[i], nz)
        away = jnp.where(i == 0, 0, jnp.where(i == 3, 1, i + 1))
        return lax.rem(z + away, nz)

    def ends(u):
        flip = lax.rem(u, 2)
        return rx + flip * (ry - rx), ry + flip * (rx - ry)

    def span_of(u, b):
        return pl.ds(pl.multiple_of(side(u) * hw + starts[b], 128), widths[b])

    def gather(full, ssem, rsem):
        def hop(zz, to):
            slot = zz * 2 + d
            ref = full.at[block(slot, tl)]
            where = ({"col": z + 1}, {"col": z - 1}, sibling)[to]
            return remote(ref, ref, ssem.at[zz, to], rsem.at[slot], where)

        def arrived(slot):
            ref = full.at[block(slot, tl)]
            remote(ref, ref, ssem.at[0, 0], rsem.at[slot], sibling).wait_recv()

        def first(shard):
            full[block(z * 2 + d, tl), :] = shard[...]
            hop(z, 2).start()

            @pl.when(z + 1 < nz)
            def _():
                hop(z, 0).start()

            @pl.when(z > 0)
            def _():
                hop(z, 1).start()

        def stage(s):
            low, high = z - s, z + s

            @pl.when(low >= 0)
            def _():
                arrived(low * 2 + d)

                @pl.when(z + 1 < nz)
                def _():
                    hop(low, 0).start()

                hop(low, 2).start()

            @pl.when(high < nz)
            def _():
                arrived(high * 2 + d)

                @pl.when(z > 0)
                def _():
                    hop(high, 1).start()

                hop(high, 2).start()

        def other(g):
            arrived(g * 2 + 1 - d)

        def drain():
            for zz in range(nz):
                @pl.when((zz <= z) & (z + 1 < nz))
                def _():
                    hop(zz, 0).wait_send()

                @pl.when((zz >= z) & (z > 0))
                def _():
                    hop(zz, 1).wait_send()

                hop(zz, 2).wait_send()

        return first, stage, other, drain

    x_first, x_stage, x_other, x_drain = gather(x_full, x_ssem, x_rsem)
    c_first, c_stage, c_other, c_drain = gather(cot_full, c_ssem, c_rsem)

    def rs(u, b, m):
        i = index(u)
        near, far = ends(u) if b == 0 else ends(u)[::-1]
        slot = m if m < 3 else m - 3
        owner = (rd, near, far)[slot]
        to = far if m == 2 else near
        cols = span_of(u, b)
        which = (pl.ds(0, 2), pl.ds(0, 2), pl.ds(0, 3), pl.ds(2, 1), pl.ds(2, 1))[m]
        return remote(part.at[i, which, block(owner, tr), cols],
                      recv.at[i, slot, which, :, cols],
                      rs_ssem.at[u, b, m], rs_rsem.at[u, b, m], {"row": to})

    def rows(g, owner):
        return pl.ds(pl.multiple_of(g * tg + owner * tr, tr), tr)

    def ag(u, m, incoming=False):
        g = group(index(u))
        p, q = ends(u)
        owner = (p, q, rd, rd)[m] if incoming else (r, r, p, q)[m]
        cols = block(side(u), hw) if m < 2 else span_of(u, m - 2)
        ref = h.at[:, rows(g, owner), cols]
        to = (p, q, q, p)[m]
        return remote(ref, ref, ag_ssem.at[u, m], ag_rsem.at[u, m], {"row": to})

    def to_sibling(i):
        g = group(i)
        return remote(s_part.at[g, :, 1 - d], s_sib.at[g], sib_ssem.at[i], sib_rsem.at[i], sibling)

    def to_col(i):
        g = group(i)
        k = lax.rem(z - g + nz, nz) - 1
        return remote(s_sum.at[g], s_recv.at[k], z_ssem.at[i], z_rsem.at[k], {"col": g})

    def saves(u):
        span, cols = block(group(index(u)), tg), block(side(u), hw)
        return [
            pltpu.make_async_copy(h.at[j, span, cols], out.at[span, cols], save_sem.at[u, j])
            for j, out in enumerate((act_out, dg_out, du_out))
        ]

    x_save = pltpu.make_async_copy(x_full, x_out, copy_sem.at[0])
    cot_save = pltpu.make_async_copy(cot_full, cot_out, copy_sem.at[1])

    def gate_up(u):
        i = index(u)
        g = group(i)
        span = block(g, tg)
        cols = block(side(u), hw)

        @pl.when((u == 2) | (u == 4))
        def _():
            x_stage(1 + u // 2)

        @pl.when(side(u) == 0)
        def _():
            x_other(g)

        @pl.when(u < 2)
        def _():
            load(0, u).wait()
            load(1, u).wait()

        part[i, 0, :, cols] = dot_nn(x_full[span, :], wg[:, cols]).astype(BF16)
        part[i, 1, :, cols] = dot_nn(x_full[span, :], wu[:, cols]).astype(BF16)
        for m in range(2):
            for b in range(2):
                rs(u, b, m).start()

    def hidden_grad(u):
        i = index(u)
        g = group(i)
        span = block(g, tg)
        cols = block(side(u), hw)

        @pl.when((u == 2) | (u == 4))
        def _():
            c_stage(1 + u // 2)

        @pl.when(side(u) == 0)
        def _():
            c_other(g)

        @pl.when(u < 2)
        def _():
            load(2, u).wait()

        @pl.when(u == 0)
        def _():
            for k in range(3):
                load(k, 1).start()

        part[i, 2, :, cols] = dot_nt(cot_full[span, :], wd[cols, :]).astype(BF16)
        for m in range(3, 5):
            for b in range(2):
                rs(u, b, m).start()

    def relay(u):
        i = index(u)
        for b in range(2):
            rs(u, b, 0).wait_recv()
            rs(u, b, 3).wait_recv()
            spot, cols = block(ends(u)[1 - b], tr), span_of(u, b)
            part[i, :, spot, cols] = (
                part[i, :, spot, cols].astype(F32) + recv[i, 0, :, :, cols].astype(F32)
            ).astype(BF16)
            rs(u, b, 2).start()

    def hidden(u):
        i = index(u)
        own = rows(group(i), r)
        for b in range(2):
            for m in (1, 4, 2):
                rs(u, b, m).wait_recv()
            cols = span_of(u, b)
            gate, up, dact = (
                part[i, j, block(r, tr), cols].astype(F32)
                + recv[i, 1, j, :, cols].astype(F32)
                + recv[i, 2, j, :, cols].astype(F32)
                for j in range(3)
            )
            sig = jax.nn.sigmoid(gate)
            h[0, own, cols] = (gate * sig * up).astype(BF16)
            h[1, own, cols] = (dact * up * sig * (1.0 + gate * (1.0 - sig))).astype(BF16)
            h[2, own, cols] = (dact * gate * sig).astype(BF16)
        ag(u, 0).start()
        ag(u, 1).start()

    def forward(u):
        for m in range(2):
            ag(u, m, True).wait_recv()
            ag(u, m + 2).start()

    def project(u):
        i = index(u)
        g = group(i)
        span, hid = block(g, tg), block(side(u), hw)
        ag(u, 2, True).wait_recv()
        ag(u, 3, True).wait_recv()
        for save in saves(u):
            save.start()

        def products(cols):
            out = dot_nn(h[0, span, hid], wd[hid, cols])
            grad = dot_nt(h[1, span, hid], wg[cols, hid]) + dot_nt(h[2, span, hid], wu[cols, hid])
            return out, grad

        @pl.when(side(u) == 0)
        def _():
            @pl.loop(0, feats // pw)
            def _(p):
                cols = block(p, pw)
                out, grad = products(cols)
                acc[0, :, cols] = out
                acc[1, :, cols] = grad

        @pl.when(side(u) == 1)
        def _():
            @pl.loop(0, feats // pw)
            def _(p):
                cols = block(p, pw)
                for j, value in enumerate(products(cols)):
                    value = (value + acc[j, :, cols]).astype(BF16)
                    for dd in range(2):
                        s_part[g, j, dd, :, cols] = value[dd * tl:(dd + 1) * tl]

            to_sibling(i).start()

    def spread(i):
        g = group(i)
        to_sibling(i).wait_recv()
        for j in range(2):
            s_sum[g, j] = (s_part[g, j, d].astype(F32) + s_sib[g, j].astype(F32)).astype(BF16)

        @pl.when((i > 0) & (i < nz - 1))
        def _():
            to_col(i).start()

    pl.semaphore_wait(barrier, 2 + nz - 1 + 1)
    x_first(x_ref)
    c_first(cot_ref)

    @pl.loop(0, units + 3)
    def _(t):
        @pl.when(t < units)
        def _():
            gate_up(t)

        @pl.when((t >= 2) & (t < units + 2))
        def _():
            forward(t - 2)

        @pl.when(t < units)
        def _():
            hidden_grad(t)

        @pl.when((t >= 1) & (t < units + 1))
        def _():
            hidden(t - 1)

        @pl.when(t >= 3)
        def _():
            project(t - 3)

        @pl.when(t == 1)
        def _():
            c_stage(1)

        @pl.when(t < units)
        def _():
            relay(t)

        @pl.when(t == 0)
        def _():
            x_stage(1)

        @pl.when(t == units - 2)
        def _():
            x_save.start()
            cot_save.start()

        @pl.when((t >= 4) & (lax.rem(t, 2) == 0))
        def _():
            spread(t // 2 - 2)

    to_last = pltpu.make_async_copy(s_sum.at[group(nz - 1)], last_ref, last_sem)
    to_last.start()

    def landed(k):
        remote(s_sum.at[0], s_recv.at[k], z_ssem.at[0], z_rsem.at[k], sibling).wait_recv()

    for k in range(nz - 2):
        landed(k)

    value = s_sum[z].astype(F32)
    for k in range(nz - 2):
        value += s_recv[k].astype(F32)
    base_ref[...] = value

    x_drain()
    c_drain()

    @pl.loop(0, units)
    def _(u):
        for b in range(2):
            for m in range(5):
                rs(u, b, m).wait_send()
        for m in range(4):
            ag(u, m).wait_send()
        for save in saves(u):
            save.wait()

    @pl.loop(0, nz)
    def _(i):
        to_sibling(i).wait_send()

        @pl.when((i > 0) & (i < nz - 1))
        def _():
            to_col(i).wait_send()

    x_save.wait()
    cot_save.wait()
    to_last.wait()


def per_device(n, nz, tokens, gate_weight, up_weight, down_weight, cotangent):
    tl, feats = tokens.shape
    half = gate_weight.shape[1] // 2
    total = tl * nz * 2
    tr = total // n
    ch = 256 if half % 256 == 0 else half
    chunks = half // ch
    pw = 512 if feats % 512 == 0 else feats
    parts = feats // pw
    sliced = half % 128 != 0
    if sliced:
        start = lax.axis_index("depth") * half
        weights = (
            lax.dynamic_slice_in_dim(gate_weight, start, half, 1),
            lax.dynamic_slice_in_dim(up_weight, start, half, 1),
            lax.dynamic_slice_in_dim(down_weight, start, half, 0),
        )
    else:
        weights = (gate_weight, up_weight, down_weight)

    def sds(*shape):
        return jax.ShapeDtypeStruct(shape, BF16)

    def buf(*shape):
        return pltpu.VMEM(shape, BF16)

    def sem(*shape):
        return pltpu.SemaphoreType.DMA(shape)

    vmem = pl.BlockSpec(memory_space=pltpu.VMEM)
    hbm = pl.BlockSpec(memory_space=pl.ANY)
    if n == 4 and nz == 4 and tl % 32 == 0 and half % 256 == 0 and half >= 512:
        base, last, x_both, cot_both, act, dgate, dup = pl.pallas_call(
            functools.partial(group_kernel, (nz, tl, half, 2 * pw if parts % 2 == 0 else pw)),
            out_shape=(
                jax.ShapeDtypeStruct((2, tl, feats), F32), sds(2, tl, feats),
                sds(total, feats), sds(total, feats),
                sds(total, half), sds(total, half), sds(total, half),
            ),
            in_specs=[vmem, vmem, hbm, hbm, hbm],
            out_specs=(vmem, hbm, hbm, hbm, hbm, hbm, hbm),
            scratch_shapes=[
                buf(feats, half), buf(feats, half), buf(half, feats),
                buf(total, feats), buf(total, feats),
                buf(nz, 3, 2 * tl, half), buf(nz, 3, 3, tl // 2, half),
                buf(3, total, half), pltpu.VMEM((2, 2 * tl, feats), F32),
                buf(nz, 2, 2, tl, feats), buf(nz, 2, tl, feats), buf(nz, 2, tl, feats),
                buf(nz - 2, 2, tl, feats),
                sem(3, 2), sem(2), sem(2 * nz, 3),
                sem(nz, 3), sem(nz * 2), sem(nz, 3), sem(nz * 2),
                sem(2 * nz, 2, 5), sem(2 * nz, 2, 5), sem(2 * nz, 4), sem(2 * nz, 4),
                sem(nz), sem(nz), sem(nz), sem(nz), pltpu.SemaphoreType.DMA,
            ],
            compiler_params=pltpu.CompilerParams(
                collective_id=1, has_side_effects=True, vmem_limit_bytes=60 * 2**20
            ),
            cost_estimate=pl.CostEstimate(
                flops=12 * total * feats * half, bytes_accessed=8 * feats * half,
                transcendentals=0,
            ),
        )(tokens, cotangent, *weights)
        sent = lax.ppermute(last, "col", LAST)
        total_sums = (base + sent.astype(F32)).astype(BF16)
        output, tokens_grad = total_sums[0], total_sums[1]
    else:
        sums = [
            buf(2, nz, tl, feats), buf(nz, tl, feats), buf(nz, tl, feats),
            buf(max(nz - 1, 1), tl, feats),
        ]
        sum_sems = [sem(parts), sem(parts), sem(parts, nz), sem(parts, nz)]
        output, tokens_grad, x_both, cot_both, act, dgate, dup = pl.pallas_call(
            functools.partial(kernel, (n, nz, tl, tr, chunks, ch, parts, pw, sliced)),
            out_shape=(
                sds(tl, feats), sds(tl, feats), sds(total, feats), sds(total, feats),
                sds(total, half), sds(total, half), sds(total, half),
            ),
            in_specs=[vmem, vmem, hbm, hbm, hbm],
            out_specs=(vmem, vmem, hbm, hbm, hbm, hbm, hbm),
            scratch_shapes=[
                buf(feats, half), buf(feats, half), buf(half, feats),
                buf(total, feats), buf(total, feats),
                buf(chunks, 2, total, ch), buf(chunks, n - 1, 2, tr, ch),
                buf(chunks, total, ch), buf(chunks, n - 1, tr, ch),
                pltpu.VMEM((chunks, 2, tr, ch), F32),
                buf(total, half), buf(total, half), buf(total, half),
                *sums, *sums,
                sem(3), sem(5),
                sem(nz, 3), sem(nz * 2), sem(nz, 3), sem(nz * 2),
                sem(chunks, n - 1), sem(chunks, n - 1),
                sem(chunks, n - 1), sem(chunks, n - 1),
                sem(chunks, n - 1), sem(chunks, n - 1),
                sem(2, chunks, n - 1), sem(2, chunks, n - 1),
                *sum_sems, *sum_sems,
            ],
            compiler_params=pltpu.CompilerParams(
                collective_id=0, has_side_effects=True, vmem_limit_bytes=60 * 2**20
            ),
            cost_estimate=pl.CostEstimate(
                flops=12 * total * feats * half, bytes_accessed=8 * feats * half,
                transcendentals=0,
            ),
        )(tokens, cotangent, *weights)
    gate_grad = dot_tn(x_both, dgate)
    up_grad = dot_tn(x_both, dup)
    down_grad = dot_tn(act, cot_both)
    return (
        output,
        tokens_grad,
        gate_grad.astype(BF16),
        up_grad.astype(BF16),
        down_grad.astype(BF16),
    )


def solution(mesh):
    return jax.shard_map(
        functools.partial(per_device, mesh.shape["row"], mesh.shape["col"]),
        mesh=mesh,
        in_specs=(
            P(("col", "depth"), "row"),
            P("row", "col"),
            P("row", "col"),
            P("col", "row"),
            P(("col", "depth"), "row"),
        ),
        out_specs=(
            P(("col", "depth"), "row"),
            P(("col", "depth"), "row"),
            P("row", ("col", "depth")),
            P("row", ("col", "depth")),
            P(("col", "depth"), "row"),
        ),
        check_vma=False,
    )
```

```python
import functools

import jax
import jax.numpy as jnp
from jax import lax
from jax.experimental import pallas as pl
from jax.experimental.pallas import tpu as pltpu
from jax.sharding import PartitionSpec as P

MESH = pl.DeviceIdType.MESH
BF16 = jnp.bfloat16
F32 = jnp.float32


def dot_nn(left, right):
    return jnp.dot(left, right, preferred_element_type=F32)


def dot_nt(left, right):
    return lax.dot_general(
        left, right, (((1,), (1,)), ((), ())), preferred_element_type=F32
    )


def dot_tn(left, right):
    return lax.dot_general(
        left, right, (((0,), (0,)), ((), ())), preferred_element_type=F32
    )


def block(index, size):
    return pl.ds(pl.multiple_of(index * size, size), size)


def kernel(
    dims,
    x_ref, cot_ref, wg_hbm, wu_hbm, wd_hbm,
    out_ref, tg_ref, x_out, cot_out, act_out, dg_out, du_out,
    wg, wu, wd, x_full, cot_full,
    gu_part, gu_recv, d_part, d_recv, gu_own, act, dg, du,
    o_part, o_sib, o_sum, o_recv, t_part, t_sib, t_sum, t_recv,
    w_sem, copy_sem, x_ssem, x_rsem, c_ssem, c_rsem,
    gu_ssem, gu_rsem, d_ssem, d_rsem, act_ssem, act_rsem, h_ssem, h_rsem,
    osib_ssem, osib_rsem, oz_ssem, oz_rsem,
    tsib_ssem, tsib_rsem, tz_ssem, tz_rsem,
):
    n, nz, tl, tr, chunks, ch, parts, pw, sliced = dims
    r = lax.axis_index("row")
    z = lax.axis_index("col")
    d = lax.axis_index("depth")
    half = chunks * ch

    def peer(k):
        return {"row": lax.rem(r + k, n)}

    def zpeer(k):
        return {"col": lax.rem(z + k, nz)}

    sibling = {"depth": 1 - d}

    barrier = pltpu.get_barrier_semaphore()
    for k in range(1, n):
        pl.semaphore_signal(barrier, inc=1, device_id=peer(k), device_id_type=MESH)
    for k in range(1, nz):
        pl.semaphore_signal(barrier, inc=1, device_id=zpeer(k), device_id_type=MESH)
    pl.semaphore_signal(barrier, inc=1, device_id=sibling, device_id_type=MESH)

    if sliced:
        sources = (wg_hbm, wu_hbm, wd_hbm)
    else:
        mine = block(d, half)
        sources = (wg_hbm.at[:, mine], wu_hbm.at[:, mine], wd_hbm.at[mine, :])
    loads = [
        pltpu.make_async_copy(src, dst, w_sem.at[i])
        for i, (src, dst) in enumerate(zip(sources, (wg, wu, wd)))
    ]
    for load in loads:
        load.start()

    def remote(src, dst, ssem, rsem, where):
        return pltpu.make_async_remote_copy(
            src_ref=src, dst_ref=dst, send_sem=ssem, recv_sem=rsem,
            device_id=where, device_id_type=MESH,
        )

    def gather(full, ssem, rsem):
        def hop(zz, way):
            slot = zz * 2 + d
            ref = full.at[block(slot, tl)]
            where = ({"col": z + 1}, {"col": z - 1}, sibling)[way]
            return remote(ref, ref, ssem.at[zz, way], rsem.at[slot], where)

        def arrived(slot):
            ref = full.at[block(slot, tl)]
            remote(ref, ref, ssem.at[0, 0], rsem.at[slot], sibling).wait_recv()

        def first(shard):
            full[block(z * 2 + d, tl), :] = shard[...]

            @pl.when(z + 1 < nz)
            def _():
                hop(z, 0).start()

            @pl.when(z > 0)
            def _():
                hop(z, 1).start()

            hop(z, 2).start()

        def stage(s):
            low, high = z - s, z + s

            @pl.when(low >= 0)
            def _():
                arrived(low * 2 + d)

                @pl.when(z + 1 < nz)
                def _():
                    hop(low, 0).start()

                hop(low, 2).start()

            @pl.when(high < nz)
            def _():
                arrived(high * 2 + d)

                @pl.when(z > 0)
                def _():
                    hop(high, 1).start()

                hop(high, 2).start()

        def last():
            for zz in range(nz):
                arrived(zz * 2 + 1 - d)

        def drain():
            for zz in range(nz):
                @pl.when((zz <= z) & (z + 1 < nz))
                def _():
                    hop(zz, 0).wait_send()

                @pl.when((zz >= z) & (z > 0))
                def _():
                    hop(zz, 1).wait_send()

                hop(zz, 2).wait_send()

        return first, stage, last, drain

    x_first, x_stage, x_last, x_drain = gather(x_full, x_ssem, x_rsem)
    c_first, c_stage, c_last, c_drain = gather(cot_full, c_ssem, c_rsem)

    def gu_copy(c, k):
        rows = block(lax.rem(r + k, n), tr)
        return remote(gu_part.at[c, :, rows, :], gu_recv.at[c, k - 1],
                      gu_ssem.at[c, k - 1], gu_rsem.at[c, k - 1], peer(k))

    def d_copy(c, k):
        rows = block(lax.rem(r + k, n), tr)
        return remote(d_part.at[c, rows, :], d_recv.at[c, k - 1],
                      d_ssem.at[c, k - 1], d_rsem.at[c, k - 1], peer(k))

    mine_rows = block(r, tr)

    def act_copy(c, k, owner=None):
        rows = mine_rows if owner is None else block(owner, tr)
        ref = act.at[rows, block(c, ch)]
        return remote(ref, ref, act_ssem.at[c, k - 1], act_rsem.at[c, k - 1], peer(k))

    def h_copy(which, c, k, owner=None):
        rows = mine_rows if owner is None else block(owner, tr)
        ref = (dg, du)[which].at[rows, block(c, ch)]
        return remote(ref, ref, h_ssem.at[which, c, k - 1], h_rsem.at[which, c, k - 1], peer(k))

    def sender(k):
        return lax.rem(r - k + n, n)

    pl.semaphore_wait(barrier, n - 1 + nz - 1 + 1)

    x_first(x_ref)
    for s in range(1, nz):
        if s == nz - 1:
            c_first(cot_ref)
        x_stage(s)
    x_last()
    if nz == 1:
        c_first(cot_ref)
    x_save = pltpu.make_async_copy(x_full, x_out, copy_sem.at[0])
    x_save.start()

    loads[0].wait()
    loads[1].wait()

    @pl.loop(0, chunks)
    def _(c):
        gu_part[c, 0, :, :] = dot_nn(x_full[...], wg[:, block(c, ch)]).astype(BF16)
        gu_part[c, 1, :, :] = dot_nn(x_full[...], wu[:, block(c, ch)]).astype(BF16)
        for k in range(1, n):
            gu_copy(c, k).start()
        for s in range(1, nz):
            @pl.when(c == min(2 * s - 1, chunks - 1))
            def _():
                c_stage(s)

    c_last()
    cot_save = pltpu.make_async_copy(cot_full, cot_out, copy_sem.at[1])
    cot_save.start()
    loads[2].wait()

    @pl.loop(0, chunks)
    def _(c):
        d_part[c, :, :] = dot_nt(cot_full[...], wd[block(c, ch), :]).astype(BF16)
        for k in range(1, n):
            d_copy(c, k).start()

    @pl.loop(0, chunks)
    def _(c):
        gate = gu_part[c, 0, mine_rows, :].astype(F32)
        up = gu_part[c, 1, mine_rows, :].astype(F32)
        for k in range(1, n):
            gu_copy(c, k).wait_recv()
            gate += gu_recv[c, k - 1, 0].astype(F32)
            up += gu_recv[c, k - 1, 1].astype(F32)
        gu_own[c, 0] = gate
        gu_own[c, 1] = up
        act[mine_rows, block(c, ch)] = (gate * jax.nn.sigmoid(gate) * up).astype(BF16)
        for k in range(1, n):
            act_copy(c, k).start()

    @pl.loop(0, chunks)
    def _(c):
        dact = d_part[c, mine_rows, :].astype(F32)
        for k in range(1, n):
            d_copy(c, k).wait_recv()
            dact += d_recv[c, k - 1].astype(F32)
        gate, up = gu_own[c, 0], gu_own[c, 1]
        sig = jax.nn.sigmoid(gate)
        dg[mine_rows, block(c, ch)] = (
            dact * up * sig * (1.0 + gate * (1.0 - sig))
        ).astype(BF16)
        du[mine_rows, block(c, ch)] = (dact * gate * sig).astype(BF16)
        for k in range(1, n):
            h_copy(0, c, k).start()
            h_copy(1, c, k).start()

    def summing(part, sib, total, recv, sib_ssem, sib_rsem, z_ssem, z_rsem):
        def to_sibling(p):
            cols = block(p, pw)
            return remote(part.at[1 - d, :, :, cols], sib.at[:, :, cols],
                          sib_ssem.at[p], sib_rsem.at[p], sibling)

        def to_col(p, k):
            cols = block(p, pw)
            return remote(total.at[lax.rem(z + k, nz), :, cols], recv.at[k - 1, :, cols],
                          z_ssem.at[p, k - 1], z_rsem.at[p, k - 1], zpeer(k))

        def put(p, value):
            cols = block(p, pw)
            for zz in range(nz):
                for dd in range(2):
                    slot = zz * 2 + dd
                    part[dd, zz, :, cols] = value[slot * tl:(slot + 1) * tl].astype(BF16)
            to_sibling(p).start()

        def spread():
            @pl.loop(0, parts)
            def _(p):
                cols = block(p, pw)
                to_sibling(p).wait_recv()
                total[:, :, cols] = (
                    part[d, :, :, cols].astype(F32) + sib[:, :, cols].astype(F32)
                ).astype(BF16)
                for k in range(1, nz):
                    to_col(p, k).start()

        def finish(result):
            @pl.loop(0, parts)
            def _(p):
                cols = block(p, pw)
                value = total[z, :, cols].astype(F32)
                for k in range(1, nz):
                    to_col(p, k).wait_recv()
                    value += recv[k - 1, :, cols].astype(F32)
                result[:, cols] = value.astype(BF16)

        def drain():
            @pl.loop(0, parts)
            def _(p):
                to_sibling(p).wait_send()
                for k in range(1, nz):
                    to_col(p, k).wait_send()

        return put, spread, finish, drain

    o_put, o_spread, o_finish, o_drain = summing(
        o_part, o_sib, o_sum, o_recv, osib_ssem, osib_rsem, oz_ssem, oz_rsem)
    t_put, t_spread, t_finish, t_drain = summing(
        t_part, t_sib, t_sum, t_recv, tsib_ssem, tsib_rsem, tz_ssem, tz_rsem)

    @pl.loop(0, chunks)
    def _(c):
        for k in range(1, n):
            act_copy(c, k, sender(k)).wait_recv()

    act_save = pltpu.make_async_copy(act, act_out, copy_sem.at[2])
    act_save.start()

    @pl.loop(0, parts)
    def _(p):
        o_put(p, dot_nn(act[...], wd[:, block(p, pw)]))

    o_spread()

    @pl.loop(0, chunks)
    def _(c):
        for k in range(1, n):
            h_copy(0, c, k, sender(k)).wait_recv()
            h_copy(1, c, k, sender(k)).wait_recv()

    dg_save = pltpu.make_async_copy(dg, dg_out, copy_sem.at[3])
    du_save = pltpu.make_async_copy(du, du_out, copy_sem.at[4])
    dg_save.start()
    du_save.start()

    @pl.loop(0, parts)
    def _(p):
        t_put(p, dot_nt(dg[...], wg[block(p, pw), :]) + dot_nt(du[...], wu[block(p, pw), :]))

    t_spread()
    o_finish(out_ref)
    t_finish(tg_ref)

    x_drain()
    c_drain()

    @pl.loop(0, chunks)
    def _(c):
        for k in range(1, n):
            gu_copy(c, k).wait_send()
            d_copy(c, k).wait_send()
            act_copy(c, k).wait_send()
            h_copy(0, c, k).wait_send()
            h_copy(1, c, k).wait_send()

    o_drain()
    t_drain()
    for save in (x_save, cot_save, act_save, dg_save, du_save):
        save.wait()


VISITS = (0, 2, 3, 1)
LAST = tuple((z, (z + VISITS[3]) % 4) for z in range(4))


def group_kernel(
    dims,
    x_ref, cot_ref, wg_hbm, wu_hbm, wd_hbm,
    out_ref, tg_ref, last_ref, x_out, cot_out, act_out, dg_out, du_out,
    wg, wu, wd, x_full, cot_full, part, recv, h, acc, s_part, s_sib, s_sum, s_recv,
    w_sem, copy_sem, save_sem, x_ssem, x_rsem, c_ssem, c_rsem,
    rs_ssem, rs_rsem, ag_ssem, ag_rsem, sib_ssem, sib_rsem, z_ssem, z_rsem, last_sem,
):
    nz, tl, half, pw = dims
    feats = x_full.shape[1]
    tg, tr, hw = 2 * tl, tl // 2, half // 2
    units = 2 * nz
    wide = (hw // 2 + 127) // 128 * 128
    widths = (wide, hw - wide)
    starts = (0, wide)
    r = lax.axis_index("row")
    z = lax.axis_index("col")
    d = lax.axis_index("depth")
    rx = r + 1 - 2 * (r % 2)
    ry = r + 2 - 4 * (r // 2)
    rd = 3 - r
    sibling = {"depth": 1 - d}

    barrier = pltpu.get_barrier_semaphore()
    for where in (rx, ry):
        pl.semaphore_signal(barrier, inc=1, device_id={"row": where}, device_id_type=MESH)
    for k in range(1, nz):
        pl.semaphore_signal(barrier, inc=1, device_id={"col": lax.rem(z + k, nz)}, device_id_type=MESH)
    pl.semaphore_signal(barrier, inc=1, device_id=sibling, device_id_type=MESH)

    def load(i, s):
        here = block(s, hw)
        there = block(2 * d + s, hw)
        src, dst = (
            (wg_hbm.at[:, there], wg.at[:, here]),
            (wu_hbm.at[:, there], wu.at[:, here]),
            (wd_hbm.at[there, :], wd.at[here, :]),
        )[i]
        return pltpu.make_async_copy(src, dst, w_sem.at[i, s])

    for i in range(3):
        load(i, 0).start()

    def remote(src, dst, ssem, rsem, where):
        return pltpu.make_async_remote_copy(
            src_ref=src, dst_ref=dst, send_sem=ssem, recv_sem=rsem,
            device_id=where, device_id_type=MESH,
        )

    def index(u):
        return u // 2

    def side(u):
        return lax.rem(u, 2)

    def group(i):
        if isinstance(i, int):
            return lax.rem(z + VISITS[i], nz)
        away = jnp.where(i == 0, 0, jnp.where(i == 3, 1, i + 1))
        return lax.rem(z + away, nz)

    def ends(u):
        flip = lax.rem(u, 2)
        return rx + flip * (ry - rx), ry + flip * (rx - ry)

    def span_of(u, b):
        return pl.ds(pl.multiple_of(side(u) * hw + starts[b], 128), widths[b])

    def gather(full, ssem, rsem):
        def hop(zz, to):
            slot = zz * 2 + d
            ref = full.at[block(slot, tl)]
            where = ({"col": z + 1}, {"col": z - 1}, sibling)[to]
            return remote(ref, ref, ssem.at[zz, to], rsem.at[slot], where)

        def arrived(slot):
            ref = full.at[block(slot, tl)]
            remote(ref, ref, ssem.at[0, 0], rsem.at[slot], sibling).wait_recv()

        def first(shard):
            full[block(z * 2 + d, tl), :] = shard[...]
            hop(z, 2).start()

            @pl.when(z + 1 < nz)
            def _():
                hop(z, 0).start()

            @pl.when(z > 0)
            def _():
                hop(z, 1).start()

        def stage(s):
            low, high = z - s, z + s

            @pl.when(low >= 0)
            def _():
                arrived(low * 2 + d)

                @pl.when(z + 1 < nz)
                def _():
                    hop(low, 0).start()

                hop(low, 2).start()

            @pl.when(high < nz)
            def _():
                arrived(high * 2 + d)

                @pl.when(z > 0)
                def _():
                    hop(high, 1).start()

                hop(high, 2).start()

        def other(g):
            arrived(g * 2 + 1 - d)

        def drain():
            for zz in range(nz):
                @pl.when((zz <= z) & (z + 1 < nz))
                def _():
                    hop(zz, 0).wait_send()

                @pl.when((zz >= z) & (z > 0))
                def _():
                    hop(zz, 1).wait_send()

                hop(zz, 2).wait_send()

        return first, stage, other, drain

    x_first, x_stage, x_other, x_drain = gather(x_full, x_ssem, x_rsem)
    c_first, c_stage, c_other, c_drain = gather(cot_full, c_ssem, c_rsem)

    def rs(u, b, m):
        i = index(u)
        near, far = ends(u) if b == 0 else ends(u)[::-1]
        slot = m if m < 3 else m - 3
        owner = (rd, near, far)[slot]
        to = far if m == 2 else near
        cols = span_of(u, b)
        which = (pl.ds(0, 2), pl.ds(0, 2), pl.ds(0, 3), pl.ds(2, 1), pl.ds(2, 1))[m]
        return remote(part.at[i, which, block(owner, tr), cols],
                      recv.at[i, slot, which, :, cols],
                      rs_ssem.at[u, b, m], rs_rsem.at[u, b, m], {"row": to})

    def rows(g, owner):
        return pl.ds(pl.multiple_of(g * tg + owner * tr, tr), tr)

    def ag(u, m, incoming=False):
        g = group(index(u))
        p, q = ends(u)
        owner = (p, q, rd, rd)[m] if incoming else (r, r, p, q)[m]
        cols = block(side(u), hw) if m < 2 else span_of(u, m - 2)
        ref = h.at[:, rows(g, owner), cols]
        to = (p, q, q, p)[m]
        return remote(ref, ref, ag_ssem.at[u, m], ag_rsem.at[u, m], {"row": to})

    def to_sibling(i):
        g = group(i)
        return remote(s_part.at[g, :, 1 - d], s_sib.at[g], sib_ssem.at[i], sib_rsem.at[i], sibling)

    def to_col(i):
        g = group(i)
        k = lax.rem(z - g + nz, nz) - 1
        return remote(s_sum.at[g], s_recv.at[k], z_ssem.at[i], z_rsem.at[k], {"col": g})

    def saves(u):
        span, cols = block(group(index(u)), tg), block(side(u), hw)
        return [
            pltpu.make_async_copy(h.at[j, span, cols], out.at[span, cols], save_sem.at[u, j])
            for j, out in enumerate((act_out, dg_out, du_out))
        ]

    x_save = pltpu.make_async_copy(x_full, x_out, copy_sem.at[0])
    cot_save = pltpu.make_async_copy(cot_full, cot_out, copy_sem.at[1])

    def gate_up(u):
        i = index(u)
        g = group(i)
        span = block(g, tg)
        cols = block(side(u), hw)

        @pl.when((u == 2) | (u == 4))
        def _():
            x_stage(1 + u // 2)

        @pl.when(side(u) == 0)
        def _():
            x_other(g)

        @pl.when(u < 2)
        def _():
            load(0, u).wait()
            load(1, u).wait()

        part[i, 0, :, cols] = dot_nn(x_full[span, :], wg[:, cols]).astype(BF16)
        part[i, 1, :, cols] = dot_nn(x_full[span, :], wu[:, cols]).astype(BF16)
        for m in range(2):
            for b in range(2):
                rs(u, b, m).start()

    def hidden_grad(u):
        i = index(u)
        g = group(i)
        span = block(g, tg)
        cols = block(side(u), hw)

        @pl.when((u == 2) | (u == 4))
        def _():
            c_stage(1 + u // 2)

        @pl.when(side(u) == 0)
        def _():
            c_other(g)

        @pl.when(u < 2)
        def _():
            load(2, u).wait()

        @pl.when(u == 0)
        def _():
            for k in range(3):
                load(k, 1).start()

        part[i, 2, :, cols] = dot_nt(cot_full[span, :], wd[cols, :]).astype(BF16)
        for m in range(3, 5):
            for b in range(2):
                rs(u, b, m).start()

    def relay(u):
        i = index(u)
        for b in range(2):
            rs(u, b, 0).wait_recv()
            rs(u, b, 3).wait_recv()
            spot, cols = block(ends(u)[1 - b], tr), span_of(u, b)
            part[i, :, spot, cols] = (
                part[i, :, spot, cols].astype(F32) + recv[i, 0, :, :, cols].astype(F32)
            ).astype(BF16)
            rs(u, b, 2).start()

    def hidden(u):
        i = index(u)
        own = rows(group(i), r)
        for b in range(2):
            for m in (1, 4, 2):
                rs(u, b, m).wait_recv()
            cols = span_of(u, b)
            gate, up, dact = (
                part[i, j, block(r, tr), cols].astype(F32)
                + recv[i, 1, j, :, cols].astype(F32)
                + recv[i, 2, j, :, cols].astype(F32)
                for j in range(3)
            )
            sig = jax.nn.sigmoid(gate)
            h[0, own, cols] = (gate * sig * up).astype(BF16)
            h[1, own, cols] = (dact * up * sig * (1.0 + gate * (1.0 - sig))).astype(BF16)
            h[2, own, cols] = (dact * gate * sig).astype(BF16)
        ag(u, 0).start()
        ag(u, 1).start()

    def forward(u):
        for m in range(2):
            ag(u, m, True).wait_recv()
            ag(u, m + 2).start()

    def project(u):
        i = index(u)
        g = group(i)
        span, hid = block(g, tg), block(side(u), hw)
        ag(u, 2, True).wait_recv()
        ag(u, 3, True).wait_recv()
        for save in saves(u):
            save.start()

        def products(cols):
            out = dot_nn(h[0, span, hid], wd[hid, cols])
            grad = dot_nt(h[1, span, hid], wg[cols, hid]) + dot_nt(h[2, span, hid], wu[cols, hid])
            return out, grad

        @pl.when(side(u) == 0)
        def _():
            @pl.loop(0, feats // pw)
            def _(p):
                cols = block(p, pw)
                out, grad = products(cols)
                acc[0, :, cols] = out
                acc[1, :, cols] = grad

        @pl.when(side(u) == 1)
        def _():
            @pl.loop(0, feats // pw)
            def _(p):
                cols = block(p, pw)
                for j, value in enumerate(products(cols)):
                    value = (value + acc[j, :, cols]).astype(BF16)
                    for dd in range(2):
                        s_part[g, j, dd, :, cols] = value[dd * tl:(dd + 1) * tl]

            to_sibling(i).start()

    def spread(i):
        g = group(i)
        to_sibling(i).wait_recv()
        for j in range(2):
            s_sum[g, j] = (s_part[g, j, d].astype(F32) + s_sib[g, j].astype(F32)).astype(BF16)

        @pl.when((i > 0) & (i < nz - 1))
        def _():
            to_col(i).start()

    pl.semaphore_wait(barrier, 2 + nz - 1 + 1)
    x_first(x_ref)
    c_first(cot_ref)

    @pl.loop(0, units + 3)
    def _(t):
        @pl.when(t < units)
        def _():
            gate_up(t)

        @pl.when(t >= 3)
        def _():
            project(t - 3)

        @pl.when((t >= 2) & (t < units + 2))
        def _():
            forward(t - 2)

        @pl.when(t < units)
        def _():
            hidden_grad(t)

        @pl.when((t >= 1) & (t < units + 1))
        def _():
            hidden(t - 1)

        @pl.when((t >= 4) & (lax.rem(t, 2) == 0))
        def _():
            spread((t - 4) // 2)

        @pl.when(t == 1)
        def _():
            c_stage(1)

        @pl.when(t < units)
        def _():
            relay(t)

        @pl.when(t == 0)
        def _():
            x_stage(1)

        @pl.when(t == units - 2)
        def _():
            x_save.start()
            cot_save.start()

    to_last = pltpu.make_async_copy(s_sum.at[group(nz - 1)], last_ref, last_sem)
    to_last.start()

    def landed(k):
        remote(s_sum.at[0], s_recv.at[k], z_ssem.at[0], z_rsem.at[k], sibling).wait_recv()

    for k in range(nz - 2):
        landed(k)

    for j, result in enumerate((out_ref, tg_ref)):
        value = s_sum[z, j].astype(F32)
        for k in range(nz - 2):
            value += s_recv[k, j].astype(F32)
        result[...] = value

    x_drain()
    c_drain()

    @pl.loop(0, units)
    def _(u):
        for b in range(2):
            for m in range(5):
                rs(u, b, m).wait_send()
        for m in range(4):
            ag(u, m).wait_send()
        for save in saves(u):
            save.wait()

    @pl.loop(0, nz)
    def _(i):
        to_sibling(i).wait_send()

        @pl.when((i > 0) & (i < nz - 1))
        def _():
            to_col(i).wait_send()

    x_save.wait()
    cot_save.wait()
    to_last.wait()


def weight_kernel(
    x_hbm, dg_hbm, du_hbm, act_hbm, cot_hbm, gate_hbm, up_hbm, down_hbm,
    x, dg, du, act, cot, gate_tile, up_tile, down_tile, in_sem, out_sem,
):
    loads = [
        pltpu.make_async_copy(src, dst, in_sem.at[k])
        for k, (src, dst) in enumerate(
            ((x_hbm, x), (dg_hbm, dg), (du_hbm, du), (act_hbm, act), (cot_hbm, cot)))
    ]
    for load in loads:
        load.start()

    def product(k, left, right, tile, result):
        size, width = tile.shape[1], right.shape[1] // 2
        tiles = left.shape[1] // size

        def save(i):
            slot = lax.rem(i, 2)
            return pltpu.make_async_copy(tile.at[slot], result.at[block(i, size)], out_sem.at[k, slot])

        @pl.loop(0, tiles)
        def _(i):
            @pl.when(i > 1)
            def _():
                save(i - 2).wait()

            rows, slot = left[:, block(i, size)], lax.rem(i, 2)
            for cols in (pl.ds(0, width), pl.ds(width, width)):
                tile[slot, :, cols] = dot_tn(rows, right[:, cols]).astype(BF16)
            save(i).start()

        return [save(i) for i in range(max(tiles - 2, 0), tiles)]

    loads[0].wait()
    loads[1].wait()
    left_over = product(0, x, dg, gate_tile, gate_hbm)
    loads[2].wait()
    left_over += product(1, x, du, up_tile, up_hbm)
    loads[3].wait()
    loads[4].wait()
    left_over += product(2, act, cot, down_tile, down_hbm)
    for save in left_over:
        save.wait()


def weight_grads(x, dgate, dup, act, cot):
    total, feats = x.shape
    half = act.shape[1]
    tall, short = feats // 2, half // 2
    hbm = pl.BlockSpec(memory_space=pl.ANY)

    def buf(*shape):
        return pltpu.VMEM(shape, BF16)

    return pl.pallas_call(
        weight_kernel,
        in_specs=[hbm] * 5,
        out_specs=(hbm, hbm, hbm),
        out_shape=(
            jax.ShapeDtypeStruct((feats, half), BF16),
            jax.ShapeDtypeStruct((feats, half), BF16),
            jax.ShapeDtypeStruct((half, feats), BF16),
        ),
        scratch_shapes=[
            buf(total, feats), buf(total, half), buf(total, half), buf(total, half), buf(total, feats),
            buf(2, tall, half), buf(2, tall, half), buf(2, short, feats),
            pltpu.SemaphoreType.DMA((5,)), pltpu.SemaphoreType.DMA((3, 2)),
        ],
        compiler_params=pltpu.CompilerParams(vmem_limit_bytes=60 * 2**20),
        cost_estimate=pl.CostEstimate(
            flops=6 * total * feats * half,
            bytes_accessed=6 * feats * half + 4 * total * feats + 6 * total * half,
            transcendentals=0,
        ),
    )(x, dgate, dup, act, cot)


def per_device(n, nz, tokens, gate_weight, up_weight, down_weight, cotangent):
    tl, feats = tokens.shape
    half = gate_weight.shape[1] // 2
    total = tl * nz * 2
    tr = total // n
    ch = 256 if half % 256 == 0 else half
    chunks = half // ch
    pw = 512 if feats % 512 == 0 else feats
    parts = feats // pw
    sliced = half % 128 != 0
    if sliced:
        start = lax.axis_index("depth") * half
        weights = (
            lax.dynamic_slice_in_dim(gate_weight, start, half, 1),
            lax.dynamic_slice_in_dim(up_weight, start, half, 1),
            lax.dynamic_slice_in_dim(down_weight, start, half, 0),
        )
    else:
        weights = (gate_weight, up_weight, down_weight)

    def sds(*shape):
        return jax.ShapeDtypeStruct(shape, BF16)

    def buf(*shape):
        return pltpu.VMEM(shape, BF16)

    def sem(*shape):
        return pltpu.SemaphoreType.DMA(shape)

    vmem = pl.BlockSpec(memory_space=pltpu.VMEM)
    hbm = pl.BlockSpec(memory_space=pl.ANY)
    if n == 4 and nz == 4 and tl % 32 == 0 and half % 256 == 0 and half >= 512:
        out_part, tg_part, last, x_both, cot_both, act, dgate, dup = pl.pallas_call(
            functools.partial(group_kernel, (nz, tl, half, 2 * pw if parts % 2 == 0 else pw)),
            out_shape=(
                jax.ShapeDtypeStruct((tl, feats), F32), jax.ShapeDtypeStruct((tl, feats), F32),
                sds(2, tl, feats),
                sds(total, feats), sds(total, feats),
                sds(total, half), sds(total, half), sds(total, half),
            ),
            in_specs=[vmem, vmem, hbm, hbm, hbm],
            out_specs=(vmem, vmem, hbm, hbm, hbm, hbm, hbm, hbm),
            scratch_shapes=[
                buf(feats, half), buf(feats, half), buf(half, feats),
                buf(total, feats), buf(total, feats),
                buf(nz, 3, 2 * tl, half), buf(nz, 3, 3, tl // 2, half),
                buf(3, total, half), pltpu.VMEM((2, 2 * tl, feats), F32),
                buf(nz, 2, 2, tl, feats), buf(nz, 2, tl, feats), buf(nz, 2, tl, feats),
                buf(nz - 2, 2, tl, feats),
                sem(3, 2), sem(2), sem(2 * nz, 3),
                sem(nz, 3), sem(nz * 2), sem(nz, 3), sem(nz * 2),
                sem(2 * nz, 2, 5), sem(2 * nz, 2, 5), sem(2 * nz, 4), sem(2 * nz, 4),
                sem(nz), sem(nz), sem(nz), sem(nz), pltpu.SemaphoreType.DMA,
            ],
            compiler_params=pltpu.CompilerParams(
                collective_id=1, has_side_effects=True, vmem_limit_bytes=60 * 2**20
            ),
            cost_estimate=pl.CostEstimate(
                flops=12 * total * feats * half, bytes_accessed=8 * feats * half,
                transcendentals=0,
            ),
        )(tokens, cotangent, *weights)
        sent = lax.ppermute(last, "col", LAST)
        output = (out_part + sent[0].astype(F32)).astype(BF16)
        tokens_grad = (tg_part + sent[1].astype(F32)).astype(BF16)
        if feats % 256 == 0:
            return (output, tokens_grad, *weight_grads(x_both, dgate, dup, act, cot_both))
    else:
        sums = [
            buf(2, nz, tl, feats), buf(nz, tl, feats), buf(nz, tl, feats),
            buf(max(nz - 1, 1), tl, feats),
        ]
        sum_sems = [sem(parts), sem(parts), sem(parts, nz), sem(parts, nz)]
        output, tokens_grad, x_both, cot_both, act, dgate, dup = pl.pallas_call(
            functools.partial(kernel, (n, nz, tl, tr, chunks, ch, parts, pw, sliced)),
            out_shape=(
                sds(tl, feats), sds(tl, feats), sds(total, feats), sds(total, feats),
                sds(total, half), sds(total, half), sds(total, half),
            ),
            in_specs=[vmem, vmem, hbm, hbm, hbm],
            out_specs=(vmem, vmem, hbm, hbm, hbm, hbm, hbm),
            scratch_shapes=[
                buf(feats, half), buf(feats, half), buf(half, feats),
                buf(total, feats), buf(total, feats),
                buf(chunks, 2, total, ch), buf(chunks, n - 1, 2, tr, ch),
                buf(chunks, total, ch), buf(chunks, n - 1, tr, ch),
                pltpu.VMEM((chunks, 2, tr, ch), F32),
                buf(total, half), buf(total, half), buf(total, half),
                *sums, *sums,
                sem(3), sem(5),
                sem(nz, 3), sem(nz * 2), sem(nz, 3), sem(nz * 2),
                sem(chunks, n - 1), sem(chunks, n - 1),
                sem(chunks, n - 1), sem(chunks, n - 1),
                sem(chunks, n - 1), sem(chunks, n - 1),
                sem(2, chunks, n - 1), sem(2, chunks, n - 1),
                *sum_sems, *sum_sems,
            ],
            compiler_params=pltpu.CompilerParams(
                collective_id=0, has_side_effects=True, vmem_limit_bytes=60 * 2**20
            ),
            cost_estimate=pl.CostEstimate(
                flops=12 * total * feats * half, bytes_accessed=8 * feats * half,
                transcendentals=0,
            ),
        )(tokens, cotangent, *weights)
    gate_grad = dot_tn(x_both, dgate)
    up_grad = dot_tn(x_both, dup)
    down_grad = dot_tn(act, cot_both)
    return (
        output,
        tokens_grad,
        gate_grad.astype(BF16),
        up_grad.astype(BF16),
        down_grad.astype(BF16),
    )


def solution(mesh):
    return jax.shard_map(
        functools.partial(per_device, mesh.shape["row"], mesh.shape["col"]),
        mesh=mesh,
        in_specs=(
            P(("col", "depth"), "row"),
            P("row", "col"),
            P("row", "col"),
            P("col", "row"),
            P(("col", "depth"), "row"),
        ),
        out_specs=(
            P(("col", "depth"), "row"),
            P(("col", "depth"), "row"),
            P("row", ("col", "depth")),
            P("row", ("col", "depth")),
            P(("col", "depth"), "row"),
        ),
        check_vma=False,
    )
```

```python
import functools

import jax
import jax.numpy as jnp
from jax import lax
from jax.experimental import pallas as pl
from jax.experimental.pallas import tpu as pltpu
from jax.sharding import PartitionSpec as P

MESH = pl.DeviceIdType.MESH
BF16 = jnp.bfloat16
F32 = jnp.float32


def dot_nn(left, right):
    return jnp.dot(left, right, preferred_element_type=F32)


def dot_nt(left, right):
    return lax.dot_general(
        left, right, (((1,), (1,)), ((), ())), preferred_element_type=F32
    )


def dot_tn(left, right):
    return lax.dot_general(
        left, right, (((0,), (0,)), ((), ())), preferred_element_type=F32
    )


def block(index, size):
    return pl.ds(pl.multiple_of(index * size, size), size)


def kernel(
    dims,
    x_ref, cot_ref, wg_hbm, wu_hbm, wd_hbm,
    out_ref, tg_ref, x_out, cot_out, act_out, dg_out, du_out,
    wg, wu, wd, x_full, cot_full,
    gu_part, gu_recv, d_part, d_recv, gu_own, act, dg, du,
    o_part, o_sib, o_sum, o_recv, t_part, t_sib, t_sum, t_recv,
    w_sem, copy_sem, x_ssem, x_rsem, c_ssem, c_rsem,
    gu_ssem, gu_rsem, d_ssem, d_rsem, act_ssem, act_rsem, h_ssem, h_rsem,
    osib_ssem, osib_rsem, oz_ssem, oz_rsem,
    tsib_ssem, tsib_rsem, tz_ssem, tz_rsem,
):
    n, nz, tl, tr, chunks, ch, parts, pw, sliced = dims
    r = lax.axis_index("row")
    z = lax.axis_index("col")
    d = lax.axis_index("depth")
    half = chunks * ch

    def peer(k):
        return {"row": lax.rem(r + k, n)}

    def zpeer(k):
        return {"col": lax.rem(z + k, nz)}

    sibling = {"depth": 1 - d}

    barrier = pltpu.get_barrier_semaphore()
    for k in range(1, n):
        pl.semaphore_signal(barrier, inc=1, device_id=peer(k), device_id_type=MESH)
    for k in range(1, nz):
        pl.semaphore_signal(barrier, inc=1, device_id=zpeer(k), device_id_type=MESH)
    pl.semaphore_signal(barrier, inc=1, device_id=sibling, device_id_type=MESH)

    if sliced:
        sources = (wg_hbm, wu_hbm, wd_hbm)
    else:
        mine = block(d, half)
        sources = (wg_hbm.at[:, mine], wu_hbm.at[:, mine], wd_hbm.at[mine, :])
    loads = [
        pltpu.make_async_copy(src, dst, w_sem.at[i])
        for i, (src, dst) in enumerate(zip(sources, (wg, wu, wd)))
    ]
    for load in loads:
        load.start()

    def remote(src, dst, ssem, rsem, where):
        return pltpu.make_async_remote_copy(
            src_ref=src, dst_ref=dst, send_sem=ssem, recv_sem=rsem,
            device_id=where, device_id_type=MESH,
        )

    def gather(full, ssem, rsem):
        def hop(zz, way):
            slot = zz * 2 + d
            ref = full.at[block(slot, tl)]
            where = ({"col": z + 1}, {"col": z - 1}, sibling)[way]
            return remote(ref, ref, ssem.at[zz, way], rsem.at[slot], where)

        def arrived(slot):
            ref = full.at[block(slot, tl)]
            remote(ref, ref, ssem.at[0, 0], rsem.at[slot], sibling).wait_recv()

        def first(shard):
            full[block(z * 2 + d, tl), :] = shard[...]

            @pl.when(z + 1 < nz)
            def _():
                hop(z, 0).start()

            @pl.when(z > 0)
            def _():
                hop(z, 1).start()

            hop(z, 2).start()

        def stage(s):
            low, high = z - s, z + s

            @pl.when(low >= 0)
            def _():
                arrived(low * 2 + d)

                @pl.when(z + 1 < nz)
                def _():
                    hop(low, 0).start()

                hop(low, 2).start()

            @pl.when(high < nz)
            def _():
                arrived(high * 2 + d)

                @pl.when(z > 0)
                def _():
                    hop(high, 1).start()

                hop(high, 2).start()

        def last():
            for zz in range(nz):
                arrived(zz * 2 + 1 - d)

        def drain():
            for zz in range(nz):
                @pl.when((zz <= z) & (z + 1 < nz))
                def _():
                    hop(zz, 0).wait_send()

                @pl.when((zz >= z) & (z > 0))
                def _():
                    hop(zz, 1).wait_send()

                hop(zz, 2).wait_send()

        return first, stage, last, drain

    x_first, x_stage, x_last, x_drain = gather(x_full, x_ssem, x_rsem)
    c_first, c_stage, c_last, c_drain = gather(cot_full, c_ssem, c_rsem)

    def gu_copy(c, k):
        rows = block(lax.rem(r + k, n), tr)
        return remote(gu_part.at[c, :, rows, :], gu_recv.at[c, k - 1],
                      gu_ssem.at[c, k - 1], gu_rsem.at[c, k - 1], peer(k))

    def d_copy(c, k):
        rows = block(lax.rem(r + k, n), tr)
        return remote(d_part.at[c, rows, :], d_recv.at[c, k - 1],
                      d_ssem.at[c, k - 1], d_rsem.at[c, k - 1], peer(k))

    mine_rows = block(r, tr)

    def act_copy(c, k, owner=None):
        rows = mine_rows if owner is None else block(owner, tr)
        ref = act.at[rows, block(c, ch)]
        return remote(ref, ref, act_ssem.at[c, k - 1], act_rsem.at[c, k - 1], peer(k))

    def h_copy(which, c, k, owner=None):
        rows = mine_rows if owner is None else block(owner, tr)
        ref = (dg, du)[which].at[rows, block(c, ch)]
        return remote(ref, ref, h_ssem.at[which, c, k - 1], h_rsem.at[which, c, k - 1], peer(k))

    def sender(k):
        return lax.rem(r - k + n, n)

    pl.semaphore_wait(barrier, n - 1 + nz - 1 + 1)

    x_first(x_ref)
    for s in range(1, nz):
        if s == nz - 1:
            c_first(cot_ref)
        x_stage(s)
    x_last()
    if nz == 1:
        c_first(cot_ref)
    x_save = pltpu.make_async_copy(x_full, x_out, copy_sem.at[0])
    x_save.start()

    loads[0].wait()
    loads[1].wait()

    @pl.loop(0, chunks)
    def _(c):
        gu_part[c, 0, :, :] = dot_nn(x_full[...], wg[:, block(c, ch)]).astype(BF16)
        gu_part[c, 1, :, :] = dot_nn(x_full[...], wu[:, block(c, ch)]).astype(BF16)
        for k in range(1, n):
            gu_copy(c, k).start()
        for s in range(1, nz):
            @pl.when(c == min(2 * s - 1, chunks - 1))
            def _():
                c_stage(s)

    c_last()
    cot_save = pltpu.make_async_copy(cot_full, cot_out, copy_sem.at[1])
    cot_save.start()
    loads[2].wait()

    @pl.loop(0, chunks)
    def _(c):
        d_part[c, :, :] = dot_nt(cot_full[...], wd[block(c, ch), :]).astype(BF16)
        for k in range(1, n):
            d_copy(c, k).start()

    @pl.loop(0, chunks)
    def _(c):
        gate = gu_part[c, 0, mine_rows, :].astype(F32)
        up = gu_part[c, 1, mine_rows, :].astype(F32)
        for k in range(1, n):
            gu_copy(c, k).wait_recv()
            gate += gu_recv[c, k - 1, 0].astype(F32)
            up += gu_recv[c, k - 1, 1].astype(F32)
        gu_own[c, 0] = gate
        gu_own[c, 1] = up
        act[mine_rows, block(c, ch)] = (gate * jax.nn.sigmoid(gate) * up).astype(BF16)
        for k in range(1, n):
            act_copy(c, k).start()

    @pl.loop(0, chunks)
    def _(c):
        dact = d_part[c, mine_rows, :].astype(F32)
        for k in range(1, n):
            d_copy(c, k).wait_recv()
            dact += d_recv[c, k - 1].astype(F32)
        gate, up = gu_own[c, 0], gu_own[c, 1]
        sig = jax.nn.sigmoid(gate)
        dg[mine_rows, block(c, ch)] = (
            dact * up * sig * (1.0 + gate * (1.0 - sig))
        ).astype(BF16)
        du[mine_rows, block(c, ch)] = (dact * gate * sig).astype(BF16)
        for k in range(1, n):
            h_copy(0, c, k).start()
            h_copy(1, c, k).start()

    def summing(part, sib, total, recv, sib_ssem, sib_rsem, z_ssem, z_rsem):
        def to_sibling(p):
            cols = block(p, pw)
            return remote(part.at[1 - d, :, :, cols], sib.at[:, :, cols],
                          sib_ssem.at[p], sib_rsem.at[p], sibling)

        def to_col(p, k):
            cols = block(p, pw)
            return remote(total.at[lax.rem(z + k, nz), :, cols], recv.at[k - 1, :, cols],
                          z_ssem.at[p, k - 1], z_rsem.at[p, k - 1], zpeer(k))

        def put(p, value):
            cols = block(p, pw)
            for zz in range(nz):
                for dd in range(2):
                    slot = zz * 2 + dd
                    part[dd, zz, :, cols] = value[slot * tl:(slot + 1) * tl].astype(BF16)
            to_sibling(p).start()

        def spread():
            @pl.loop(0, parts)
            def _(p):
                cols = block(p, pw)
                to_sibling(p).wait_recv()
                total[:, :, cols] = (
                    part[d, :, :, cols].astype(F32) + sib[:, :, cols].astype(F32)
                ).astype(BF16)
                for k in range(1, nz):
                    to_col(p, k).start()

        def finish(result):
            @pl.loop(0, parts)
            def _(p):
                cols = block(p, pw)
                value = total[z, :, cols].astype(F32)
                for k in range(1, nz):
                    to_col(p, k).wait_recv()
                    value += recv[k - 1, :, cols].astype(F32)
                result[:, cols] = value.astype(BF16)

        def drain():
            @pl.loop(0, parts)
            def _(p):
                to_sibling(p).wait_send()
                for k in range(1, nz):
                    to_col(p, k).wait_send()

        return put, spread, finish, drain

    o_put, o_spread, o_finish, o_drain = summing(
        o_part, o_sib, o_sum, o_recv, osib_ssem, osib_rsem, oz_ssem, oz_rsem)
    t_put, t_spread, t_finish, t_drain = summing(
        t_part, t_sib, t_sum, t_recv, tsib_ssem, tsib_rsem, tz_ssem, tz_rsem)

    @pl.loop(0, chunks)
    def _(c):
        for k in range(1, n):
            act_copy(c, k, sender(k)).wait_recv()

    act_save = pltpu.make_async_copy(act, act_out, copy_sem.at[2])
    act_save.start()

    @pl.loop(0, parts)
    def _(p):
        o_put(p, dot_nn(act[...], wd[:, block(p, pw)]))

    o_spread()

    @pl.loop(0, chunks)
    def _(c):
        for k in range(1, n):
            h_copy(0, c, k, sender(k)).wait_recv()
            h_copy(1, c, k, sender(k)).wait_recv()

    dg_save = pltpu.make_async_copy(dg, dg_out, copy_sem.at[3])
    du_save = pltpu.make_async_copy(du, du_out, copy_sem.at[4])
    dg_save.start()
    du_save.start()

    @pl.loop(0, parts)
    def _(p):
        t_put(p, dot_nt(dg[...], wg[block(p, pw), :]) + dot_nt(du[...], wu[block(p, pw), :]))

    t_spread()
    o_finish(out_ref)
    t_finish(tg_ref)

    x_drain()
    c_drain()

    @pl.loop(0, chunks)
    def _(c):
        for k in range(1, n):
            gu_copy(c, k).wait_send()
            d_copy(c, k).wait_send()
            act_copy(c, k).wait_send()
            h_copy(0, c, k).wait_send()
            h_copy(1, c, k).wait_send()

    o_drain()
    t_drain()
    for save in (x_save, cot_save, act_save, dg_save, du_save):
        save.wait()


VISITS = (0, 2, 3, 1)
LAST = tuple((z, (z + VISITS[3]) % 4) for z in range(4))


def group_kernel(
    dims,
    x_ref, cot_ref, wg_hbm, wu_hbm, wd_hbm,
    out_hbm, tg_hbm, last_ref, x_out, cot_out, act_out, dg_out, du_out,
    wg, wu, wd, x_full, cot_full, part, recv, h, acc, s_part, s_sib, s_sum, s_recv, base,
    w_sem, copy_sem, save_sem, x_ssem, x_rsem, c_ssem, c_rsem,
    rs_ssem, rs_rsem, ag_ssem, ag_rsem, sib_ssem, sib_rsem, z_ssem, z_rsem, last_sem, base_sem,
):
    nz, tl, half, pw = dims
    feats = x_full.shape[1]
    tg, tr, hw = 2 * tl, tl // 2, half // 2
    units = 2 * nz
    wide = (hw // 2 + 127) // 128 * 128
    widths = (wide, hw - wide)
    starts = (0, wide)
    r = lax.axis_index("row")
    z = lax.axis_index("col")
    d = lax.axis_index("depth")
    rx = r + 1 - 2 * (r % 2)
    ry = r + 2 - 4 * (r // 2)
    rd = 3 - r
    sibling = {"depth": 1 - d}

    barrier = pltpu.get_barrier_semaphore()
    for where in (rx, ry):
        pl.semaphore_signal(barrier, inc=1, device_id={"row": where}, device_id_type=MESH)
    for k in range(1, nz):
        pl.semaphore_signal(barrier, inc=1, device_id={"col": lax.rem(z + k, nz)}, device_id_type=MESH)
    pl.semaphore_signal(barrier, inc=1, device_id=sibling, device_id_type=MESH)

    def load(i, s):
        here = block(s, hw)
        there = block(2 * d + s, hw)
        src, dst = (
            (wg_hbm.at[:, there], wg.at[:, here]),
            (wu_hbm.at[:, there], wu.at[:, here]),
            (wd_hbm.at[there, :], wd.at[here, :]),
        )[i]
        return pltpu.make_async_copy(src, dst, w_sem.at[i, s])

    for i in range(3):
        load(i, 0).start()

    def remote(src, dst, ssem, rsem, where):
        return pltpu.make_async_remote_copy(
            src_ref=src, dst_ref=dst, send_sem=ssem, recv_sem=rsem,
            device_id=where, device_id_type=MESH,
        )

    def index(u):
        return u // 2

    def side(u):
        return lax.rem(u, 2)

    def group(i):
        if isinstance(i, int):
            return lax.rem(z + VISITS[i], nz)
        away = jnp.where(i == 0, 0, jnp.where(i == 3, 1, i + 1))
        return lax.rem(z + away, nz)

    def ends(u):
        flip = lax.rem(u, 2)
        return rx + flip * (ry - rx), ry + flip * (rx - ry)

    def span_of(u, b):
        return pl.ds(pl.multiple_of(side(u) * hw + starts[b], 128), widths[b])

    def gather(full, ssem, rsem):
        def hop(zz, to):
            slot = zz * 2 + d
            ref = full.at[block(slot, tl)]
            where = ({"col": z + 1}, {"col": z - 1}, sibling)[to]
            return remote(ref, ref, ssem.at[zz, to], rsem.at[slot], where)

        def arrived(slot):
            ref = full.at[block(slot, tl)]
            remote(ref, ref, ssem.at[0, 0], rsem.at[slot], sibling).wait_recv()

        def first(shard):
            full[block(z * 2 + d, tl), :] = shard[...]
            hop(z, 2).start()

            @pl.when(z + 1 < nz)
            def _():
                hop(z, 0).start()

            @pl.when(z > 0)
            def _():
                hop(z, 1).start()

        def stage(s):
            low, high = z - s, z + s

            @pl.when(low >= 0)
            def _():
                arrived(low * 2 + d)

                @pl.when(z + 1 < nz)
                def _():
                    hop(low, 0).start()

                hop(low, 2).start()

            @pl.when(high < nz)
            def _():
                arrived(high * 2 + d)

                @pl.when(z > 0)
                def _():
                    hop(high, 1).start()

                hop(high, 2).start()

        def other(g):
            arrived(g * 2 + 1 - d)

        def drain():
            for zz in range(nz):
                @pl.when((zz <= z) & (z + 1 < nz))
                def _():
                    hop(zz, 0).wait_send()

                @pl.when((zz >= z) & (z > 0))
                def _():
                    hop(zz, 1).wait_send()

                hop(zz, 2).wait_send()

        return first, stage, other, drain

    x_first, x_stage, x_other, x_drain = gather(x_full, x_ssem, x_rsem)
    c_first, c_stage, c_other, c_drain = gather(cot_full, c_ssem, c_rsem)

    def rs(u, b, m):
        i = index(u)
        near, far = ends(u) if b == 0 else ends(u)[::-1]
        slot = m if m < 3 else m - 3
        owner = (rd, near, far)[slot]
        to = far if m == 2 else near
        cols = span_of(u, b)
        which = (pl.ds(0, 2), pl.ds(0, 2), pl.ds(0, 3), pl.ds(2, 1), pl.ds(2, 1))[m]
        return remote(part.at[i, which, block(owner, tr), cols],
                      recv.at[i, slot, which, :, cols],
                      rs_ssem.at[u, b, m], rs_rsem.at[u, b, m], {"row": to})

    def rows(g, owner):
        return pl.ds(pl.multiple_of(g * tg + owner * tr, tr), tr)

    def ag(u, m, incoming=False):
        g = group(index(u))
        p, q = ends(u)
        owner = (p, q, rd, rd)[m] if incoming else (r, r, p, q)[m]
        cols = block(side(u), hw) if m < 2 else span_of(u, m - 2)
        ref = h.at[:, rows(g, owner), cols]
        to = (p, q, q, p)[m]
        return remote(ref, ref, ag_ssem.at[u, m], ag_rsem.at[u, m], {"row": to})

    def to_sibling(i):
        g = group(i)
        return remote(s_part.at[g, :, 1 - d], s_sib.at[g], sib_ssem.at[i], sib_rsem.at[i], sibling)

    def to_col(i):
        g = group(i)
        k = lax.rem(z - g + nz, nz) - 1
        return remote(s_sum.at[g], s_recv.at[k], z_ssem.at[i], z_rsem.at[k], {"col": g})

    def saves(u):
        span, cols = block(group(index(u)), tg), block(side(u), hw)
        return [
            pltpu.make_async_copy(h.at[j, span, cols], out.at[span, cols], save_sem.at[u, j])
            for j, out in enumerate((act_out, dg_out, du_out))
        ]

    x_save = pltpu.make_async_copy(x_full, x_out, copy_sem.at[0])
    cot_save = pltpu.make_async_copy(cot_full, cot_out, copy_sem.at[1])

    def gate_up(u):
        i = index(u)
        g = group(i)
        span = block(g, tg)
        cols = block(side(u), hw)

        @pl.when((u == 2) | (u == 4))
        def _():
            x_stage(1 + u // 2)

        @pl.when(side(u) == 0)
        def _():
            x_other(g)

        @pl.when(u < 2)
        def _():
            load(0, u).wait()
            load(1, u).wait()

        part[i, 0, :, cols] = dot_nn(x_full[span, :], wg[:, cols]).astype(BF16)
        part[i, 1, :, cols] = dot_nn(x_full[span, :], wu[:, cols]).astype(BF16)
        for m in range(2):
            for b in range(2):
                rs(u, b, m).start()

    def hidden_grad(u):
        i = index(u)
        g = group(i)
        span = block(g, tg)
        cols = block(side(u), hw)

        @pl.when((u == 2) | (u == 4))
        def _():
            c_stage(1 + u // 2)

        @pl.when(side(u) == 0)
        def _():
            c_other(g)

        @pl.when(u < 2)
        def _():
            load(2, u).wait()

        @pl.when(u == 0)
        def _():
            for k in range(3):
                load(k, 1).start()

        part[i, 2, :, cols] = dot_nt(cot_full[span, :], wd[cols, :]).astype(BF16)
        for m in range(3, 5):
            for b in range(2):
                rs(u, b, m).start()

    def relay(u):
        i = index(u)
        for b in range(2):
            rs(u, b, 0).wait_recv()
            rs(u, b, 3).wait_recv()
            spot, cols = block(ends(u)[1 - b], tr), span_of(u, b)
            part[i, :, spot, cols] = (
                part[i, :, spot, cols].astype(F32) + recv[i, 0, :, :, cols].astype(F32)
            ).astype(BF16)
            rs(u, b, 2).start()

    def hidden(u):
        i = index(u)
        own = rows(group(i), r)
        for b in range(2):
            for m in (1, 4, 2):
                rs(u, b, m).wait_recv()
            cols = span_of(u, b)
            gate, up, dact = (
                part[i, j, block(r, tr), cols].astype(F32)
                + recv[i, 1, j, :, cols].astype(F32)
                + recv[i, 2, j, :, cols].astype(F32)
                for j in range(3)
            )
            sig = jax.nn.sigmoid(gate)
            h[0, own, cols] = (gate * sig * up).astype(BF16)
            h[1, own, cols] = (dact * up * sig * (1.0 + gate * (1.0 - sig))).astype(BF16)
            h[2, own, cols] = (dact * gate * sig).astype(BF16)
        ag(u, 0).start()
        ag(u, 1).start()

    def forward(u):
        for m in range(2):
            ag(u, m, True).wait_recv()
            ag(u, m + 2).start()

    def project(u):
        i = index(u)
        g = group(i)
        span, hid = block(g, tg), block(side(u), hw)
        ag(u, 2, True).wait_recv()
        ag(u, 3, True).wait_recv()
        for save in saves(u):
            save.start()

        def products(cols):
            out = dot_nn(h[0, span, hid], wd[hid, cols])
            grad = dot_nt(h[1, span, hid], wg[cols, hid]) + dot_nt(h[2, span, hid], wu[cols, hid])
            return out, grad

        @pl.when(side(u) == 0)
        def _():
            @pl.loop(0, feats // pw)
            def _(p):
                cols = block(p, pw)
                out, grad = products(cols)
                acc[0, :, cols] = out
                acc[1, :, cols] = grad

        @pl.when(side(u) == 1)
        def _():
            @pl.loop(0, feats // pw)
            def _(p):
                cols = block(p, pw)
                for j, value in enumerate(products(cols)):
                    value = (value + acc[j, :, cols]).astype(BF16)
                    for dd in range(2):
                        s_part[g, j, dd, :, cols] = value[dd * tl:(dd + 1) * tl]

            to_sibling(i).start()

    def spread(i):
        g = group(i)
        to_sibling(i).wait_recv()
        for j in range(2):
            s_sum[g, j] = (s_part[g, j, d].astype(F32) + s_sib[g, j].astype(F32)).astype(BF16)


        @pl.when((i > 0) & (i < nz - 1))
        def _():
            to_col(i).start()

    def settle(u):
        for b in range(2):
            for m in range(5):
                rs(u, b, m).wait_send()
        for m in range(4):
            ag(u, m).wait_send()
        for save in saves(u):
            save.wait()

    pl.semaphore_wait(barrier, 2 + nz - 1 + 1)
    x_first(x_ref)
    c_first(cot_ref)

    @pl.loop(0, units + 3)
    def _(t):
        @pl.when(t < units)
        def _():
            gate_up(t)

        @pl.when(t >= 3)
        def _():
            project(t - 3)

        @pl.when((t >= 2) & (t < units + 2))
        def _():
            forward(t - 2)

        @pl.when(t < units)
        def _():
            hidden_grad(t)

        @pl.when((t >= 1) & (t < units + 1))
        def _():
            hidden(t - 1)

        @pl.when((t >= 4) & (t < units + 2) & (lax.rem(t, 2) == 0))
        def _():
            spread((t - 4) // 2)

        @pl.when(t == 1)
        def _():
            c_stage(1)

        @pl.when(t < units)
        def _():
            relay(t)

        @pl.when(t == 0)
        def _():
            x_stage(1)

        @pl.when(t >= 5)
        def _():
            settle(t - 5)

        @pl.when(t == units)
        def _():
            x_drain()
            c_drain()

        @pl.when(t == units - 2)
        def _():
            x_save.start()
            cot_save.start()

    def landed(k):
        remote(s_sum.at[0], s_recv.at[k], z_ssem.at[0], z_rsem.at[k], sibling).wait_recv()

    for k in range(nz - 2):
        landed(k)

    to_base = [
        pltpu.make_async_copy(base.at[j], result, base_sem.at[j])
        for j, result in enumerate((out_hbm, tg_hbm))
    ]
    for j in range(2):
        value = s_sum[z, j].astype(F32)
        for k in range(nz - 2):
            value += s_recv[k, j].astype(F32)
        base[j] = value
        to_base[j].start()

    settle(units - 2)
    settle(units - 1)
    for i in range(1, nz - 1):
        to_col(i).wait_send()
    spread(nz - 1)
    to_last = pltpu.make_async_copy(s_sum.at[group(nz - 1)], last_ref, last_sem)
    to_last.start()
    for i in range(nz):
        to_sibling(i).wait_send()
    x_save.wait()
    cot_save.wait()
    for copy in to_base:
        copy.wait()
    to_last.wait()


def weight_kernel(
    x_hbm, dg_hbm, du_hbm, act_hbm, cot_hbm, gate_hbm, up_hbm, down_hbm,
    x, dg, du, act, cot, gate_tile, up_tile, down_tile, in_sem, out_sem,
):
    halves = []
    for k, (src, dst) in enumerate(((x_hbm, x), (dg_hbm, dg), (du_hbm, du), (act_hbm, act), (cot_hbm, cot))):
        width = src.shape[1] // 2
        halves.append([
            pltpu.make_async_copy(src.at[:, cols], dst.at[:, cols], in_sem.at[k, c])
            for c, cols in enumerate((pl.ds(0, width), pl.ds(width, width)))
        ])

    def product(k, left, right, tile, result, before):
        rows, width = left.shape[1] // 2, right.shape[1] // 2
        saves = []
        for i in range(2):
            for c in range(2):
                for step in before.pop((i, c), ()):
                    step()
                here, cols = pl.ds(i * rows, rows), pl.ds(c * width, width)
                tile[i, :, cols] = dot_tn(left[:, here], right[:, cols]).astype(BF16)
                save = pltpu.make_async_copy(
                    tile.at[i, :, cols], result.at[here, cols], out_sem.at[k, i, c])
                save.start()
                saves.append(save)
        return saves

    def start(*names):
        return [halves[k][c].start for k, c in names]

    def wait(*names):
        return [halves[k][c].wait for k, c in names]

    for step in start((0, 0), (1, 0), (1, 1), (0, 1)):
        step()
    saves = product(0, x, dg, gate_tile, gate_hbm, {
        (0, 0): wait((0, 0), (1, 0)) + start((2, 0), (2, 1)),
        (0, 1): wait((1, 1)),
        (1, 0): wait((0, 1)) + start((3, 0), (4, 0), (4, 1), (3, 1)),
    })
    saves += product(1, x, du, up_tile, up_hbm, {(0, 0): wait((2, 0)), (0, 1): wait((2, 1))})
    saves += product(2, act, cot, down_tile, down_hbm, {
        (0, 0): wait((3, 0), (4, 0)), (0, 1): wait((4, 1)), (1, 0): wait((3, 1)),
    })
    for save in saves:
        save.wait()


def weight_grads(x, dgate, dup, act, cot):
    total, feats = x.shape
    half = act.shape[1]
    tall, short = feats // 2, half // 2
    hbm = pl.BlockSpec(memory_space=pl.ANY)

    def buf(*shape):
        return pltpu.VMEM(shape, BF16)

    return pl.pallas_call(
        weight_kernel,
        in_specs=[hbm] * 5,
        out_specs=(hbm, hbm, hbm),
        out_shape=(
            jax.ShapeDtypeStruct((feats, half), BF16),
            jax.ShapeDtypeStruct((feats, half), BF16),
            jax.ShapeDtypeStruct((half, feats), BF16),
        ),
        scratch_shapes=[
            buf(total, feats), buf(total, half), buf(total, half), buf(total, half), buf(total, feats),
            buf(2, tall, half), buf(2, tall, half), buf(2, short, feats),
            pltpu.SemaphoreType.DMA((5, 2)), pltpu.SemaphoreType.DMA((3, 2, 2)),
        ],
        compiler_params=pltpu.CompilerParams(vmem_limit_bytes=60 * 2**20),
        cost_estimate=pl.CostEstimate(
            flops=6 * total * feats * half,
            bytes_accessed=6 * feats * half + 4 * total * feats + 6 * total * half,
            transcendentals=0,
        ),
    )(x, dgate, dup, act, cot)


def per_device(n, nz, tokens, gate_weight, up_weight, down_weight, cotangent):
    tl, feats = tokens.shape
    half = gate_weight.shape[1] // 2
    total = tl * nz * 2
    tr = total // n
    ch = 256 if half % 256 == 0 else half
    chunks = half // ch
    pw = 512 if feats % 512 == 0 else feats
    parts = feats // pw
    sliced = half % 128 != 0
    if sliced:
        start = lax.axis_index("depth") * half
        weights = (
            lax.dynamic_slice_in_dim(gate_weight, start, half, 1),
            lax.dynamic_slice_in_dim(up_weight, start, half, 1),
            lax.dynamic_slice_in_dim(down_weight, start, half, 0),
        )
    else:
        weights = (gate_weight, up_weight, down_weight)

    def sds(*shape):
        return jax.ShapeDtypeStruct(shape, BF16)

    def buf(*shape):
        return pltpu.VMEM(shape, BF16)

    def sem(*shape):
        return pltpu.SemaphoreType.DMA(shape)

    vmem = pl.BlockSpec(memory_space=pltpu.VMEM)
    hbm = pl.BlockSpec(memory_space=pl.ANY)
    if n == 4 and nz == 4 and tl % 32 == 0 and half % 256 == 0 and half >= 512:
        out_part, tg_part, last, x_both, cot_both, act, dgate, dup = pl.pallas_call(
            functools.partial(group_kernel, (nz, tl, half, 2 * pw if parts % 2 == 0 else pw)),
            out_shape=(
                jax.ShapeDtypeStruct((tl, feats), F32), jax.ShapeDtypeStruct((tl, feats), F32),
                sds(2, tl, feats),
                sds(total, feats), sds(total, feats),
                sds(total, half), sds(total, half), sds(total, half),
            ),
            in_specs=[vmem, vmem, hbm, hbm, hbm],
            out_specs=(hbm, hbm, hbm, hbm, hbm, hbm, hbm, hbm),
            scratch_shapes=[
                buf(feats, half), buf(feats, half), buf(half, feats),
                buf(total, feats), buf(total, feats),
                buf(nz, 3, 2 * tl, half), buf(nz, 3, 3, tl // 2, half),
                buf(3, total, half), pltpu.VMEM((2, 2 * tl, feats), F32),
                buf(nz, 2, 2, tl, feats), buf(nz, 2, tl, feats), buf(nz, 2, tl, feats),
                buf(nz - 2, 2, tl, feats), pltpu.VMEM((2, tl, feats), F32),
                sem(3, 2), sem(2), sem(2 * nz, 3),
                sem(nz, 3), sem(nz * 2), sem(nz, 3), sem(nz * 2),
                sem(2 * nz, 2, 5), sem(2 * nz, 2, 5), sem(2 * nz, 4), sem(2 * nz, 4),
                sem(nz), sem(nz), sem(nz), sem(nz), pltpu.SemaphoreType.DMA, sem(2),
            ],
            compiler_params=pltpu.CompilerParams(
                collective_id=1, has_side_effects=True, vmem_limit_bytes=60 * 2**20
            ),
            cost_estimate=pl.CostEstimate(
                flops=12 * total * feats * half, bytes_accessed=8 * feats * half,
                transcendentals=0,
            ),
        )(tokens, cotangent, *weights)
        sent = lax.ppermute(last, "col", LAST)
        output = (out_part + sent[0].astype(F32)).astype(BF16)
        tokens_grad = (tg_part + sent[1].astype(F32)).astype(BF16)
        if feats % 256 == 0:
            return (output, tokens_grad, *weight_grads(x_both, dgate, dup, act, cot_both))
    else:
        sums = [
            buf(2, nz, tl, feats), buf(nz, tl, feats), buf(nz, tl, feats),
            buf(max(nz - 1, 1), tl, feats),
        ]
        sum_sems = [sem(parts), sem(parts), sem(parts, nz), sem(parts, nz)]
        output, tokens_grad, x_both, cot_both, act, dgate, dup = pl.pallas_call(
            functools.partial(kernel, (n, nz, tl, tr, chunks, ch, parts, pw, sliced)),
            out_shape=(
                sds(tl, feats), sds(tl, feats), sds(total, feats), sds(total, feats),
                sds(total, half), sds(total, half), sds(total, half),
            ),
            in_specs=[vmem, vmem, hbm, hbm, hbm],
            out_specs=(vmem, vmem, hbm, hbm, hbm, hbm, hbm),
            scratch_shapes=[
                buf(feats, half), buf(feats, half), buf(half, feats),
                buf(total, feats), buf(total, feats),
                buf(chunks, 2, total, ch), buf(chunks, n - 1, 2, tr, ch),
                buf(chunks, total, ch), buf(chunks, n - 1, tr, ch),
                pltpu.VMEM((chunks, 2, tr, ch), F32),
                buf(total, half), buf(total, half), buf(total, half),
                *sums, *sums,
                sem(3), sem(5),
                sem(nz, 3), sem(nz * 2), sem(nz, 3), sem(nz * 2),
                sem(chunks, n - 1), sem(chunks, n - 1),
                sem(chunks, n - 1), sem(chunks, n - 1),
                sem(chunks, n - 1), sem(chunks, n - 1),
                sem(2, chunks, n - 1), sem(2, chunks, n - 1),
                *sum_sems, *sum_sems,
            ],
            compiler_params=pltpu.CompilerParams(
                collective_id=0, has_side_effects=True, vmem_limit_bytes=60 * 2**20
            ),
            cost_estimate=pl.CostEstimate(
                flops=12 * total * feats * half, bytes_accessed=8 * feats * half,
                transcendentals=0,
            ),
        )(tokens, cotangent, *weights)
    gate_grad = dot_tn(x_both, dgate)
    up_grad = dot_tn(x_both, dup)
    down_grad = dot_tn(act, cot_both)
    return (
        output,
        tokens_grad,
        gate_grad.astype(BF16),
        up_grad.astype(BF16),
        down_grad.astype(BF16),
    )


def solution(mesh):
    return jax.shard_map(
        functools.partial(per_device, mesh.shape["row"], mesh.shape["col"]),
        mesh=mesh,
        in_specs=(
            P(("col", "depth"), "row"),
            P("row", "col"),
            P("row", "col"),
            P("col", "row"),
            P(("col", "depth"), "row"),
        ),
        out_specs=(
            P(("col", "depth"), "row"),
            P(("col", "depth"), "row"),
            P("row", ("col", "depth")),
            P("row", ("col", "depth")),
            P(("col", "depth"), "row"),
        ),
        check_vma=False,
    )
```

```python
import functools

import jax
import jax.numpy as jnp
from jax import lax
from jax.experimental import pallas as pl
from jax.experimental.pallas import tpu as pltpu
from jax.sharding import PartitionSpec as P

MESH = pl.DeviceIdType.MESH
BF16 = jnp.bfloat16
F32 = jnp.float32


def dot_nn(left, right):
    return jnp.dot(left, right, preferred_element_type=F32)


def dot_nt(left, right):
    return lax.dot_general(
        left, right, (((1,), (1,)), ((), ())), preferred_element_type=F32
    )


def dot_tn(left, right):
    return lax.dot_general(
        left, right, (((0,), (0,)), ((), ())), preferred_element_type=F32
    )


def block(index, size):
    return pl.ds(pl.multiple_of(index * size, size), size)


def kernel(
    dims,
    x_ref, cot_ref, wg_hbm, wu_hbm, wd_hbm,
    out_ref, tg_ref, x_out, cot_out, act_out, dg_out, du_out,
    wg, wu, wd, x_full, cot_full,
    gu_part, gu_recv, d_part, d_recv, gu_own, act, dg, du,
    o_part, o_sib, o_sum, o_recv, t_part, t_sib, t_sum, t_recv,
    w_sem, copy_sem, x_ssem, x_rsem, c_ssem, c_rsem,
    gu_ssem, gu_rsem, d_ssem, d_rsem, act_ssem, act_rsem, h_ssem, h_rsem,
    osib_ssem, osib_rsem, oz_ssem, oz_rsem,
    tsib_ssem, tsib_rsem, tz_ssem, tz_rsem,
):
    n, nz, tl, tr, chunks, ch, parts, pw, sliced = dims
    r = lax.axis_index("row")
    z = lax.axis_index("col")
    d = lax.axis_index("depth")
    half = chunks * ch

    def peer(k):
        return {"row": lax.rem(r + k, n)}

    def zpeer(k):
        return {"col": lax.rem(z + k, nz)}

    sibling = {"depth": 1 - d}

    barrier = pltpu.get_barrier_semaphore()
    for k in range(1, n):
        pl.semaphore_signal(barrier, inc=1, device_id=peer(k), device_id_type=MESH)
    for k in range(1, nz):
        pl.semaphore_signal(barrier, inc=1, device_id=zpeer(k), device_id_type=MESH)
    pl.semaphore_signal(barrier, inc=1, device_id=sibling, device_id_type=MESH)

    if sliced:
        sources = (wg_hbm, wu_hbm, wd_hbm)
    else:
        mine = block(d, half)
        sources = (wg_hbm.at[:, mine], wu_hbm.at[:, mine], wd_hbm.at[mine, :])
    loads = [
        pltpu.make_async_copy(src, dst, w_sem.at[i])
        for i, (src, dst) in enumerate(zip(sources, (wg, wu, wd)))
    ]
    for load in loads:
        load.start()

    def remote(src, dst, ssem, rsem, where):
        return pltpu.make_async_remote_copy(
            src_ref=src, dst_ref=dst, send_sem=ssem, recv_sem=rsem,
            device_id=where, device_id_type=MESH,
        )

    def gather(full, ssem, rsem):
        def hop(zz, way):
            slot = zz * 2 + d
            ref = full.at[block(slot, tl)]
            where = ({"col": z + 1}, {"col": z - 1}, sibling)[way]
            return remote(ref, ref, ssem.at[zz, way], rsem.at[slot], where)

        def arrived(slot):
            ref = full.at[block(slot, tl)]
            remote(ref, ref, ssem.at[0, 0], rsem.at[slot], sibling).wait_recv()

        def first(shard):
            full[block(z * 2 + d, tl), :] = shard[...]

            @pl.when(z + 1 < nz)
            def _():
                hop(z, 0).start()

            @pl.when(z > 0)
            def _():
                hop(z, 1).start()

            hop(z, 2).start()

        def stage(s):
            low, high = z - s, z + s

            @pl.when(low >= 0)
            def _():
                arrived(low * 2 + d)

                @pl.when(z + 1 < nz)
                def _():
                    hop(low, 0).start()

                hop(low, 2).start()

            @pl.when(high < nz)
            def _():
                arrived(high * 2 + d)

                @pl.when(z > 0)
                def _():
                    hop(high, 1).start()

                hop(high, 2).start()

        def last():
            for zz in range(nz):
                arrived(zz * 2 + 1 - d)

        def drain():
            for zz in range(nz):
                @pl.when((zz <= z) & (z + 1 < nz))
                def _():
                    hop(zz, 0).wait_send()

                @pl.when((zz >= z) & (z > 0))
                def _():
                    hop(zz, 1).wait_send()

                hop(zz, 2).wait_send()

        return first, stage, last, drain

    x_first, x_stage, x_last, x_drain = gather(x_full, x_ssem, x_rsem)
    c_first, c_stage, c_last, c_drain = gather(cot_full, c_ssem, c_rsem)

    def gu_copy(c, k):
        rows = block(lax.rem(r + k, n), tr)
        return remote(gu_part.at[c, :, rows, :], gu_recv.at[c, k - 1],
                      gu_ssem.at[c, k - 1], gu_rsem.at[c, k - 1], peer(k))

    def d_copy(c, k):
        rows = block(lax.rem(r + k, n), tr)
        return remote(d_part.at[c, rows, :], d_recv.at[c, k - 1],
                      d_ssem.at[c, k - 1], d_rsem.at[c, k - 1], peer(k))

    mine_rows = block(r, tr)

    def act_copy(c, k, owner=None):
        rows = mine_rows if owner is None else block(owner, tr)
        ref = act.at[rows, block(c, ch)]
        return remote(ref, ref, act_ssem.at[c, k - 1], act_rsem.at[c, k - 1], peer(k))

    def h_copy(which, c, k, owner=None):
        rows = mine_rows if owner is None else block(owner, tr)
        ref = (dg, du)[which].at[rows, block(c, ch)]
        return remote(ref, ref, h_ssem.at[which, c, k - 1], h_rsem.at[which, c, k - 1], peer(k))

    def sender(k):
        return lax.rem(r - k + n, n)

    pl.semaphore_wait(barrier, n - 1 + nz - 1 + 1)

    x_first(x_ref)
    for s in range(1, nz):
        if s == nz - 1:
            c_first(cot_ref)
        x_stage(s)
    x_last()
    if nz == 1:
        c_first(cot_ref)
    x_save = pltpu.make_async_copy(x_full, x_out, copy_sem.at[0])
    x_save.start()

    loads[0].wait()
    loads[1].wait()

    @pl.loop(0, chunks)
    def _(c):
        gu_part[c, 0, :, :] = dot_nn(x_full[...], wg[:, block(c, ch)]).astype(BF16)
        gu_part[c, 1, :, :] = dot_nn(x_full[...], wu[:, block(c, ch)]).astype(BF16)
        for k in range(1, n):
            gu_copy(c, k).start()
        for s in range(1, nz):
            @pl.when(c == min(2 * s - 1, chunks - 1))
            def _():
                c_stage(s)

    c_last()
    cot_save = pltpu.make_async_copy(cot_full, cot_out, copy_sem.at[1])
    cot_save.start()
    loads[2].wait()

    @pl.loop(0, chunks)
    def _(c):
        d_part[c, :, :] = dot_nt(cot_full[...], wd[block(c, ch), :]).astype(BF16)
        for k in range(1, n):
            d_copy(c, k).start()

    @pl.loop(0, chunks)
    def _(c):
        gate = gu_part[c, 0, mine_rows, :].astype(F32)
        up = gu_part[c, 1, mine_rows, :].astype(F32)
        for k in range(1, n):
            gu_copy(c, k).wait_recv()
            gate += gu_recv[c, k - 1, 0].astype(F32)
            up += gu_recv[c, k - 1, 1].astype(F32)
        gu_own[c, 0] = gate
        gu_own[c, 1] = up
        act[mine_rows, block(c, ch)] = (gate * jax.nn.sigmoid(gate) * up).astype(BF16)
        for k in range(1, n):
            act_copy(c, k).start()

    @pl.loop(0, chunks)
    def _(c):
        dact = d_part[c, mine_rows, :].astype(F32)
        for k in range(1, n):
            d_copy(c, k).wait_recv()
            dact += d_recv[c, k - 1].astype(F32)
        gate, up = gu_own[c, 0], gu_own[c, 1]
        sig = jax.nn.sigmoid(gate)
        dg[mine_rows, block(c, ch)] = (
            dact * up * sig * (1.0 + gate * (1.0 - sig))
        ).astype(BF16)
        du[mine_rows, block(c, ch)] = (dact * gate * sig).astype(BF16)
        for k in range(1, n):
            h_copy(0, c, k).start()
            h_copy(1, c, k).start()

    def summing(part, sib, total, recv, sib_ssem, sib_rsem, z_ssem, z_rsem):
        def to_sibling(p):
            cols = block(p, pw)
            return remote(part.at[1 - d, :, :, cols], sib.at[:, :, cols],
                          sib_ssem.at[p], sib_rsem.at[p], sibling)

        def to_col(p, k):
            cols = block(p, pw)
            return remote(total.at[lax.rem(z + k, nz), :, cols], recv.at[k - 1, :, cols],
                          z_ssem.at[p, k - 1], z_rsem.at[p, k - 1], zpeer(k))

        def put(p, value):
            cols = block(p, pw)
            for zz in range(nz):
                for dd in range(2):
                    slot = zz * 2 + dd
                    part[dd, zz, :, cols] = value[slot * tl:(slot + 1) * tl].astype(BF16)
            to_sibling(p).start()

        def spread():
            @pl.loop(0, parts)
            def _(p):
                cols = block(p, pw)
                to_sibling(p).wait_recv()
                total[:, :, cols] = (
                    part[d, :, :, cols].astype(F32) + sib[:, :, cols].astype(F32)
                ).astype(BF16)
                for k in range(1, nz):
                    to_col(p, k).start()

        def finish(result):
            @pl.loop(0, parts)
            def _(p):
                cols = block(p, pw)
                value = total[z, :, cols].astype(F32)
                for k in range(1, nz):
                    to_col(p, k).wait_recv()
                    value += recv[k - 1, :, cols].astype(F32)
                result[:, cols] = value.astype(BF16)

        def drain():
            @pl.loop(0, parts)
            def _(p):
                to_sibling(p).wait_send()
                for k in range(1, nz):
                    to_col(p, k).wait_send()

        return put, spread, finish, drain

    o_put, o_spread, o_finish, o_drain = summing(
        o_part, o_sib, o_sum, o_recv, osib_ssem, osib_rsem, oz_ssem, oz_rsem)
    t_put, t_spread, t_finish, t_drain = summing(
        t_part, t_sib, t_sum, t_recv, tsib_ssem, tsib_rsem, tz_ssem, tz_rsem)

    @pl.loop(0, chunks)
    def _(c):
        for k in range(1, n):
            act_copy(c, k, sender(k)).wait_recv()

    act_save = pltpu.make_async_copy(act, act_out, copy_sem.at[2])
    act_save.start()

    @pl.loop(0, parts)
    def _(p):
        o_put(p, dot_nn(act[...], wd[:, block(p, pw)]))

    o_spread()

    @pl.loop(0, chunks)
    def _(c):
        for k in range(1, n):
            h_copy(0, c, k, sender(k)).wait_recv()
            h_copy(1, c, k, sender(k)).wait_recv()

    dg_save = pltpu.make_async_copy(dg, dg_out, copy_sem.at[3])
    du_save = pltpu.make_async_copy(du, du_out, copy_sem.at[4])
    dg_save.start()
    du_save.start()

    @pl.loop(0, parts)
    def _(p):
        t_put(p, dot_nt(dg[...], wg[block(p, pw), :]) + dot_nt(du[...], wu[block(p, pw), :]))

    t_spread()
    o_finish(out_ref)
    t_finish(tg_ref)

    x_drain()
    c_drain()

    @pl.loop(0, chunks)
    def _(c):
        for k in range(1, n):
            gu_copy(c, k).wait_send()
            d_copy(c, k).wait_send()
            act_copy(c, k).wait_send()
            h_copy(0, c, k).wait_send()
            h_copy(1, c, k).wait_send()

    o_drain()
    t_drain()
    for save in (x_save, cot_save, act_save, dg_save, du_save):
        save.wait()


VISITS = (0, 2, 3, 1)
LAST = tuple((z, (z + VISITS[3]) % 4) for z in range(4))


def group_kernel(
    dims,
    x_ref, cot_ref, wg_hbm, wu_hbm, wd_hbm,
    out_hbm, tg_hbm, last_ref, x_out, cot_out, act_out, dg_out, du_out,
    wg, wu, wd, x_full, cot_full, part, recv, h, acc, s_part, s_sib, s_sum, s_recv, base,
    w_sem, copy_sem, save_sem, x_ssem, x_rsem, c_ssem, c_rsem,
    rs_ssem, rs_rsem, ag_ssem, ag_rsem, sib_ssem, sib_rsem, z_ssem, z_rsem, last_sem, base_sem,
):
    nz, tl, half, pw = dims
    feats = x_full.shape[1]
    tg, tr, hw = 2 * tl, tl // 2, half // 2
    units = 2 * nz
    wide = (hw // 2 + 127) // 128 * 128
    widths = (wide, hw - wide)
    starts = (0, wide)
    r = lax.axis_index("row")
    z = lax.axis_index("col")
    d = lax.axis_index("depth")
    rx = r + 1 - 2 * (r % 2)
    ry = r + 2 - 4 * (r // 2)
    rd = 3 - r
    sibling = {"depth": 1 - d}

    barrier = pltpu.get_barrier_semaphore()
    for where in (rx, ry):
        pl.semaphore_signal(barrier, inc=1, device_id={"row": where}, device_id_type=MESH)
    for k in range(1, nz):
        pl.semaphore_signal(barrier, inc=1, device_id={"col": lax.rem(z + k, nz)}, device_id_type=MESH)
    pl.semaphore_signal(barrier, inc=1, device_id=sibling, device_id_type=MESH)

    def load(i, s):
        here = block(s, hw)
        there = block(2 * d + s, hw)
        src, dst = (
            (wg_hbm.at[:, there], wg.at[:, here]),
            (wu_hbm.at[:, there], wu.at[:, here]),
            (wd_hbm.at[there, :], wd.at[here, :]),
        )[i]
        return pltpu.make_async_copy(src, dst, w_sem.at[i, s])

    for i in range(3):
        load(i, 0).start()

    def remote(src, dst, ssem, rsem, where):
        return pltpu.make_async_remote_copy(
            src_ref=src, dst_ref=dst, send_sem=ssem, recv_sem=rsem,
            device_id=where, device_id_type=MESH,
        )

    def index(u):
        return u // 2

    def side(u):
        return lax.rem(u, 2)

    def group(i):
        if isinstance(i, int):
            return lax.rem(z + VISITS[i], nz)
        away = jnp.where(i == 0, 0, jnp.where(i == 3, 1, i + 1))
        return lax.rem(z + away, nz)

    def ends(u):
        flip = lax.rem(u, 2)
        return rx + flip * (ry - rx), ry + flip * (rx - ry)

    def span_of(u, b):
        return pl.ds(pl.multiple_of(side(u) * hw + starts[b], 128), widths[b])

    def gather(full, ssem, rsem):
        def hop(zz, to):
            slot = zz * 2 + d
            ref = full.at[block(slot, tl)]
            where = ({"col": z + 1}, {"col": z - 1}, sibling)[to]
            return remote(ref, ref, ssem.at[zz, to], rsem.at[slot], where)

        def arrived(slot):
            ref = full.at[block(slot, tl)]
            remote(ref, ref, ssem.at[0, 0], rsem.at[slot], sibling).wait_recv()

        def first(shard):
            full[block(z * 2 + d, tl), :] = shard[...]
            hop(z, 2).start()

            @pl.when(z + 1 < nz)
            def _():
                hop(z, 0).start()

            @pl.when(z > 0)
            def _():
                hop(z, 1).start()

        def stage(s):
            low, high = z - s, z + s

            @pl.when(low >= 0)
            def _():
                arrived(low * 2 + d)

                @pl.when(z + 1 < nz)
                def _():
                    hop(low, 0).start()

                hop(low, 2).start()

            @pl.when(high < nz)
            def _():
                arrived(high * 2 + d)

                @pl.when(z > 0)
                def _():
                    hop(high, 1).start()

                hop(high, 2).start()

        def other(g):
            arrived(g * 2 + 1 - d)

        def drain():
            for zz in range(nz):
                @pl.when((zz <= z) & (z + 1 < nz))
                def _():
                    hop(zz, 0).wait_send()

                @pl.when((zz >= z) & (z > 0))
                def _():
                    hop(zz, 1).wait_send()

                hop(zz, 2).wait_send()

        return first, stage, other, drain

    x_first, x_stage, x_other, x_drain = gather(x_full, x_ssem, x_rsem)
    c_first, c_stage, c_other, c_drain = gather(cot_full, c_ssem, c_rsem)

    def rs(u, b, m):
        i = index(u)
        near, far = ends(u) if b == 0 else ends(u)[::-1]
        slot = m if m < 3 else m - 3
        owner = (rd, near, far)[slot]
        to = far if m == 2 else near
        cols = span_of(u, b)
        which = (pl.ds(0, 2), pl.ds(0, 2), pl.ds(0, 3), pl.ds(2, 1), pl.ds(2, 1))[m]
        return remote(part.at[i, which, block(owner, tr), cols],
                      recv.at[i, slot, which, :, cols],
                      rs_ssem.at[u, b, m], rs_rsem.at[u, b, m], {"row": to})

    def rows(g, owner):
        return pl.ds(pl.multiple_of(g * tg + owner * tr, tr), tr)

    def ag(u, m, incoming=False):
        g = group(index(u))
        p, q = ends(u)
        owner = (p, q, rd, rd)[m] if incoming else (r, r, p, q)[m]
        cols = block(side(u), hw) if m < 2 else span_of(u, m - 2)
        ref = h.at[:, rows(g, owner), cols]
        to = (p, q, q, p)[m]
        return remote(ref, ref, ag_ssem.at[u, m], ag_rsem.at[u, m], {"row": to})

    def to_sibling(i, p):
        g, cols = group(i), block(p, pw)
        return remote(s_part.at[g, :, 1 - d, :, cols], s_sib.at[g, :, :, cols],
                      sib_ssem.at[i, p], sib_rsem.at[i, p], sibling)

    def to_col(i):
        g = group(i)
        k = lax.rem(z - g + nz, nz) - 1
        return remote(s_sum.at[g], s_recv.at[k], z_ssem.at[i], z_rsem.at[k], {"col": g})

    def saves(u):
        span, cols = block(group(index(u)), tg), block(side(u), hw)
        return [
            pltpu.make_async_copy(h.at[j, span, cols], out.at[span, cols], save_sem.at[u, j])
            for j, out in enumerate((act_out, dg_out, du_out))
        ]

    x_save = pltpu.make_async_copy(x_full, x_out, copy_sem.at[0])
    cot_save = pltpu.make_async_copy(cot_full, cot_out, copy_sem.at[1])

    def gate_up(u):
        i = index(u)
        g = group(i)
        span = block(g, tg)
        cols = block(side(u), hw)

        @pl.when((u == 2) | (u == 4))
        def _():
            x_stage(1 + u // 2)

        @pl.when(side(u) == 0)
        def _():
            x_other(g)

        @pl.when(u < 2)
        def _():
            load(0, u).wait()
            load(1, u).wait()

        part[i, 0, :, cols] = dot_nn(x_full[span, :], wg[:, cols]).astype(BF16)
        part[i, 1, :, cols] = dot_nn(x_full[span, :], wu[:, cols]).astype(BF16)
        for m in range(2):
            for b in range(2):
                rs(u, b, m).start()

    def hidden_grad(u):
        i = index(u)
        g = group(i)
        span = block(g, tg)
        cols = block(side(u), hw)

        @pl.when((u == 2) | (u == 4))
        def _():
            c_stage(1 + u // 2)

        @pl.when(side(u) == 0)
        def _():
            c_other(g)

        @pl.when(u < 2)
        def _():
            load(2, u).wait()

        @pl.when(u == 0)
        def _():
            for k in range(3):
                load(k, 1).start()

        part[i, 2, :, cols] = dot_nt(cot_full[span, :], wd[cols, :]).astype(BF16)
        for m in range(3, 5):
            for b in range(2):
                rs(u, b, m).start()

    def relay(u):
        i = index(u)
        for b in range(2):
            rs(u, b, 0).wait_recv()
            rs(u, b, 3).wait_recv()
            spot, cols = block(ends(u)[1 - b], tr), span_of(u, b)
            part[i, :, spot, cols] = (
                part[i, :, spot, cols].astype(F32) + recv[i, 0, :, :, cols].astype(F32)
            ).astype(BF16)
            rs(u, b, 2).start()

    def hidden(u):
        i = index(u)
        own = rows(group(i), r)
        for b in range(2):
            for m in (1, 4, 2):
                rs(u, b, m).wait_recv()
            cols = span_of(u, b)
            gate, up, dact = (
                part[i, j, block(r, tr), cols].astype(F32)
                + recv[i, 1, j, :, cols].astype(F32)
                + recv[i, 2, j, :, cols].astype(F32)
                for j in range(3)
            )
            sig = jax.nn.sigmoid(gate)
            h[0, own, cols] = (gate * sig * up).astype(BF16)
            h[1, own, cols] = (dact * up * sig * (1.0 + gate * (1.0 - sig))).astype(BF16)
            h[2, own, cols] = (dact * gate * sig).astype(BF16)
        ag(u, 0).start()
        ag(u, 1).start()

    def forward(u):
        for m in range(2):
            ag(u, m, True).wait_recv()
            ag(u, m + 2).start()

    def project(u):
        i = index(u)
        g = group(i)
        span, hid = block(g, tg), block(side(u), hw)
        ag(u, 2, True).wait_recv()
        ag(u, 3, True).wait_recv()
        for save in saves(u):
            save.start()

        def products(cols):
            out = dot_nn(h[0, span, hid], wd[hid, cols])
            grad = dot_nt(h[1, span, hid], wg[cols, hid]) + dot_nt(h[2, span, hid], wu[cols, hid])
            return out, grad

        @pl.when(side(u) == 0)
        def _():
            @pl.loop(0, feats // pw)
            def _(p):
                cols = block(p, pw)
                out, grad = products(cols)
                acc[0, :, cols] = out
                acc[1, :, cols] = grad

        @pl.when(side(u) == 1)
        def _():
            @pl.loop(0, feats // pw)
            def _(p):
                cols = block(p, pw)
                for j, value in enumerate(products(cols)):
                    value = (value + acc[j, :, cols]).astype(BF16)
                    for dd in range(2):
                        s_part[g, j, dd, :, cols] = value[dd * tl:(dd + 1) * tl]
                to_sibling(i, p).start()

    def spread(i):
        g = group(i)
        for p in range(feats // pw):
            to_sibling(i, p).wait_recv()
            cols = pl.ds(p * pw, pw)
            for j in range(2):
                s_sum[g, j, :, cols] = (
                    s_part[g, j, d, :, cols].astype(F32) + s_sib[g, j, :, cols].astype(F32)
                ).astype(BF16)


        @pl.when((i > 0) & (i < nz - 1))
        def _():
            to_col(i).start()

    def settle(u):
        for b in range(2):
            for m in range(5):
                rs(u, b, m).wait_send()
        for m in range(4):
            ag(u, m).wait_send()
        for save in saves(u):
            save.wait()

    pl.semaphore_wait(barrier, 2 + nz - 1 + 1)
    x_first(x_ref)
    c_first(cot_ref)

    @pl.loop(0, units + 3)
    def _(t):
        @pl.when(t < units)
        def _():
            gate_up(t)

        @pl.when(t >= 3)
        def _():
            project(t - 3)

        @pl.when((t >= 2) & (t < units + 2))
        def _():
            forward(t - 2)

        @pl.when(t < units)
        def _():
            hidden_grad(t)

        @pl.when((t >= 1) & (t < units + 1))
        def _():
            hidden(t - 1)

        @pl.when((t >= 4) & (t < units + 2) & (lax.rem(t, 2) == 0))
        def _():
            spread((t - 4) // 2)

        @pl.when(t == 1)
        def _():
            c_stage(1)

        @pl.when(t < units)
        def _():
            relay(t)

        @pl.when(t == 0)
        def _():
            x_stage(1)

        @pl.when(t >= 5)
        def _():
            settle(t - 5)

        @pl.when(t == units)
        def _():
            x_drain()
            c_drain()

        @pl.when(t == units - 2)
        def _():
            x_save.start()
            cot_save.start()

    def landed(k):
        remote(s_sum.at[0], s_recv.at[k], z_ssem.at[0], z_rsem.at[k], sibling).wait_recv()

    for k in range(nz - 2):
        landed(k)

    to_base = [
        pltpu.make_async_copy(base.at[j], result, base_sem.at[j])
        for j, result in enumerate((out_hbm, tg_hbm))
    ]
    for j in range(2):
        value = s_sum[z, j].astype(F32)
        for k in range(nz - 2):
            value += s_recv[k, j].astype(F32)
        base[j] = value
        to_base[j].start()

    settle(units - 2)
    settle(units - 1)
    for i in range(1, nz - 1):
        to_col(i).wait_send()
    spread(nz - 1)
    to_last = pltpu.make_async_copy(s_sum.at[group(nz - 1)], last_ref, last_sem)
    to_last.start()
    for i in range(nz):
        for p in range(feats // pw):
            to_sibling(i, p).wait_send()
    x_save.wait()
    cot_save.wait()
    for copy in to_base:
        copy.wait()
    to_last.wait()


def weight_kernel(
    x_hbm, dg_hbm, du_hbm, act_hbm, cot_hbm, gate_hbm, up_hbm, down_hbm,
    x, dg, du, act, cot, gate_tile, up_tile, down_tile, in_sem, out_sem,
):
    halves = []
    for k, (src, dst) in enumerate(((x_hbm, x), (dg_hbm, dg), (du_hbm, du), (act_hbm, act), (cot_hbm, cot))):
        width = (src.shape[1] // 2 + 255) // 256 * 256
        halves.append([
            pltpu.make_async_copy(src.at[:, cols], dst.at[:, cols], in_sem.at[k, c])
            for c, cols in enumerate((pl.ds(0, width), pl.ds(width, src.shape[1] - width)))
        ])

    def spans(ref, cut):
        return pl.ds(0, cut), pl.ds(cut, ref.shape[1] - cut)

    def product(k, left, right, tile, result, before):
        rows, width = ((ref.shape[1] // 2 + 255) // 256 * 256 for ref in (left, right))
        saves = []
        for i in range(2):
            for c in range(2):
                for step in before.pop((i, c), ()):
                    step()
                here, cols = spans(left, rows)[i], spans(right, width)[c]
                tile[i, :spans(left, rows)[i].size, cols] = dot_tn(left[:, here], right[:, cols]).astype(BF16)
                save = pltpu.make_async_copy(
                    tile.at[i, :spans(left, rows)[i].size, cols], result.at[here, cols], out_sem.at[k, i, c])
                save.start()
                saves.append(save)
        return saves

    def start(*names):
        return [halves[k][c].start for k, c in names]

    def wait(*names):
        return [halves[k][c].wait for k, c in names]

    for step in start((0, 0), (1, 0), (1, 1), (0, 1)):
        step()
    saves = product(0, x, dg, gate_tile, gate_hbm, {
        (0, 0): wait((0, 0), (1, 0)) + start((2, 0), (2, 1)),
        (0, 1): wait((1, 1)),
        (1, 0): wait((0, 1)) + start((3, 0), (4, 0), (4, 1), (3, 1)),
    })
    saves += product(1, x, du, up_tile, up_hbm, {(0, 0): wait((2, 0)), (0, 1): wait((2, 1))})
    saves += product(2, act, cot, down_tile, down_hbm, {
        (0, 0): wait((3, 0), (4, 0)), (0, 1): wait((4, 1)), (1, 0): wait((3, 1)),
    })
    for save in saves:
        save.wait()


def weight_grads(x, dgate, dup, act, cot):
    total, feats = x.shape
    half = act.shape[1]
    tall, short = ((size // 2 + 255) // 256 * 256 for size in (feats, half))
    hbm = pl.BlockSpec(memory_space=pl.ANY)

    def buf(*shape):
        return pltpu.VMEM(shape, BF16)

    return pl.pallas_call(
        weight_kernel,
        in_specs=[hbm] * 5,
        out_specs=(hbm, hbm, hbm),
        out_shape=(
            jax.ShapeDtypeStruct((feats, half), BF16),
            jax.ShapeDtypeStruct((feats, half), BF16),
            jax.ShapeDtypeStruct((half, feats), BF16),
        ),
        scratch_shapes=[
            buf(total, feats), buf(total, half), buf(total, half), buf(total, half), buf(total, feats),
            buf(2, tall, half), buf(2, tall, half), buf(2, short, feats),
            pltpu.SemaphoreType.DMA((5, 2)), pltpu.SemaphoreType.DMA((3, 2, 2)),
        ],
        compiler_params=pltpu.CompilerParams(vmem_limit_bytes=60 * 2**20),
        cost_estimate=pl.CostEstimate(
            flops=6 * total * feats * half,
            bytes_accessed=6 * feats * half + 4 * total * feats + 6 * total * half,
            transcendentals=0,
        ),
    )(x, dgate, dup, act, cot)


def per_device(n, nz, tokens, gate_weight, up_weight, down_weight, cotangent):
    tl, feats = tokens.shape
    half = gate_weight.shape[1] // 2
    total = tl * nz * 2
    tr = total // n
    ch = 256 if half % 256 == 0 else half
    chunks = half // ch
    pw = 512 if feats % 512 == 0 else feats
    parts = feats // pw
    sliced = half % 128 != 0
    if sliced:
        start = lax.axis_index("depth") * half
        weights = (
            lax.dynamic_slice_in_dim(gate_weight, start, half, 1),
            lax.dynamic_slice_in_dim(up_weight, start, half, 1),
            lax.dynamic_slice_in_dim(down_weight, start, half, 0),
        )
    else:
        weights = (gate_weight, up_weight, down_weight)

    def sds(*shape):
        return jax.ShapeDtypeStruct(shape, BF16)

    def buf(*shape):
        return pltpu.VMEM(shape, BF16)

    def sem(*shape):
        return pltpu.SemaphoreType.DMA(shape)

    vmem = pl.BlockSpec(memory_space=pltpu.VMEM)
    hbm = pl.BlockSpec(memory_space=pl.ANY)
    if n == 4 and nz == 4 and tl % 32 == 0 and half % 256 == 0 and half >= 512:
        out_part, tg_part, last, x_both, cot_both, act, dgate, dup = pl.pallas_call(
            functools.partial(group_kernel, (nz, tl, half, 2 * pw if parts % 2 == 0 else pw)),
            out_shape=(
                jax.ShapeDtypeStruct((tl, feats), F32), jax.ShapeDtypeStruct((tl, feats), F32),
                sds(2, tl, feats),
                sds(total, feats), sds(total, feats),
                sds(total, half), sds(total, half), sds(total, half),
            ),
            in_specs=[vmem, vmem, hbm, hbm, hbm],
            out_specs=(hbm, hbm, hbm, hbm, hbm, hbm, hbm, hbm),
            scratch_shapes=[
                buf(feats, half), buf(feats, half), buf(half, feats),
                buf(total, feats), buf(total, feats),
                buf(nz, 3, 2 * tl, half), buf(nz, 3, 3, tl // 2, half),
                buf(3, total, half), pltpu.VMEM((2, 2 * tl, feats), F32),
                buf(nz, 2, 2, tl, feats), buf(nz, 2, tl, feats), buf(nz, 2, tl, feats),
                buf(nz - 2, 2, tl, feats), pltpu.VMEM((2, tl, feats), F32),
                sem(3, 2), sem(2), sem(2 * nz, 3),
                sem(nz, 3), sem(nz * 2), sem(nz, 3), sem(nz * 2),
                sem(2 * nz, 2, 5), sem(2 * nz, 2, 5), sem(2 * nz, 4), sem(2 * nz, 4),
                sem(nz, parts), sem(nz, parts), sem(nz), sem(nz), pltpu.SemaphoreType.DMA, sem(2),
            ],
            compiler_params=pltpu.CompilerParams(
                collective_id=1, has_side_effects=True, vmem_limit_bytes=60 * 2**20
            ),
            cost_estimate=pl.CostEstimate(
                flops=12 * total * feats * half, bytes_accessed=8 * feats * half,
                transcendentals=0,
            ),
        )(tokens, cotangent, *weights)
        sent = lax.ppermute(last, "col", LAST)
        output = (out_part + sent[0].astype(F32)).astype(BF16)
        tokens_grad = (tg_part + sent[1].astype(F32)).astype(BF16)
        if feats % 256 == 0:
            return (output, tokens_grad, *weight_grads(x_both, dgate, dup, act, cot_both))
    else:
        sums = [
            buf(2, nz, tl, feats), buf(nz, tl, feats), buf(nz, tl, feats),
            buf(max(nz - 1, 1), tl, feats),
        ]
        sum_sems = [sem(parts), sem(parts), sem(parts, nz), sem(parts, nz)]
        output, tokens_grad, x_both, cot_both, act, dgate, dup = pl.pallas_call(
            functools.partial(kernel, (n, nz, tl, tr, chunks, ch, parts, pw, sliced)),
            out_shape=(
                sds(tl, feats), sds(tl, feats), sds(total, feats), sds(total, feats),
                sds(total, half), sds(total, half), sds(total, half),
            ),
            in_specs=[vmem, vmem, hbm, hbm, hbm],
            out_specs=(vmem, vmem, hbm, hbm, hbm, hbm, hbm),
            scratch_shapes=[
                buf(feats, half), buf(feats, half), buf(half, feats),
                buf(total, feats), buf(total, feats),
                buf(chunks, 2, total, ch), buf(chunks, n - 1, 2, tr, ch),
                buf(chunks, total, ch), buf(chunks, n - 1, tr, ch),
                pltpu.VMEM((chunks, 2, tr, ch), F32),
                buf(total, half), buf(total, half), buf(total, half),
                *sums, *sums,
                sem(3), sem(5),
                sem(nz, 3), sem(nz * 2), sem(nz, 3), sem(nz * 2),
                sem(chunks, n - 1), sem(chunks, n - 1),
                sem(chunks, n - 1), sem(chunks, n - 1),
                sem(chunks, n - 1), sem(chunks, n - 1),
                sem(2, chunks, n - 1), sem(2, chunks, n - 1),
                *sum_sems, *sum_sems,
            ],
            compiler_params=pltpu.CompilerParams(
                collective_id=0, has_side_effects=True, vmem_limit_bytes=60 * 2**20
            ),
            cost_estimate=pl.CostEstimate(
                flops=12 * total * feats * half, bytes_accessed=8 * feats * half,
                transcendentals=0,
            ),
        )(tokens, cotangent, *weights)
    gate_grad = dot_tn(x_both, dgate)
    up_grad = dot_tn(x_both, dup)
    down_grad = dot_tn(act, cot_both)
    return (
        output,
        tokens_grad,
        gate_grad.astype(BF16),
        up_grad.astype(BF16),
        down_grad.astype(BF16),
    )


def solution(mesh):
    return jax.shard_map(
        functools.partial(per_device, mesh.shape["row"], mesh.shape["col"]),
        mesh=mesh,
        in_specs=(
            P(("col", "depth"), "row"),
            P("row", "col"),
            P("row", "col"),
            P("col", "row"),
            P(("col", "depth"), "row"),
        ),
        out_specs=(
            P(("col", "depth"), "row"),
            P(("col", "depth"), "row"),
            P("row", ("col", "depth")),
            P("row", ("col", "depth")),
            P(("col", "depth"), "row"),
        ),
        check_vma=False,
    )
```

```python
import functools

import jax
import jax.numpy as jnp
from jax import lax
from jax.experimental import pallas as pl
from jax.experimental.pallas import tpu as pltpu
from jax.sharding import PartitionSpec as P

MESH = pl.DeviceIdType.MESH
BF16 = jnp.bfloat16
F32 = jnp.float32


def dot_nn(left, right):
    return jnp.dot(left, right, preferred_element_type=F32)


def dot_nt(left, right):
    return lax.dot_general(
        left, right, (((1,), (1,)), ((), ())), preferred_element_type=F32
    )


def dot_tn(left, right):
    return lax.dot_general(
        left, right, (((0,), (0,)), ((), ())), preferred_element_type=F32
    )


def block(index, size):
    return pl.ds(pl.multiple_of(index * size, size), size)


def kernel(
    dims,
    x_ref, cot_ref, wg_hbm, wu_hbm, wd_hbm,
    out_ref, tg_ref, x_out, cot_out, act_out, dg_out, du_out,
    wg, wu, wd, x_full, cot_full,
    gu_part, gu_recv, d_part, d_recv, gu_own, act, dg, du,
    o_part, o_sib, o_sum, o_recv, t_part, t_sib, t_sum, t_recv,
    w_sem, copy_sem, x_ssem, x_rsem, c_ssem, c_rsem,
    gu_ssem, gu_rsem, d_ssem, d_rsem, act_ssem, act_rsem, h_ssem, h_rsem,
    osib_ssem, osib_rsem, oz_ssem, oz_rsem,
    tsib_ssem, tsib_rsem, tz_ssem, tz_rsem,
):
    n, nz, tl, tr, chunks, ch, parts, pw, sliced = dims
    r = lax.axis_index("row")
    z = lax.axis_index("col")
    d = lax.axis_index("depth")
    half = chunks * ch

    def peer(k):
        return {"row": lax.rem(r + k, n)}

    def zpeer(k):
        return {"col": lax.rem(z + k, nz)}

    sibling = {"depth": 1 - d}

    barrier = pltpu.get_barrier_semaphore()
    for k in range(1, n):
        pl.semaphore_signal(barrier, inc=1, device_id=peer(k), device_id_type=MESH)
    for k in range(1, nz):
        pl.semaphore_signal(barrier, inc=1, device_id=zpeer(k), device_id_type=MESH)
    pl.semaphore_signal(barrier, inc=1, device_id=sibling, device_id_type=MESH)

    if sliced:
        sources = (wg_hbm, wu_hbm, wd_hbm)
    else:
        mine = block(d, half)
        sources = (wg_hbm.at[:, mine], wu_hbm.at[:, mine], wd_hbm.at[mine, :])
    loads = [
        pltpu.make_async_copy(src, dst, w_sem.at[i])
        for i, (src, dst) in enumerate(zip(sources, (wg, wu, wd)))
    ]
    for load in loads:
        load.start()

    def remote(src, dst, ssem, rsem, where):
        return pltpu.make_async_remote_copy(
            src_ref=src, dst_ref=dst, send_sem=ssem, recv_sem=rsem,
            device_id=where, device_id_type=MESH,
        )

    def gather(full, ssem, rsem):
        def hop(zz, way):
            slot = zz * 2 + d
            ref = full.at[block(slot, tl)]
            where = ({"col": z + 1}, {"col": z - 1}, sibling)[way]
            return remote(ref, ref, ssem.at[zz, way], rsem.at[slot], where)

        def arrived(slot):
            ref = full.at[block(slot, tl)]
            remote(ref, ref, ssem.at[0, 0], rsem.at[slot], sibling).wait_recv()

        def first(shard):
            full[block(z * 2 + d, tl), :] = shard[...]

            @pl.when(z + 1 < nz)
            def _():
                hop(z, 0).start()

            @pl.when(z > 0)
            def _():
                hop(z, 1).start()

            hop(z, 2).start()

        def stage(s):
            low, high = z - s, z + s

            @pl.when(low >= 0)
            def _():
                arrived(low * 2 + d)

                @pl.when(z + 1 < nz)
                def _():
                    hop(low, 0).start()

                hop(low, 2).start()

            @pl.when(high < nz)
            def _():
                arrived(high * 2 + d)

                @pl.when(z > 0)
                def _():
                    hop(high, 1).start()

                hop(high, 2).start()

        def last():
            for zz in range(nz):
                arrived(zz * 2 + 1 - d)

        def drain():
            for zz in range(nz):
                @pl.when((zz <= z) & (z + 1 < nz))
                def _():
                    hop(zz, 0).wait_send()

                @pl.when((zz >= z) & (z > 0))
                def _():
                    hop(zz, 1).wait_send()

                hop(zz, 2).wait_send()

        return first, stage, last, drain

    x_first, x_stage, x_last, x_drain = gather(x_full, x_ssem, x_rsem)
    c_first, c_stage, c_last, c_drain = gather(cot_full, c_ssem, c_rsem)

    def gu_copy(c, k):
        rows = block(lax.rem(r + k, n), tr)
        return remote(gu_part.at[c, :, rows, :], gu_recv.at[c, k - 1],
                      gu_ssem.at[c, k - 1], gu_rsem.at[c, k - 1], peer(k))

    def d_copy(c, k):
        rows = block(lax.rem(r + k, n), tr)
        return remote(d_part.at[c, rows, :], d_recv.at[c, k - 1],
                      d_ssem.at[c, k - 1], d_rsem.at[c, k - 1], peer(k))

    mine_rows = block(r, tr)

    def act_copy(c, k, owner=None):
        rows = mine_rows if owner is None else block(owner, tr)
        ref = act.at[rows, block(c, ch)]
        return remote(ref, ref, act_ssem.at[c, k - 1], act_rsem.at[c, k - 1], peer(k))

    def h_copy(which, c, k, owner=None):
        rows = mine_rows if owner is None else block(owner, tr)
        ref = (dg, du)[which].at[rows, block(c, ch)]
        return remote(ref, ref, h_ssem.at[which, c, k - 1], h_rsem.at[which, c, k - 1], peer(k))

    def sender(k):
        return lax.rem(r - k + n, n)

    pl.semaphore_wait(barrier, n - 1 + nz - 1 + 1)

    x_first(x_ref)
    for s in range(1, nz):
        if s == nz - 1:
            c_first(cot_ref)
        x_stage(s)
    x_last()
    if nz == 1:
        c_first(cot_ref)
    x_save = pltpu.make_async_copy(x_full, x_out, copy_sem.at[0])
    x_save.start()

    loads[0].wait()
    loads[1].wait()

    @pl.loop(0, chunks)
    def _(c):
        gu_part[c, 0, :, :] = dot_nn(x_full[...], wg[:, block(c, ch)]).astype(BF16)
        gu_part[c, 1, :, :] = dot_nn(x_full[...], wu[:, block(c, ch)]).astype(BF16)
        for k in range(1, n):
            gu_copy(c, k).start()
        for s in range(1, nz):
            @pl.when(c == min(2 * s - 1, chunks - 1))
            def _():
                c_stage(s)

    c_last()
    cot_save = pltpu.make_async_copy(cot_full, cot_out, copy_sem.at[1])
    cot_save.start()
    loads[2].wait()

    @pl.loop(0, chunks)
    def _(c):
        d_part[c, :, :] = dot_nt(cot_full[...], wd[block(c, ch), :]).astype(BF16)
        for k in range(1, n):
            d_copy(c, k).start()

    @pl.loop(0, chunks)
    def _(c):
        gate = gu_part[c, 0, mine_rows, :].astype(F32)
        up = gu_part[c, 1, mine_rows, :].astype(F32)
        for k in range(1, n):
            gu_copy(c, k).wait_recv()
            gate += gu_recv[c, k - 1, 0].astype(F32)
            up += gu_recv[c, k - 1, 1].astype(F32)
        gu_own[c, 0] = gate
        gu_own[c, 1] = up
        act[mine_rows, block(c, ch)] = (gate * jax.nn.sigmoid(gate) * up).astype(BF16)
        for k in range(1, n):
            act_copy(c, k).start()

    @pl.loop(0, chunks)
    def _(c):
        dact = d_part[c, mine_rows, :].astype(F32)
        for k in range(1, n):
            d_copy(c, k).wait_recv()
            dact += d_recv[c, k - 1].astype(F32)
        gate, up = gu_own[c, 0], gu_own[c, 1]
        sig = jax.nn.sigmoid(gate)
        dg[mine_rows, block(c, ch)] = (
            dact * up * sig * (1.0 + gate * (1.0 - sig))
        ).astype(BF16)
        du[mine_rows, block(c, ch)] = (dact * gate * sig).astype(BF16)
        for k in range(1, n):
            h_copy(0, c, k).start()
            h_copy(1, c, k).start()

    def summing(part, sib, total, recv, sib_ssem, sib_rsem, z_ssem, z_rsem):
        def to_sibling(p):
            cols = block(p, pw)
            return remote(part.at[1 - d, :, :, cols], sib.at[:, :, cols],
                          sib_ssem.at[p], sib_rsem.at[p], sibling)

        def to_col(p, k):
            cols = block(p, pw)
            return remote(total.at[lax.rem(z + k, nz), :, cols], recv.at[k - 1, :, cols],
                          z_ssem.at[p, k - 1], z_rsem.at[p, k - 1], zpeer(k))

        def put(p, value):
            cols = block(p, pw)
            for zz in range(nz):
                for dd in range(2):
                    slot = zz * 2 + dd
                    part[dd, zz, :, cols] = value[slot * tl:(slot + 1) * tl].astype(BF16)
            to_sibling(p).start()

        def spread():
            @pl.loop(0, parts)
            def _(p):
                cols = block(p, pw)
                to_sibling(p).wait_recv()
                total[:, :, cols] = (
                    part[d, :, :, cols].astype(F32) + sib[:, :, cols].astype(F32)
                ).astype(BF16)
                for k in range(1, nz):
                    to_col(p, k).start()

        def finish(result):
            @pl.loop(0, parts)
            def _(p):
                cols = block(p, pw)
                value = total[z, :, cols].astype(F32)
                for k in range(1, nz):
                    to_col(p, k).wait_recv()
                    value += recv[k - 1, :, cols].astype(F32)
                result[:, cols] = value.astype(BF16)

        def drain():
            @pl.loop(0, parts)
            def _(p):
                to_sibling(p).wait_send()
                for k in range(1, nz):
                    to_col(p, k).wait_send()

        return put, spread, finish, drain

    o_put, o_spread, o_finish, o_drain = summing(
        o_part, o_sib, o_sum, o_recv, osib_ssem, osib_rsem, oz_ssem, oz_rsem)
    t_put, t_spread, t_finish, t_drain = summing(
        t_part, t_sib, t_sum, t_recv, tsib_ssem, tsib_rsem, tz_ssem, tz_rsem)

    @pl.loop(0, chunks)
    def _(c):
        for k in range(1, n):
            act_copy(c, k, sender(k)).wait_recv()

    act_save = pltpu.make_async_copy(act, act_out, copy_sem.at[2])
    act_save.start()

    @pl.loop(0, parts)
    def _(p):
        o_put(p, dot_nn(act[...], wd[:, block(p, pw)]))

    o_spread()

    @pl.loop(0, chunks)
    def _(c):
        for k in range(1, n):
            h_copy(0, c, k, sender(k)).wait_recv()
            h_copy(1, c, k, sender(k)).wait_recv()

    dg_save = pltpu.make_async_copy(dg, dg_out, copy_sem.at[3])
    du_save = pltpu.make_async_copy(du, du_out, copy_sem.at[4])
    dg_save.start()
    du_save.start()

    @pl.loop(0, parts)
    def _(p):
        t_put(p, dot_nt(dg[...], wg[block(p, pw), :]) + dot_nt(du[...], wu[block(p, pw), :]))

    t_spread()
    o_finish(out_ref)
    t_finish(tg_ref)

    x_drain()
    c_drain()

    @pl.loop(0, chunks)
    def _(c):
        for k in range(1, n):
            gu_copy(c, k).wait_send()
            d_copy(c, k).wait_send()
            act_copy(c, k).wait_send()
            h_copy(0, c, k).wait_send()
            h_copy(1, c, k).wait_send()

    o_drain()
    t_drain()
    for save in (x_save, cot_save, act_save, dg_save, du_save):
        save.wait()


VISITS = (0, 2, 3, 1)
LAST = tuple((z, (z + VISITS[3]) % 4) for z in range(4))


def group_kernel(
    dims,
    x_ref, cot_ref, wg_hbm, wu_hbm, wd_hbm,
    out_hbm, tg_hbm, last_ref, x_out, cot_out, act_out, dg_out, du_out,
    wg, wu, wd, x_full, cot_full, part, recv, h, acc, s_part, s_sib, s_sum, s_recv, base,
    w_sem, copy_sem, save_sem, x_ssem, x_rsem, c_ssem, c_rsem,
    rs_ssem, rs_rsem, ag_ssem, ag_rsem, sib_ssem, sib_rsem, z_ssem, z_rsem, last_sem, base_sem,
):
    nz, tl, half, pw = dims
    feats = x_full.shape[1]
    tg, tr, hw = 2 * tl, tl // 2, half // 2
    units = 2 * nz
    wide = (hw // 2 + 127) // 128 * 128
    widths = (wide, hw - wide)
    starts = (0, wide)
    r = lax.axis_index("row")
    z = lax.axis_index("col")
    d = lax.axis_index("depth")
    rx = r + 1 - 2 * (r % 2)
    ry = r + 2 - 4 * (r // 2)
    rd = 3 - r
    sibling = {"depth": 1 - d}

    barrier = pltpu.get_barrier_semaphore()
    for where in (rx, ry):
        pl.semaphore_signal(barrier, inc=1, device_id={"row": where}, device_id_type=MESH)
    for k in range(1, nz):
        pl.semaphore_signal(barrier, inc=1, device_id={"col": lax.rem(z + k, nz)}, device_id_type=MESH)
    pl.semaphore_signal(barrier, inc=1, device_id=sibling, device_id_type=MESH)

    def load(i, s):
        here = block(s, hw)
        there = block(2 * d + s, hw)
        src, dst = (
            (wg_hbm.at[:, there], wg.at[:, here]),
            (wu_hbm.at[:, there], wu.at[:, here]),
            (wd_hbm.at[there, :], wd.at[here, :]),
        )[i]
        return pltpu.make_async_copy(src, dst, w_sem.at[i, s])

    for i in range(2):
        load(i, 0).start()

    def remote(src, dst, ssem, rsem, where):
        return pltpu.make_async_remote_copy(
            src_ref=src, dst_ref=dst, send_sem=ssem, recv_sem=rsem,
            device_id=where, device_id_type=MESH,
        )

    def index(u):
        return u // 2

    def side(u):
        return lax.rem(u, 2)

    def group(i):
        if isinstance(i, int):
            return lax.rem(z + VISITS[i], nz)
        away = jnp.where(i == 0, 0, jnp.where(i == 3, 1, i + 1))
        return lax.rem(z + away, nz)

    def ends(u):
        flip = lax.rem(u, 2)
        return rx + flip * (ry - rx), ry + flip * (rx - ry)

    def span_of(u, b):
        return pl.ds(pl.multiple_of(side(u) * hw + starts[b], 128), widths[b])

    def gather(full, ssem, rsem):
        def hop(zz, to):
            slot = zz * 2 + d
            ref = full.at[block(slot, tl)]
            where = ({"col": z + 1}, {"col": z - 1}, sibling)[to]
            return remote(ref, ref, ssem.at[zz, to], rsem.at[slot], where)

        def arrived(slot):
            ref = full.at[block(slot, tl)]
            remote(ref, ref, ssem.at[0, 0], rsem.at[slot], sibling).wait_recv()

        def first(shard):
            full[block(z * 2 + d, tl), :] = shard[...]
            hop(z, 2).start()

            @pl.when(z + 1 < nz)
            def _():
                hop(z, 0).start()

            @pl.when(z > 0)
            def _():
                hop(z, 1).start()

        def stage(s):
            low, high = z - s, z + s

            @pl.when(low >= 0)
            def _():
                arrived(low * 2 + d)

                @pl.when(z + 1 < nz)
                def _():
                    hop(low, 0).start()

                hop(low, 2).start()

            @pl.when(high < nz)
            def _():
                arrived(high * 2 + d)

                @pl.when(z > 0)
                def _():
                    hop(high, 1).start()

                hop(high, 2).start()

        def other(g):
            arrived(g * 2 + 1 - d)

        def drain():
            for zz in range(nz):
                @pl.when((zz <= z) & (z + 1 < nz))
                def _():
                    hop(zz, 0).wait_send()

                @pl.when((zz >= z) & (z > 0))
                def _():
                    hop(zz, 1).wait_send()

                hop(zz, 2).wait_send()

        return first, stage, other, drain

    x_first, x_stage, x_other, x_drain = gather(x_full, x_ssem, x_rsem)
    c_first, c_stage, c_other, c_drain = gather(cot_full, c_ssem, c_rsem)

    def rs(u, b, m):
        i = index(u)
        near, far = ends(u) if b == 0 else ends(u)[::-1]
        slot = m if m < 3 else m - 3
        owner = (rd, near, far)[slot]
        to = far if m == 2 else near
        cols = span_of(u, b)
        which = (pl.ds(0, 2), pl.ds(0, 2), pl.ds(0, 3), pl.ds(2, 1), pl.ds(2, 1))[m]
        return remote(part.at[i, which, block(owner, tr), cols],
                      recv.at[i, slot, which, :, cols],
                      rs_ssem.at[u, b, m], rs_rsem.at[u, b, m], {"row": to})

    def rows(g, owner):
        return pl.ds(pl.multiple_of(g * tg + owner * tr, tr), tr)

    def ag(u, m, incoming=False):
        g = group(index(u))
        p, q = ends(u)
        owner = (p, q, rd, rd)[m] if incoming else (r, r, p, q)[m]
        cols = block(side(u), hw) if m < 2 else span_of(u, m - 2)
        ref = h.at[:, rows(g, owner), cols]
        to = (p, q, q, p)[m]
        return remote(ref, ref, ag_ssem.at[u, m], ag_rsem.at[u, m], {"row": to})

    def to_sibling(i, p):
        g, cols = group(i), block(p, pw)
        return remote(s_part.at[g, :, 1 - d, :, cols], s_sib.at[g, :, :, cols],
                      sib_ssem.at[i, p], sib_rsem.at[i, p], sibling)

    def to_col(i):
        g = group(i)
        k = lax.rem(z - g + nz, nz) - 1
        return remote(s_sum.at[g], s_recv.at[k], z_ssem.at[i], z_rsem.at[k], {"col": g})

    def saves(u):
        span, cols = block(group(index(u)), tg), block(side(u), hw)
        return [
            pltpu.make_async_copy(h.at[j, span, cols], out.at[span, cols], save_sem.at[u, j])
            for j, out in enumerate((act_out, dg_out, du_out))
        ]

    x_save = pltpu.make_async_copy(x_full, x_out, copy_sem.at[0])
    cot_save = pltpu.make_async_copy(cot_full, cot_out, copy_sem.at[1])

    def gate_up(u):
        i = index(u)
        g = group(i)
        span = block(g, tg)
        cols = block(side(u), hw)

        @pl.when((u == 2) | (u == 4))
        def _():
            x_stage(1 + u // 2)

        @pl.when(side(u) == 0)
        def _():
            x_other(g)

        @pl.when(u < 2)
        def _():
            load(0, u).wait()
            load(1, u).wait()

        part[i, 0, :, cols] = dot_nn(x_full[span, :], wg[:, cols]).astype(BF16)
        part[i, 1, :, cols] = dot_nn(x_full[span, :], wu[:, cols]).astype(BF16)
        for m in range(2):
            for b in range(2):
                rs(u, b, m).start()

    def hidden_grad(u):
        i = index(u)
        g = group(i)
        span = block(g, tg)
        cols = block(side(u), hw)

        @pl.when((u == 2) | (u == 4))
        def _():
            c_stage(1 + u // 2)

        @pl.when(side(u) == 0)
        def _():
            c_other(g)

        @pl.when(u < 2)
        def _():
            load(2, u).wait()

        @pl.when(u == 0)
        def _():
            for k in range(3):
                load(k, 1).start()

        part[i, 2, :, cols] = dot_nt(cot_full[span, :], wd[cols, :]).astype(BF16)
        for m in range(3, 5):
            for b in range(2):
                rs(u, b, m).start()

    def relay(u):
        i = index(u)
        for b in range(2):
            rs(u, b, 0).wait_recv()
            rs(u, b, 3).wait_recv()
            spot, cols = block(ends(u)[1 - b], tr), span_of(u, b)
            part[i, :, spot, cols] = (
                part[i, :, spot, cols].astype(F32) + recv[i, 0, :, :, cols].astype(F32)
            ).astype(BF16)
            rs(u, b, 2).start()

    def hidden(u):
        i = index(u)
        own = rows(group(i), r)
        for b in range(2):
            for m in (1, 4, 2):
                rs(u, b, m).wait_recv()
            cols = span_of(u, b)
            gate, up, dact = (
                part[i, j, block(r, tr), cols].astype(F32)
                + recv[i, 1, j, :, cols].astype(F32)
                + recv[i, 2, j, :, cols].astype(F32)
                for j in range(3)
            )
            sig = jax.nn.sigmoid(gate)
            h[0, own, cols] = (gate * sig * up).astype(BF16)
            h[1, own, cols] = (dact * up * sig * (1.0 + gate * (1.0 - sig))).astype(BF16)
            h[2, own, cols] = (dact * gate * sig).astype(BF16)
        ag(u, 0).start()
        ag(u, 1).start()

    def forward(u):
        for m in range(2):
            ag(u, m, True).wait_recv()
            ag(u, m + 2).start()

    def project(u):
        i = index(u)
        g = group(i)
        span, hid = block(g, tg), block(side(u), hw)
        ag(u, 2, True).wait_recv()
        ag(u, 3, True).wait_recv()
        for save in saves(u):
            save.start()

        def products(cols):
            out = dot_nn(h[0, span, hid], wd[hid, cols])
            grad = dot_nt(h[1, span, hid], wg[cols, hid]) + dot_nt(h[2, span, hid], wu[cols, hid])
            return out, grad

        @pl.when(side(u) == 0)
        def _():
            @pl.loop(0, feats // pw)
            def _(p):
                cols = block(p, pw)
                out, grad = products(cols)
                acc[0, :, cols] = out
                acc[1, :, cols] = grad

        @pl.when(side(u) == 1)
        def _():
            @pl.loop(0, feats // pw)
            def _(p):
                cols = block(p, pw)
                for j, value in enumerate(products(cols)):
                    value = (value + acc[j, :, cols]).astype(BF16)
                    for dd in range(2):
                        s_part[g, j, dd, :, cols] = value[dd * tl:(dd + 1) * tl]
                to_sibling(i, p).start()

    def spread(i):
        g = group(i)
        for p in range(feats // pw):
            to_sibling(i, p).wait_recv()
            cols = pl.ds(p * pw, pw)
            for j in range(2):
                s_sum[g, j, :, cols] = (
                    s_part[g, j, d, :, cols].astype(F32) + s_sib[g, j, :, cols].astype(F32)
                ).astype(BF16)


        @pl.when((i > 0) & (i < nz - 1))
        def _():
            to_col(i).start()

    def settle(u):
        for b in range(2):
            for m in range(5):
                rs(u, b, m).wait_send()
        for m in range(4):
            ag(u, m).wait_send()
        for save in saves(u):
            save.wait()

    pl.semaphore_wait(barrier, 2 + nz - 1 + 1)
    x_first(x_ref)
    c_first(cot_ref)
    load(2, 0).start()

    @pl.loop(0, units + 3)
    def _(t):
        @pl.when(t < units)
        def _():
            gate_up(t)

        @pl.when(t >= 3)
        def _():
            project(t - 3)

        @pl.when((t >= 2) & (t < units + 2))
        def _():
            forward(t - 2)

        @pl.when(t < units)
        def _():
            hidden_grad(t)

        @pl.when((t >= 1) & (t < units + 1))
        def _():
            hidden(t - 1)

        @pl.when((t >= 4) & (t < units + 2) & (lax.rem(t, 2) == 0))
        def _():
            spread((t - 4) // 2)

        @pl.when(t == 1)
        def _():
            c_stage(1)

        @pl.when(t < units)
        def _():
            relay(t)

        @pl.when(t == 0)
        def _():
            x_stage(1)

        @pl.when(t >= 5)
        def _():
            settle(t - 5)

        @pl.when(t == units)
        def _():
            x_drain()
            c_drain()

        @pl.when(t == units - 2)
        def _():
            x_save.start()
            cot_save.start()

    def landed(k):
        remote(s_sum.at[0], s_recv.at[k], z_ssem.at[0], z_rsem.at[k], sibling).wait_recv()

    for k in range(nz - 2):
        landed(k)

    to_base = [
        pltpu.make_async_copy(base.at[j], result, base_sem.at[j])
        for j, result in enumerate((out_hbm, tg_hbm))
    ]
    for j in range(2):
        value = s_sum[z, j].astype(F32)
        for k in range(nz - 2):
            value += s_recv[k, j].astype(F32)
        base[j] = value
        to_base[j].start()

    settle(units - 2)
    settle(units - 1)
    for i in range(1, nz - 1):
        to_col(i).wait_send()
    spread(nz - 1)
    to_last = pltpu.make_async_copy(s_sum.at[group(nz - 1)], last_ref, last_sem)
    to_last.start()
    for i in range(nz):
        for p in range(feats // pw):
            to_sibling(i, p).wait_send()
    x_save.wait()
    cot_save.wait()
    for copy in to_base:
        copy.wait()
    to_last.wait()


def weight_kernel(
    x_hbm, dg_hbm, du_hbm, act_hbm, cot_hbm, gate_hbm, up_hbm, down_hbm,
    x, dg, du, act, cot, gate_tile, up_tile, down_tile, in_sem, out_sem,
):
    halves = []
    for k, (src, dst) in enumerate(((x_hbm, x), (dg_hbm, dg), (du_hbm, du), (act_hbm, act), (cot_hbm, cot))):
        width = (src.shape[1] // 2 + 255) // 256 * 256
        halves.append([
            pltpu.make_async_copy(src.at[:, cols], dst.at[:, cols], in_sem.at[k, c])
            for c, cols in enumerate((pl.ds(0, width), pl.ds(width, src.shape[1] - width)))
        ])

    def spans(ref, cut):
        return pl.ds(0, cut), pl.ds(cut, ref.shape[1] - cut)

    def product(k, left, right, tile, result, before):
        rows, width = ((ref.shape[1] // 2 + 255) // 256 * 256 for ref in (left, right))
        saves = []
        for i in range(2):
            for c in range(2):
                for step in before.pop((i, c), ()):
                    step()
                here, cols = spans(left, rows)[i], spans(right, width)[c]
                tile[i, :spans(left, rows)[i].size, cols] = dot_tn(left[:, here], right[:, cols]).astype(BF16)
                save = pltpu.make_async_copy(
                    tile.at[i, :spans(left, rows)[i].size, cols], result.at[here, cols], out_sem.at[k, i, c])
                save.start()
                saves.append(save)
        return saves

    def start(*names):
        return [halves[k][c].start for k, c in names]

    def wait(*names):
        return [halves[k][c].wait for k, c in names]

    for step in start((0, 0), (1, 0), (1, 1), (0, 1)):
        step()
    saves = product(0, x, dg, gate_tile, gate_hbm, {
        (0, 0): wait((0, 0), (1, 0)) + start((2, 0), (2, 1)),
        (0, 1): wait((1, 1)),
        (1, 0): wait((0, 1)) + start((3, 0), (4, 0), (4, 1), (3, 1)),
    })
    saves += product(1, x, du, up_tile, up_hbm, {(0, 0): wait((2, 0)), (0, 1): wait((2, 1))})
    saves += product(2, act, cot, down_tile, down_hbm, {
        (0, 0): wait((3, 0), (4, 0)), (0, 1): wait((4, 1)), (1, 0): wait((3, 1)),
    })
    for save in saves:
        save.wait()


def weight_grads(x, dgate, dup, act, cot):
    total, feats = x.shape
    half = act.shape[1]
    tall, short = ((size // 2 + 255) // 256 * 256 for size in (feats, half))
    hbm = pl.BlockSpec(memory_space=pl.ANY)

    def buf(*shape):
        return pltpu.VMEM(shape, BF16)

    return pl.pallas_call(
        weight_kernel,
        in_specs=[hbm] * 5,
        out_specs=(hbm, hbm, hbm),
        out_shape=(
            jax.ShapeDtypeStruct((feats, half), BF16),
            jax.ShapeDtypeStruct((feats, half), BF16),
            jax.ShapeDtypeStruct((half, feats), BF16),
        ),
        scratch_shapes=[
            buf(total, feats), buf(total, half), buf(total, half), buf(total, half), buf(total, feats),
            buf(2, tall, half), buf(2, tall, half), buf(2, short, feats),
            pltpu.SemaphoreType.DMA((5, 2)), pltpu.SemaphoreType.DMA((3, 2, 2)),
        ],
        compiler_params=pltpu.CompilerParams(vmem_limit_bytes=60 * 2**20),
        cost_estimate=pl.CostEstimate(
            flops=6 * total * feats * half,
            bytes_accessed=6 * feats * half + 4 * total * feats + 6 * total * half,
            transcendentals=0,
        ),
    )(x, dgate, dup, act, cot)


def per_device(n, nz, tokens, gate_weight, up_weight, down_weight, cotangent):
    tl, feats = tokens.shape
    half = gate_weight.shape[1] // 2
    total = tl * nz * 2
    tr = total // n
    ch = 256 if half % 256 == 0 else half
    chunks = half // ch
    pw = 512 if feats % 512 == 0 else feats
    parts = feats // pw
    sliced = half % 128 != 0
    if sliced:
        start = lax.axis_index("depth") * half
        weights = (
            lax.dynamic_slice_in_dim(gate_weight, start, half, 1),
            lax.dynamic_slice_in_dim(up_weight, start, half, 1),
            lax.dynamic_slice_in_dim(down_weight, start, half, 0),
        )
    else:
        weights = (gate_weight, up_weight, down_weight)

    def sds(*shape):
        return jax.ShapeDtypeStruct(shape, BF16)

    def buf(*shape):
        return pltpu.VMEM(shape, BF16)

    def sem(*shape):
        return pltpu.SemaphoreType.DMA(shape)

    vmem = pl.BlockSpec(memory_space=pltpu.VMEM)
    hbm = pl.BlockSpec(memory_space=pl.ANY)
    if n == 4 and nz == 4 and tl % 32 == 0 and half % 256 == 0 and half >= 512:
        out_part, tg_part, last, x_both, cot_both, act, dgate, dup = pl.pallas_call(
            functools.partial(group_kernel, (nz, tl, half, 2 * pw if parts % 2 == 0 else pw)),
            out_shape=(
                jax.ShapeDtypeStruct((tl, feats), F32), jax.ShapeDtypeStruct((tl, feats), F32),
                sds(2, tl, feats),
                sds(total, feats), sds(total, feats),
                sds(total, half), sds(total, half), sds(total, half),
            ),
            in_specs=[vmem, vmem, hbm, hbm, hbm],
            out_specs=(hbm, hbm, hbm, hbm, hbm, hbm, hbm, hbm),
            scratch_shapes=[
                buf(feats, half), buf(feats, half), buf(half, feats),
                buf(total, feats), buf(total, feats),
                buf(nz, 3, 2 * tl, half), buf(nz, 3, 3, tl // 2, half),
                buf(3, total, half), pltpu.VMEM((2, 2 * tl, feats), F32),
                buf(nz, 2, 2, tl, feats), buf(nz, 2, tl, feats), buf(nz, 2, tl, feats),
                buf(nz - 2, 2, tl, feats), pltpu.VMEM((2, tl, feats), F32),
                sem(3, 2), sem(2), sem(2 * nz, 3),
                sem(nz, 3), sem(nz * 2), sem(nz, 3), sem(nz * 2),
                sem(2 * nz, 2, 5), sem(2 * nz, 2, 5), sem(2 * nz, 4), sem(2 * nz, 4),
                sem(nz, parts), sem(nz, parts), sem(nz), sem(nz), pltpu.SemaphoreType.DMA, sem(2),
            ],
            compiler_params=pltpu.CompilerParams(
                collective_id=1, has_side_effects=True, vmem_limit_bytes=60 * 2**20
            ),
            cost_estimate=pl.CostEstimate(
                flops=12 * total * feats * half, bytes_accessed=8 * feats * half,
                transcendentals=0,
            ),
        )(tokens, cotangent, *weights)
        sent = lax.ppermute(last, "col", LAST)
        output = (out_part + sent[0].astype(F32)).astype(BF16)
        tokens_grad = (tg_part + sent[1].astype(F32)).astype(BF16)
        if feats % 256 == 0:
            return (output, tokens_grad, *weight_grads(x_both, dgate, dup, act, cot_both))
    else:
        sums = [
            buf(2, nz, tl, feats), buf(nz, tl, feats), buf(nz, tl, feats),
            buf(max(nz - 1, 1), tl, feats),
        ]
        sum_sems = [sem(parts), sem(parts), sem(parts, nz), sem(parts, nz)]
        output, tokens_grad, x_both, cot_both, act, dgate, dup = pl.pallas_call(
            functools.partial(kernel, (n, nz, tl, tr, chunks, ch, parts, pw, sliced)),
            out_shape=(
                sds(tl, feats), sds(tl, feats), sds(total, feats), sds(total, feats),
                sds(total, half), sds(total, half), sds(total, half),
            ),
            in_specs=[vmem, vmem, hbm, hbm, hbm],
            out_specs=(vmem, vmem, hbm, hbm, hbm, hbm, hbm),
            scratch_shapes=[
                buf(feats, half), buf(feats, half), buf(half, feats),
                buf(total, feats), buf(total, feats),
                buf(chunks, 2, total, ch), buf(chunks, n - 1, 2, tr, ch),
                buf(chunks, total, ch), buf(chunks, n - 1, tr, ch),
                pltpu.VMEM((chunks, 2, tr, ch), F32),
                buf(total, half), buf(total, half), buf(total, half),
                *sums, *sums,
                sem(3), sem(5),
                sem(nz, 3), sem(nz * 2), sem(nz, 3), sem(nz * 2),
                sem(chunks, n - 1), sem(chunks, n - 1),
                sem(chunks, n - 1), sem(chunks, n - 1),
                sem(chunks, n - 1), sem(chunks, n - 1),
                sem(2, chunks, n - 1), sem(2, chunks, n - 1),
                *sum_sems, *sum_sems,
            ],
            compiler_params=pltpu.CompilerParams(
                collective_id=0, has_side_effects=True, vmem_limit_bytes=60 * 2**20
            ),
            cost_estimate=pl.CostEstimate(
                flops=12 * total * feats * half, bytes_accessed=8 * feats * half,
                transcendentals=0,
            ),
        )(tokens, cotangent, *weights)
    gate_grad = dot_tn(x_both, dgate)
    up_grad = dot_tn(x_both, dup)
    down_grad = dot_tn(act, cot_both)
    return (
        output,
        tokens_grad,
        gate_grad.astype(BF16),
        up_grad.astype(BF16),
        down_grad.astype(BF16),
    )


def solution(mesh):
    return jax.shard_map(
        functools.partial(per_device, mesh.shape["row"], mesh.shape["col"]),
        mesh=mesh,
        in_specs=(
            P(("col", "depth"), "row"),
            P("row", "col"),
            P("row", "col"),
            P("col", "row"),
            P(("col", "depth"), "row"),
        ),
        out_specs=(
            P(("col", "depth"), "row"),
            P(("col", "depth"), "row"),
            P("row", ("col", "depth")),
            P("row", ("col", "depth")),
            P(("col", "depth"), "row"),
        ),
        check_vma=False,
    )
```
